32 devices in a mesh: tile: 8 (over z, core), dp: 4 (over y, x).
Axes of the slice: x: 2, y: 2, z: 4, core: 2. Of those that a mesh axis runs over, the one named last changes fastest.
Arguments:
- face_tokens: bfloat16 [4, 48, 64, 1024], P('dp', 'tile'), may hold values from -6 to 6
- edge_tokens: bfloat16 [4, 64, 48, 1024], P('dp', 'tile'), may hold values from -6 to 6
- face_cotangent: bfloat16 [4, 48, 64, 1024], P('dp', 'tile'), may hold values from -6 to 6
- edge_cotangent: bfloat16 [4, 64, 48, 1024], P('dp', 'tile'), may hold values from -6 to 6
- rotation: int32 [48], replicated, may hold values from 0 to 3
- counts: int32 [48], replicated, may hold values from 1 to 64, 2304 in all
- norm_gain: float32 [1024], replicated, may hold values from 0.5 to 1.5
- qkv_weight: bfloat16 [1024, 3072], replicated, may hold values from -1 to 1, as said below
- out_weight: bfloat16 [1024, 1024], replicated, may hold values from -0.1875 to 0.1875
Outputs:
- face_output: bfloat16 [4, 48, 64, 1024], P('dp', 'tile')
- edge_output: bfloat16 [4, 64, 48, 1024], P('dp', 'tile')
- face_grad: bfloat16 [4, 48, 64, 1024], P('dp', 'tile')
- edge_grad: bfloat16 [4, 64, 48, 1024], P('dp', 'tile')
- qkv_grad: float32 [1024, 3072], P('tile')
- out_grad: float32 [1024, 1024], P('tile')
- gain_grad: float32 [1024], P('tile')
The draws below stay inside these ranges and needn't reach their ends.
Inputs may be any that keep to these rules, and one draw needn't show every extreme that they name: `counts`: the largest count is 64. `qkv_weight`: entries drawn independently.
All inputs are finite; a program needn't handle non-finite values.
Results may differ from the reference program's by a relative error of at most 0.007.
The reference program's roundings to bfloat16 on the way count: a program that leaves them out, or rounds other values in their place, can miss the bound.
Values may be sent and summed in bfloat16 or wider, within the bound.
No kernel may reach another device: no remote copies, remote signals or barrier semaphores. Data moves between devices by JAX's collectives and lax.ppermute only.
A program may use at most 128 MiB of HBM per device.

```python
import math
import jax
import jax.numpy as jnp
import numpy as np
from jax import lax

D = 1024
HEADS = 16
LINES_DEV = 6
LA = 64
LB = 64
NL = 48
SAMPLES = 4


def draw_qkv_weight(key, part):
    key = jax.random.fold_in(key, 7)
    return (jax.random.normal(key, (D, 3 * D), jnp.float32) * D ** (-0.5)).astype(jnp.bfloat16)


def plant(array, stream_key, smallest, largest):
    index_at = [jax.random.randint(jax.random.fold_in(stream_key, axis), (), 0, length) for axis, length in enumerate(array.shape)]
    main_axis = array.shape.index(max(array.shape))
    next_to = index_at[:main_axis] + [(index_at[main_axis] + 1) % array.shape[main_axis]] + index_at[main_axis + 1:]
    return array.at[tuple(index_at)].set(smallest).at[tuple(next_to)].set(largest)


def block_levels(key, dims, split, smallest, high):
    def one(axis_at, parts):
        draws = jax.random.uniform(jax.random.fold_in(jax.random.fold_in(key, 6), axis_at), (parts,), jnp.float32, smallest / len(split), high / len(split))
        return jnp.repeat(jnp.exp(draws), dims[axis_at] // parts).reshape((-1,) + (1,) * (len(dims) - axis_at - 1))

    factor_of = one(*split[0])
    for cut in split[1:]:
        factor_of = factor_of * one(*cut)
    return factor_of


def split_up(amount, total, limit, lean):
    loads = [(1 << 20) // math.isqrt(grade ** lean) + 1 for grade in range(2, amount + 1)]
    surplus, given = total - limit - (amount - 1), [1] * (amount - 1)
    while surplus > 0:
        candidates = [i for i in range(amount - 1) if given[i] < limit]
        whole, remaining = sum([loads[i] for i in candidates]), surplus
        for i in candidates:
            more = min(limit - given[i], max(1, remaining * loads[i] // whole), surplus)
            given[i] = given[i] + more
            surplus = surplus - more
    return np.array([limit] + given)


def uneven_parts(key, amount, total, bound, lean):
    if amount == 2:
        one = jax.random.randint(key, (), max(1, total - bound), min(bound, total - 1) + 1)
        return jnp.stack([one, total - one])
    lengths = jnp.asarray(split_up(amount, total, bound, lean), jnp.int32)
    couples = (amount - 1) // 2
    giver, receiver = lengths[1:1 + 2 * couples:2], lengths[2:2 + 2 * couples:2]
    slack = jnp.minimum(giver - 1, bound - receiver)
    shifted = jax.random.randint(jax.random.fold_in(key, 1), (couples,), 0, 1 << 20) % (slack + 1)
    lengths = lengths.at[1:1 + 2 * couples:2].set(giver - shifted).at[2:2 + 2 * couples:2].set(receiver + shifted)
    return lengths[jax.random.permutation(jax.random.fold_in(key, 2), amount)]


def scatter_about(key, dims, deviation, reach, split=(), kind=jnp.bfloat16):
    factor_of = block_levels(key, dims, split, -0.22, 0.18) if split else 1.0
    result = jax.random.normal(key, dims, jnp.float32) * deviation * factor_of
    return jnp.minimum(jnp.maximum(result, -reach), reach).astype(kind)


def setup_inputs(seed: int = 0) -> dict:
    key_of = jax.random.split(jax.random.key(seed), 10)
    return {
        "face_tokens": scatter_about(key_of[0], (SAMPLES, NL, LA, D), 1.0, 6.0, ((0, 4), (1, 8))),
        "edge_tokens": scatter_about(key_of[1], (SAMPLES, LB, NL, D), 1.0, 6.0, ((0, 4), (1, 8))),
        "face_cotangent": scatter_about(key_of[2], (SAMPLES, NL, LA, D), 1.0, 6.0, ((0, 4), (1, 8))),
        "edge_cotangent": scatter_about(key_of[3], (SAMPLES, LB, NL, D), 1.0, 6.0, ((0, 4), (1, 8))),
        "rotation": plant(jax.random.randint(key_of[4], (NL,), 0, 4), jax.random.fold_in(key_of[4], 1), 0, 3).astype(jnp.int32),
        "counts": uneven_parts(key_of[5], NL, NL * LB * 3 // 4, LB, 1).astype(jnp.int32),
        "norm_gain": jnp.clip(1.0 + 0.1 * jax.random.normal(key_of[6], (D,), jnp.float32), 0.5, 1.5),
        "qkv_weight": draw_qkv_weight(jax.random.fold_in(key_of[9], 71), 0),
        "out_weight": scatter_about(key_of[8], (D, D), D ** -0.5, 0.1875),
    }


def orient(rows, line_turns, sense):
    half_width = rows.shape[-1] // 2
    flipped = jnp.where((line_turns >= 2)[:, None, None], rows[:, ::-1, :], rows)
    cosine = ((line_turns == 0).astype(jnp.float32) - (line_turns == 2).astype(jnp.float32))[:, None, None]
    sine = sense * ((line_turns == 1).astype(jnp.float32) - (line_turns == 3).astype(jnp.float32))[:, None, None]
    first_half = flipped[..., :half_width].astype(jnp.float32)
    second_half = flipped[..., half_width:].astype(jnp.float32)
    turned = jnp.concatenate([cosine * first_half - sine * second_half, sine * first_half + cosine * second_half], axis=-1)
    return turned.astype(jnp.bfloat16)

def line_layer(tokens, cotangent, key_live, norm_gain, qkv_weight, out_weight, head_count, factor):
    line_count, length, model_width = tokens.shape
    head_dim = model_width // head_count
    score_scale = head_dim ** (-0.5)
    hidden_float = tokens.astype(jnp.float32)
    inverse = lax.rsqrt(lax.optimization_barrier(jnp.mean(hidden_float * hidden_float, axis=-1, keepdims=True)) + 1e-06)
    normed = (hidden_float * inverse * norm_gain).astype(jnp.bfloat16).reshape(line_count * length, model_width)
    projected = jnp.dot(normed, qkv_weight, preferred_element_type=jnp.float32).astype(jnp.bfloat16)
    shape_heads = (line_count, length, head_count, head_dim)
    queries = projected[:, :model_width].reshape(shape_heads).astype(jnp.float32)
    key_rows = projected[:, model_width:2 * model_width].reshape(shape_heads).astype(jnp.float32)
    value_rows = projected[:, 2 * model_width:].reshape(shape_heads).astype(jnp.float32)
    scores = jnp.einsum('lshe,lthe->lhst', queries, key_rows) * score_scale
    scores = jnp.where(key_live[:, None, None, :], scores, -1e+30)
    row_max = lax.optimization_barrier(jnp.max(scores, axis=-1, keepdims=True))
    exp_scores = jnp.exp(scores - row_max)
    soft_weights = exp_scores / lax.optimization_barrier(jnp.sum(exp_scores, axis=-1, keepdims=True))
    soft_rounded = soft_weights.astype(jnp.bfloat16).astype(jnp.float32)
    mixed_heads = jnp.einsum('lhst,lthe->lshe', soft_rounded, value_rows).astype(jnp.bfloat16)
    mixed_heads = mixed_heads.reshape(line_count * length, model_width)
    attended = jnp.dot(mixed_heads, out_weight, preferred_element_type=jnp.float32).reshape(tokens.shape)
    output = (hidden_float + attended).astype(jnp.bfloat16)
    grad_rows = cotangent.reshape(line_count * length, model_width)
    out_grad = jnp.dot(mixed_heads.T, grad_rows, preferred_element_type=jnp.float32) * factor
    mixed_grad = jnp.dot(grad_rows, out_weight.T, preferred_element_type=jnp.float32).astype(jnp.bfloat16)
    mixed_grad = mixed_grad.reshape(shape_heads).astype(jnp.float32)
    prob_grad = jnp.einsum('lshe,lthe->lhst', mixed_grad, value_rows)
    value_grad = jnp.einsum('lhst,lshe->lthe', soft_rounded, mixed_grad).astype(jnp.bfloat16)
    score_grad = soft_weights * (prob_grad - lax.optimization_barrier(jnp.sum(soft_weights * prob_grad, axis=-1, keepdims=True))) * score_scale
    score_grad = score_grad.astype(jnp.bfloat16).astype(jnp.float32)
    query_grad = jnp.einsum('lhst,lthe->lshe', score_grad, key_rows).astype(jnp.bfloat16)
    key_grad = jnp.einsum('lhst,lshe->lthe', score_grad, queries).astype(jnp.bfloat16)
    flat_rows = line_count * length
    stacked = jnp.concatenate([query_grad.reshape(flat_rows, model_width), key_grad.reshape(flat_rows, model_width), value_grad.reshape(flat_rows, model_width)], axis=1)
    qkv_grad = jnp.dot(normed.T, stacked, preferred_element_type=jnp.float32) * factor
    normed_grad = jnp.dot(stacked, qkv_weight.T, preferred_element_type=jnp.float32).reshape(tokens.shape)
    gain_grad = lax.optimization_barrier(jnp.sum(normed_grad * hidden_float * inverse, axis=(0, 1))) * factor
    scaled_grad = normed_grad * norm_gain
    token_grad = inverse * scaled_grad - hidden_float * inverse * inverse * inverse * lax.optimization_barrier(jnp.mean(scaled_grad * hidden_float, axis=-1, keepdims=True))
    input_grad = (cotangent.astype(jnp.float32) + token_grad).astype(jnp.bfloat16)
    return (output, input_grad, qkv_grad, out_grad, gain_grad)

def reference(face_tokens, edge_tokens, face_cotangent, edge_cotangent, rotation, counts, norm_gain, qkv_weight, out_weight):
    block_count = NL // LINES_DEV
    seq_length = LA + LB
    factor = float(SAMPLES * NL * seq_length) ** (-0.5)
    positions = jnp.arange(seq_length, dtype=jnp.int32)
    key_live = positions[None, :] < (counts + LA)[:, None]
    zero = jnp.zeros((), jnp.int32)

    def block_step(totals, index):
        index = index.astype(jnp.int32)
        sample = (index // block_count).astype(jnp.int32)
        first_line = (index % block_count * LINES_DEV).astype(jnp.int32)
        face_part = lax.dynamic_slice(face_tokens, (sample, first_line, zero, zero), (1, LINES_DEV, LA, D))[0]
        face_cot = lax.dynamic_slice(face_cotangent, (sample, first_line, zero, zero), (1, LINES_DEV, LA, D))[0]
        edge_part = lax.dynamic_slice(edge_tokens, (sample, zero, first_line, zero), (1, LB, LINES_DEV, D))[0].transpose(1, 0, 2)
        edge_cot = lax.dynamic_slice(edge_cotangent, (sample, zero, first_line, zero), (1, LB, LINES_DEV, D))[0].transpose(1, 0, 2)
        line_turns = lax.dynamic_slice(rotation, (first_line,), (LINES_DEV,))
        live_block = lax.dynamic_slice(key_live, (first_line, zero), (LINES_DEV, seq_length))
        tokens = jnp.concatenate([face_part, orient(edge_part, line_turns, 1.0)], axis=1)
        cotangent = jnp.concatenate([face_cot, orient(edge_cot, line_turns, 1.0)], axis=1)
        output, input_grad, qkv_part, out_part, gain_part = line_layer(tokens, cotangent, live_block, norm_gain, qkv_weight, out_weight, HEADS, factor)
        results = (output[:, :LA], orient(output[:, LA:], line_turns, -1.0), input_grad[:, :LA], orient(input_grad[:, LA:], line_turns, -1.0))
        return ((totals[0] + qkv_part, totals[1] + out_part, totals[2] + gain_part), results)
    start_totals = (jnp.zeros((D, 3 * D), jnp.float32), jnp.zeros((D, D), jnp.float32), jnp.zeros((D,), jnp.float32))
    totals, results = lax.scan(block_step, start_totals, jnp.arange(SAMPLES * block_count, dtype=jnp.int32))
    face_output = results[0].reshape(SAMPLES, NL, LA, D)
    edge_output = results[1].reshape(SAMPLES, NL, LB, D).transpose(0, 2, 1, 3)
    face_grad = results[2].reshape(SAMPLES, NL, LA, D)
    edge_grad = results[3].reshape(SAMPLES, NL, LB, D).transpose(0, 2, 1, 3)
    return (face_output, edge_output, face_grad, edge_grad, totals[0], totals[1], totals[2])
```

```python
import functools

import jax
import jax.numpy as jnp
import numpy as np
from jax import lax
from jax.experimental import pallas as pl
from jax.experimental.pallas import tpu as pltpu
from jax.sharding import PartitionSpec as P

HEADS = 16
BF = jnp.bfloat16
F32 = jnp.float32
VMEM_BYTES = 48 * 1024 * 1024


def nn(a, b):
    return lax.dot_general(a, b, (((1,), (0,)), ((), ())), preferred_element_type=F32)


def nt(a, b):
    return lax.dot_general(a, b, (((1,), (1,)), ((), ())), preferred_element_type=F32)


def tn(a, b):
    return lax.dot_general(a, b, (((0,), (0,)), ((), ())), preferred_element_type=F32)


def one_hot(index_ref, width):
    rows = index_ref.shape[0]
    columns = lax.broadcasted_iota(jnp.int32, (rows, width), 1)
    return jnp.where(columns == index_ref[...], 1.0, 0.0).astype(BF)


def pack_kernel(tok_ref, cot_ref, index_ref, *refs):
    both = refs[-1]
    rows = tok_ref.shape[0]
    both[:rows] = tok_ref[...]
    both[rows:] = cot_ref[...]
    take = index_ref.shape[0] // (len(refs) - 1)
    for c, out in enumerate(refs[:-1]):
        columns = lax.broadcasted_iota(jnp.int32, (take, 2 * rows), 1)
        picked = jnp.where(columns == index_ref[c * take : (c + 1) * take], 1.0, 0.0).astype(BF)
        out[...] = nn(picked, both[...]).astype(BF)


def unpack_kernel(chunks, *refs):
    backs, index_ref, out_tok, out_cot, both = refs[:chunks], refs[chunks], refs[-3], refs[-2], refs[-1]
    take = backs[0].shape[0]
    for c, back in enumerate(backs):
        both[c * take : (c + 1) * take] = back[...]
    rows = out_tok.shape[0]
    for w, out in enumerate((out_tok, out_cot)):
        columns = lax.broadcasted_iota(jnp.int32, (rows, chunks * take), 1)
        picked = jnp.where(columns == index_ref[w * rows : (w + 1) * rows], 1.0, 0.0).astype(BF)
        out[...] = nn(picked, both[...]).astype(BF)


def layer_kernel(
    lines,
    length,
    aliased,
    scal_ref,
    face_ref,
    fcot_ref,
    arrived_ref,
    index_ref,
    back_index_ref,
    turn_ref,
    gain_ref,
    wqkv_ref,
    wo_ref,
    *refs,
):
    refs = refs[2:] if aliased else refs
    (
        face_out,
        face_grad,
        back_ref,
        normed,
        keep_a,
        send_a,
        lhs_keep,
        rhs_keep,
        lhs_send,
        rhs_send,
        gain_part,
        z_s,
        g_s,
        qkv_s,
        dm_s,
        mix_s,
        stk_s,
        dn_s,
        y_s,
        inv_s,
        edge_s,
    ) = refs
    width = z_s.shape[1]
    half = width // 2
    face_len = face_ref.shape[2]
    edge_len = length - face_len
    edges = lines * edge_len
    rows_all = lines * length
    head_dim = width // HEADS
    scale = head_dim ** (-0.5)

    picked = one_hot(index_ref, arrived_ref.shape[0])
    first = nn(picked, arrived_ref[:, :half])
    second = nn(picked, arrived_ref[:, half:])
    cosine = turn_ref[:, 0:1]
    sine = turn_ref[:, 1:2]
    turned_first = (cosine * first - sine * second).astype(BF)
    turned_second = (sine * first + cosine * second).astype(BF)
    for l in range(lines):
        at = l * length
        z_s[at : at + face_len] = face_ref[0, l]
        g_s[at : at + face_len] = fcot_ref[0, l]
        for w, dst in enumerate((z_s, g_s)):
            src = w * edges + l * edge_len
            dst[at + face_len : at + length, :half] = turned_first[src : src + edge_len]
            dst[at + face_len : at + length, half:] = turned_second[src : src + edge_len]
    gain = gain_ref[...]
    for l in range(lines):
        at = slice(l * length, (l + 1) * length)
        hidden = z_s[at].astype(F32)
        inverse = lax.rsqrt(jnp.mean(hidden * hidden, axis=-1, keepdims=True) + 1e-06)
        inv_s[at] = inverse
        normed[at] = (hidden * inverse * gain).astype(BF)

    tile = 512

    @pl.loop(0, 3 * width // tile)
    def _(j):
        cols = pl.ds(pl.multiple_of(j * tile, tile), tile)
        qkv_s[:, cols] = nn(normed[...], wqkv_ref[:, cols]).astype(BF)

    @pl.loop(0, width // tile)
    def _(j):
        cols = pl.ds(pl.multiple_of(j * tile, tile), tile)
        dm_s[:, cols] = nt(g_s[...], wo_ref[cols, :]).astype(BF)

    pair = 2 * head_dim
    low = lax.broadcasted_iota(jnp.int32, (length, pair), 1) < head_dim
    key_row = lax.broadcasted_iota(jnp.int32, (length, length), 0)

    def split(x):
        zero = jnp.zeros_like(x)
        return jnp.concatenate([jnp.where(low, x, zero), jnp.where(low, zero, x)], axis=0)

    @pl.loop(0, lines)
    def _(l):
        rows = pl.ds(pl.multiple_of(l * length, length), length)
        live = key_row < scal_ref[l] + face_len
        for p in range(HEADS // 2):
            at = p * pair
            q = qkv_s[rows, at : at + pair]
            k2 = split(qkv_s[rows, width + at : width + at + pair])
            v2 = split(qkv_s[rows, 2 * width + at : 2 * width + at + pair])
            dm = dm_s[rows, at : at + pair]
            scores = nt(k2, q) * scale
            d_probs = nt(v2, dm)
            probs_b, d_scores = [], []
            for h in range(2):
                part = slice(h * length, (h + 1) * length)
                s = jnp.where(live, scores[part], -1e30)
                e = jnp.exp(s - jnp.max(s, axis=0, keepdims=True))
                probs = e / jnp.sum(e, axis=0, keepdims=True)
                d = d_probs[part]
                inner = jnp.sum(probs * d, axis=0, keepdims=True)
                probs_b.append(probs.astype(BF))
                d_scores.append((probs * (d - inner) * scale).astype(BF))
            pb = jnp.concatenate(probs_b, axis=0)
            ds = jnp.concatenate(d_scores, axis=0)
            mix_s[rows, at : at + pair] = tn(pb, v2).astype(BF)
            dv = nn(pb, dm)
            stk_s[rows, 2 * width + at : 2 * width + at + pair] = jnp.where(
                low, dv[:length], dv[length:]
            ).astype(BF)
            stk_s[rows, at : at + pair] = tn(ds, k2).astype(BF)
            dk = nn(ds, q)
            stk_s[rows, width + at : width + at + pair] = jnp.where(
                low, dk[:length], dk[length:]
            ).astype(BF)

    @pl.loop(0, width // tile)
    def _(j):
        cols = pl.ds(pl.multiple_of(j * tile, tile), tile)
        y_s[:, cols] = (nn(mix_s[...], wo_ref[:, cols]) + z_s[:, cols].astype(F32)).astype(BF)
        dn_s[:, cols] = nt(stk_s[...], wqkv_ref[cols, :])

    gain_sum = jnp.zeros((1, width), F32)
    for l in range(lines):
        at = slice(l * length, (l + 1) * length)
        hidden = z_s[at].astype(F32)
        inverse = inv_s[at]
        d_normed = dn_s[at]
        gain_sum = gain_sum + jnp.sum(d_normed * hidden * inverse, axis=0, keepdims=True)
        scaled = d_normed * gain
        mean = jnp.mean(scaled * hidden, axis=-1, keepdims=True)
        dz = inverse * scaled - hidden * (inverse * inverse * inverse * mean)
        dz = (g_s[at].astype(F32) + dz).astype(BF)
        face_out[0, l] = y_s[l * length : l * length + face_len]
        face_grad[0, l] = dz[:face_len]
        edge_s[l * edge_len : (l + 1) * edge_len] = y_s[l * length + face_len : (l + 1) * length]
        edge_s[edges + l * edge_len : edges + (l + 1) * edge_len] = dz[face_len:]
    gain_part[...] = jnp.broadcast_to(gain_sum, gain_part.shape)
    first = edge_s[:, :half].astype(F32)
    second = edge_s[:, half:].astype(F32)
    turned_first = (cosine * first + sine * second).astype(BF)
    turned_second = (cosine * second - sine * first).astype(BF)
    picked = one_hot(back_index_ref, 2 * edges)
    back_ref[:, :half] = nn(picked, turned_first).astype(BF)
    back_ref[:, half:] = nn(picked, turned_second).astype(BF)

    x_bit = scal_ref[lines]
    y_bit = scal_ref[lines + 1]

    @pl.when(x_bit == 0)
    def _():
        keep_a[...] = stk_s[:, :width]
        send_a[...] = stk_s[:, width : 2 * width]

    @pl.when(x_bit != 0)
    def _():
        send_a[...] = stk_s[:, :width]
        keep_a[...] = stk_s[:, width : 2 * width]

    @pl.when(y_bit == 0)
    def _():
        lhs_keep[...] = normed[...]
        rhs_keep[...] = stk_s[:, 2 * width :]
        lhs_send[...] = mix_s[...]
        rhs_send[...] = g_s[...]

    @pl.when(y_bit != 0)
    def _():
        lhs_send[...] = normed[...]
        rhs_send[...] = stk_s[:, 2 * width :]
        lhs_keep[...] = mix_s[...]
        rhs_keep[...] = g_s[...]


def weight_kernel(chunks, blocks, added, par_ref, *refs):
    lhs = refs[:chunks]
    rhs = refs[chunks : 2 * chunks]
    add_ref = refs[2 * chunks] if added else None
    out_ref, lhs_t = refs[-2], refs[-1]
    rows = lhs[0].shape[0]
    size = lhs[0].shape[1] // (2 * blocks)

    @pl.when(pl.program_id(0) == 0)
    def _():
        even = par_ref[0] == 0
        for c in range(chunks):
            for b in range(blocks):
                left = lhs[c][:, 2 * b * size : (2 * b + 1) * size]
                right = lhs[c][:, (2 * b + 1) * size : (2 * b + 2) * size]
                kept = jnp.where(even, left, right)
                lhs_t[b * size : (b + 1) * size, c * rows : (c + 1) * rows] = kept.T

    total = nn(lhs_t[:, :rows], rhs[0][...])
    for c in range(1, chunks):
        total = total + nn(lhs_t[:, c * rows : (c + 1) * rows], rhs[c][...])
    if added:
        total = total + add_ref[...]
    out_ref[...] = total


def weight_part(parity, lhs, rhs, blocks, add=None):
    chunks = len(lhs)
    rows, depth = lhs[0].shape
    width = rhs[0].shape[1]
    tile = 256
    whole = pl.BlockSpec((rows, depth), lambda j, s: (0, 0))
    piece = pl.BlockSpec((rows, tile), lambda j, s: (0, j))
    result = pl.BlockSpec((depth // 2, tile), lambda j, s: (0, j))
    operands = [*lhs, *rhs] + ([add] if add is not None else [])
    return pl.pallas_call(
        functools.partial(weight_kernel, chunks, blocks, add is not None),
        grid_spec=pltpu.PrefetchScalarGridSpec(
            num_scalar_prefetch=1,
            grid=(width // tile,),
            in_specs=[whole] * chunks + [piece] * chunks + ([result] if add is not None else []),
            out_specs=result,
            scratch_shapes=[pltpu.VMEM((depth // 2, chunks * rows), BF)],
        ),
        out_shape=jax.ShapeDtypeStruct((depth // 2, width), F32),
        compiler_params=pltpu.CompilerParams(vmem_limit_bytes=VMEM_BYTES),
        cost_estimate=pl.CostEstimate(
            flops=chunks * rows * depth * width, bytes_accessed=8 * depth * width, transcendentals=0
        ),
        name="weight_part",
    )(parity, *operands)


def exchange(x, axis, bits, size):
    return lax.ppermute(x, axis, [(i, i ^ bits) for i in range(size)])


def local(
    face_tokens,
    edge_tokens,
    face_cotangent,
    edge_cotangent,
    rotation,
    counts,
    norm_gain,
    qkv_weight,
    out_weight,
):
    T = lax.axis_size("tile")
    D = lax.axis_size("dp")
    me_t = lax.axis_index("tile")
    me_d = lax.axis_index("dp")
    LD, FL, width = face_tokens.shape[1:]
    K = edge_tokens.shape[1]
    EL = K * T
    NLG = edge_tokens.shape[2]
    length = FL + EL
    chunks = 2
    lines = LD // chunks
    RB = lines * K
    packed = T * 2 * RB
    factor = float(D * T * LD * length) ** (-0.5)

    def vmem_call(kernel, out_shape, scratch, *operands):
        return pl.pallas_call(
            kernel,
            out_shape=out_shape,
            in_specs=[pl.BlockSpec(memory_space=pltpu.VMEM)] * len(operands),
            scratch_shapes=scratch,
            compiler_params=pltpu.CompilerParams(vmem_limit_bytes=VMEM_BYTES),
            name="rows_kernel",
        )(*operands)

    order = np.zeros((chunks, T, 2, lines, K), np.int32)
    for c in range(chunks):
        for w in range(2):
            t, l, k = np.meshgrid(np.arange(T), np.arange(lines), np.arange(K), indexing="ij")
            order[c, :, w] = w * K * NLG + k * NLG + t * LD + c * lines + l
    sent = vmem_call(
        pack_kernel,
        [jax.ShapeDtypeStruct((packed, width), BF)] * chunks,
        [pltpu.VMEM((2 * K * NLG, width), BF)],
        edge_tokens.reshape(K * NLG, width),
        edge_cotangent.reshape(K * NLG, width),
        jnp.asarray(order.reshape(-1, 1)),
    )
    arrived = [lax.all_to_all(s, "tile", split_axis=0, concat_axis=0, tiled=True) for s in sent]

    my_turns = lax.dynamic_slice_in_dim(rotation, me_t * LD, LD)
    my_counts = lax.dynamic_slice_in_dim(counts, me_t * LD, LD)
    x_bit = (me_d % 2).astype(jnp.int32)
    y_bit = ((me_d // 2) % 2).astype(jnp.int32)

    spos = np.arange(EL)
    results = []
    faces = None
    for c in range(chunks):
        turns = my_turns[c * lines : (c + 1) * lines]
        flip = turns >= 2
        pos = jnp.where(flip[:, None], EL - 1 - spos[None, :], spos[None, :])
        row = (pos // K) * (2 * RB) + jnp.arange(lines)[:, None] * K + pos % K
        index = jnp.concatenate([row, row + RB], axis=0).reshape(-1, 1).astype(jnp.int32)
        cosine = (turns == 0).astype(F32) - (turns == 2).astype(F32)
        sine = (turns == 1).astype(F32) - (turns == 3).astype(F32)
        turn = jnp.stack([cosine, sine], axis=-1)
        turn = jnp.broadcast_to(turn[None, :, None, :], (2, lines, EL, 2)).reshape(-1, 2)
        sk = np.arange(T)[:, None, None, None] * K + np.arange(K)[None, None, None, :]
        bk = jnp.where(flip[None, None, :, None], EL - 1 - sk, sk)
        back_index = (
            jnp.arange(2)[None, :, None, None] * (lines * EL)
            + jnp.arange(lines)[None, None, :, None] * EL
            + bk
        )
        back_index = back_index.reshape(-1, 1).astype(jnp.int32)
        scal = jnp.concatenate(
            [my_counts[c * lines : (c + 1) * lines], jnp.stack([x_bit, y_bit])]
        )
        rows_all = lines * length
        face_spec = pl.BlockSpec((1, lines, FL, width), lambda i, s, c=c: (0, c, 0, 0))

        def full(shape):
            return pl.BlockSpec(shape, lambda i, s: (0,) * len(shape))

        row_shape = (rows_all, width)
        operands = [
            face_tokens,
            face_cotangent,
            arrived[c],
            index,
            back_index,
            turn,
            norm_gain.reshape(1, width),
            qkv_weight,
            out_weight,
        ]
        in_specs = [face_spec, face_spec] + [full(o.shape) for o in operands[2:]]
        if faces is not None:
            in_specs += [pl.BlockSpec(memory_space=pl.ANY)] * 2
            operands += list(faces)
        outs = pl.pallas_call(
            functools.partial(layer_kernel, lines, length, faces is not None),
            grid_spec=pltpu.PrefetchScalarGridSpec(
                num_scalar_prefetch=1,
                grid=(1,),
                in_specs=in_specs,
                out_specs=[face_spec, face_spec, full((packed, width))]
                + [full(row_shape)] * 7
                + [full((8, width))],
                scratch_shapes=[
                    pltpu.VMEM(row_shape, BF),
                    pltpu.VMEM(row_shape, BF),
                    pltpu.VMEM((rows_all, 3 * width), BF),
                    pltpu.VMEM(row_shape, BF),
                    pltpu.VMEM(row_shape, BF),
                    pltpu.VMEM((rows_all, 3 * width), BF),
                    pltpu.VMEM(row_shape, F32),
                    pltpu.VMEM(row_shape, BF),
                    pltpu.VMEM((rows_all, 1), F32),
                    pltpu.VMEM((2 * lines * EL, width), BF),
                ],
            ),
            out_shape=[
                jax.ShapeDtypeStruct(face_tokens.shape, BF),
                jax.ShapeDtypeStruct(face_tokens.shape, BF),
                jax.ShapeDtypeStruct((packed, width), BF),
            ]
            + [jax.ShapeDtypeStruct(row_shape, BF)] * 7
            + [jax.ShapeDtypeStruct((8, width), F32)],
            input_output_aliases={10: 0, 11: 1} if faces is not None else {},
            compiler_params=pltpu.CompilerParams(vmem_limit_bytes=VMEM_BYTES),
            cost_estimate=pl.CostEstimate(
                flops=2 * rows_all * width * width * 8 * 2, bytes_accessed=1 << 24, transcendentals=0
            ),
            name="layer",
        )(scal, *operands)
        faces = outs[:2]
        results.append(outs[2:])
    returned = [
        lax.all_to_all(r[0], "tile", split_axis=0, concat_axis=0, tiled=True) for r in results
    ]
    back_order = np.zeros((2, K, NLG), np.int32)
    for w in range(2):
        k, t, c, l = np.meshgrid(
            np.arange(K), np.arange(T), np.arange(chunks), np.arange(lines), indexing="ij"
        )
        back_order[w] = (c * packed + t * 2 * RB + w * RB + l * K + k).reshape(K, NLG)
    edge_output, edge_grad = vmem_call(
        functools.partial(unpack_kernel, chunks),
        [jax.ShapeDtypeStruct((K * NLG, width), BF)] * 2,
        [pltpu.VMEM((chunks * packed, width), BF)],
        *returned,
        jnp.asarray(back_order.reshape(-1, 1)),
    )

    blocks = T // 2
    chip = me_t // 2
    core = me_t % 2
    own = core.astype(jnp.int32).reshape(1)
    other = 1 - own
    column = list(zip(*results))
    _, normed, keep_a, send_a, lhs_keep, rhs_keep, lhs_send, rhs_send, gain_part = column

    def core_sum(lhs, rhs):
        theirs = exchange(weight_part(other, lhs, rhs, blocks), "tile", 1, T)
        return weight_part(own, lhs, rhs, blocks, theirs)

    sum_send_a = exchange(core_sum(normed, send_a), "dp", 1, D)
    sum_send_b = exchange(core_sum(lhs_send, rhs_send), "dp", 2, D)
    sum_a = core_sum(normed, keep_a)
    sum_b = core_sum(lhs_keep, rhs_keep)

    def halve(first, second, bits):
        parts = [first, second]
        for bit in bits:
            columns = parts[0].shape[-1] // 2
            mine = (me_d >> bit) & 1
            keep = [lax.dynamic_slice_in_dim(p, mine * columns, columns, 1) for p in parts]
            send = [lax.dynamic_slice_in_dim(p, (1 - mine) * columns, columns, 1) for p in parts]
            parts = [sum(keep), exchange(sum(send), "dp", 1 << bit, D)]
        return parts

    bits = D.bit_length() - 1
    rest_a = [b for b in range(bits) if b != 0]
    rest_b = [b for b in range(bits) if b != 1]
    half_a = halve(sum_a, sum_send_a, rest_a)
    half_b = halve(sum_b, sum_send_b, rest_b)
    size = width // T

    def block(parts, which):
        return sum(lax.dynamic_slice_in_dim(p, which * size, size, 0) for p in parts)

    mine_a, mine_b = block(half_a, chip), block(half_b, chip)
    for o in range(1, blocks):
        got_a = exchange(block(half_a, chip ^ o), "tile", 2 * o, T)
        got_b = exchange(block(half_b, chip ^ o), "tile", 2 * o, T)
        mine_a, mine_b = mine_a + got_a, mine_b + got_b
    mine = jnp.concatenate([mine_a, mine_b], axis=1) * factor
    pieces = [mine] + [exchange(mine, "dp", o, D) for o in range(1, D)]
    stacked = jnp.stack(pieces)
    piece = mine_a.shape[1]

    def place(bit, fixed, offset):
        rest = [b for b in range(bits) if b != fixed]
        columns = []
        for n in range(D // 2):
            device = bit << fixed
            for i, b in enumerate(rest):
                device |= ((n >> (len(rest) - 1 - i)) & 1) << b
            got = lax.dynamic_index_in_dim(stacked, me_d ^ device, 0, keepdims=False)
            columns.append(got[:, offset : offset + piece])
        return columns

    qkv_grad = jnp.concatenate(
        place(0, 0, 0) + place(1, 0, 0) + place(0, 1, piece), axis=1
    )
    out_grad = jnp.concatenate(place(1, 1, piece), axis=1)

    gain_sum = sum(g[0:1] for g in gain_part)
    for b in range(bits):
        gain_sum = gain_sum + exchange(gain_sum, "dp", 1 << b, D)
    for b in range(T.bit_length() - 1):
        gain_sum = gain_sum + exchange(gain_sum, "tile", 1 << b, T)
    gain_grad = lax.dynamic_slice_in_dim(gain_sum[0], me_t * size, size) * factor
    shape = edge_tokens.shape
    return (
        faces[0],
        edge_output.reshape(shape),
        faces[1],
        edge_grad.reshape(shape),
        qkv_grad,
        out_grad,
        gain_grad,
    )


def solution(mesh):
    return jax.shard_map(
        local,
        mesh=mesh,
        in_specs=(
            P("dp", "tile", None, None),
            P("dp", "tile", None, None),
            P("dp", "tile", None, None),
            P("dp", "tile", None, None),
            P(),
            P(),
            P(),
            P(),
            P(),
        ),
        out_specs=(
            P("dp", "tile", None, None),
            P("dp", "tile", None, None),
            P("dp", "tile", None, None),
            P("dp", "tile", None, None),
            P("tile", None),
            P("tile", None),
            P("tile"),
        ),
        check_vma=False,
    )
```

```python
import functools

import jax
import jax.numpy as jnp
import numpy as np
from jax import lax
from jax.experimental import pallas as pl
from jax.experimental.pallas import tpu as pltpu
from jax.sharding import PartitionSpec as P

HEADS = 16
BF = jnp.bfloat16
F32 = jnp.float32
VMEM_BYTES = 56 * 1024 * 1024


def nn(a, b):
    return lax.dot_general(a, b, (((1,), (0,)), ((), ())), preferred_element_type=F32)


def nt(a, b):
    return lax.dot_general(a, b, (((1,), (1,)), ((), ())), preferred_element_type=F32)


def tn(a, b):
    return lax.dot_general(a, b, (((0,), (0,)), ((), ())), preferred_element_type=F32)


def one_hot(index_ref, width):
    rows = index_ref.shape[0]
    columns = lax.broadcasted_iota(jnp.int32, (rows, width), 1)
    return jnp.where(columns == index_ref[...], 1.0, 0.0).astype(BF)


def pack_kernel(tok_ref, cot_ref, index_ref, *refs):
    both = refs[-1]
    rows = tok_ref.shape[0]
    both[:rows] = tok_ref[...]
    both[rows:] = cot_ref[...]
    take = index_ref.shape[0] // (len(refs) - 1)
    for c, out in enumerate(refs[:-1]):
        columns = lax.broadcasted_iota(jnp.int32, (take, 2 * rows), 1)
        picked = jnp.where(columns == index_ref[c * take : (c + 1) * take], 1.0, 0.0).astype(BF)
        out[...] = nn(picked, both[...]).astype(BF)


def unpack_kernel(chunks, *refs):
    backs, index_ref, out_tok, out_cot, both = refs[:chunks], refs[chunks], refs[-3], refs[-2], refs[-1]
    take = backs[0].shape[0]
    for c, back in enumerate(backs):
        both[c * take : (c + 1) * take] = back[...]
    rows = out_tok.shape[0]
    for w, out in enumerate((out_tok, out_cot)):
        columns = lax.broadcasted_iota(jnp.int32, (rows, chunks * take), 1)
        picked = jnp.where(columns == index_ref[w * rows : (w + 1) * rows], 1.0, 0.0).astype(BF)
        out[...] = nn(picked, both[...]).astype(BF)


def face_kernel(scal_ref, face_ref, fcot_ref, gain_ref, normed_ref, early_ref):
    hidden = face_ref[...].astype(F32)
    inverse = lax.rsqrt(jnp.mean(hidden * hidden, axis=-1, keepdims=True) + 1e-06)
    normed = (hidden * inverse * gain_ref[...]).astype(BF)
    normed_ref[...] = normed
    early_ref[...] = jnp.where(scal_ref[0] == 0, fcot_ref[...], normed)


def edge_kernel(
    scal_ref, arrived_ref, index_ref, turn_ref, gain_ref, z_ref, g_ref, normed_ref, early_ref
):
    half = z_ref.shape[1] // 2
    edges = z_ref.shape[0]
    picked = one_hot(index_ref, arrived_ref.shape[0])
    first = nn(picked, arrived_ref[:, :half])
    second = nn(picked, arrived_ref[:, half:])
    cosine = turn_ref[:, 0:1]
    sine = turn_ref[:, 1:2]
    turned = jnp.concatenate(
        [cosine * first - sine * second, sine * first + cosine * second], axis=1
    )
    hidden = turned[:edges]
    z_ref[...] = hidden.astype(BF)
    g = turned[edges:].astype(BF)
    g_ref[...] = g
    inverse = lax.rsqrt(jnp.mean(hidden * hidden, axis=-1, keepdims=True) + 1e-06)
    normed = (hidden * inverse * gain_ref[...]).astype(BF)
    normed_ref[...] = normed
    early_ref[...] = jnp.where(scal_ref[0] == 0, g, normed)


def layer_kernel(
    lines,
    aliased,
    scal_ref,
    face_ref,
    fcot_ref,
    z_edge_ref,
    g_edge_ref,
    normed_face_ref,
    normed_edge_ref,
    back_index_ref,
    turn_ref,
    gain_ref,
    wqkv_ref,
    wo_ref,
    *refs,
):
    refs = refs[2:] if aliased else refs
    (
        face_out,
        face_grad,
        back_ref,
        keep_a,
        send_a,
        keep_b,
        send_b,
        gain_part,
        z_s,
        g_s,
        norm_s,
        qkv_s,
        dm_s,
        mix_s,
        stk_s,
        dn_s,
        y_s,
        edge_s,
    ) = refs
    width = z_s.shape[1]
    half = width // 2
    face_len = face_ref.shape[2]
    edges = z_edge_ref.shape[0]
    edge_len = edges // lines
    length = face_len + edge_len
    faces = lines * face_len
    head_dim = width // HEADS
    scale = head_dim ** (-0.5)
    gain = gain_ref[...]

    for l in range(lines):
        z_s[l * face_len : (l + 1) * face_len] = face_ref[0, l]
        g_s[l * face_len : (l + 1) * face_len] = fcot_ref[0, l]
    z_s[faces:] = z_edge_ref[...]
    g_s[faces:] = g_edge_ref[...]
    norm_s[:faces] = normed_face_ref[...]
    norm_s[faces:] = normed_edge_ref[...]

    tile = 512

    @pl.loop(0, 3 * width // tile)
    def _(j):
        cols = pl.ds(pl.multiple_of(j * tile, tile), tile)
        qkv_s[:, cols] = nn(norm_s[...], wqkv_ref[:, cols]).astype(BF)

    @pl.loop(0, width // tile)
    def _(j):
        cols = pl.ds(pl.multiple_of(j * tile, tile), tile)
        dm_s[:, cols] = nt(g_s[...], wo_ref[cols, :]).astype(BF)

    pair = 2 * head_dim
    low = lax.broadcasted_iota(jnp.int32, (length, pair), 1) < head_dim
    key_row = lax.broadcasted_iota(jnp.int32, (length, length), 0)

    def split(x):
        zero = jnp.zeros_like(x)
        return jnp.concatenate([jnp.where(low, x, zero), jnp.where(low, zero, x)], axis=0)

    @pl.loop(0, lines)
    def _(l):
        top = pl.ds(pl.multiple_of(l * face_len, face_len), face_len)
        bottom = pl.ds(pl.multiple_of(faces + l * edge_len, edge_len), edge_len)
        live = key_row < scal_ref[l] + face_len

        def load(ref, at):
            return jnp.concatenate([ref[top, at : at + pair], ref[bottom, at : at + pair]], axis=0)

        def store(ref, at, value):
            ref[top, at : at + pair] = value[:face_len].astype(BF)
            ref[bottom, at : at + pair] = value[face_len:].astype(BF)

        for p in range(HEADS // 2):
            at = p * pair
            q = load(qkv_s, at)
            k2 = split(load(qkv_s, width + at))
            v2 = split(load(qkv_s, 2 * width + at))
            dm = load(dm_s, at)
            scores = nt(k2, q) * scale
            d_probs = nt(v2, dm)
            probs_b, d_scores = [], []
            for h in range(2):
                part = slice(h * length, (h + 1) * length)
                s = jnp.where(live, scores[part], -1e30)
                e = jnp.exp(s - jnp.max(s, axis=0, keepdims=True))
                probs = e * (1.0 / jnp.sum(e, axis=0, keepdims=True))
                d = d_probs[part]
                inner = jnp.sum(probs * d, axis=0, keepdims=True)
                probs_b.append(probs.astype(BF))
                d_scores.append((probs * (d - inner) * scale).astype(BF))
            pb = jnp.concatenate(probs_b, axis=0)
            ds = jnp.concatenate(d_scores, axis=0)
            store(mix_s, at, tn(pb, v2))
            dv = nn(pb, dm)
            store(stk_s, 2 * width + at, jnp.where(low, dv[:length], dv[length:]))
            store(stk_s, at, tn(ds, k2))
            dk = nn(ds, q)
            store(stk_s, width + at, jnp.where(low, dk[:length], dk[length:]))

    @pl.loop(0, width // tile)
    def _(j):
        cols = pl.ds(pl.multiple_of(j * tile, tile), tile)
        y_s[:, cols] = (nn(mix_s[...], wo_ref[:, cols]) + z_s[:, cols].astype(F32)).astype(BF)
        dn_s[:, cols] = nt(stk_s[...], wqkv_ref[cols, :])

    gain_sum = jnp.zeros((1, width), F32)
    for i in range(2 * lines):
        size = face_len if i < lines else edge_len
        start = i * face_len if i < lines else faces + (i - lines) * edge_len
        at = slice(start, start + size)
        hidden = z_s[at].astype(F32)
        inverse = lax.rsqrt(jnp.mean(hidden * hidden, axis=-1, keepdims=True) + 1e-06)
        d_normed = dn_s[at]
        gain_sum = gain_sum + jnp.sum(d_normed * hidden * inverse, axis=0, keepdims=True)
        scaled = d_normed * gain
        mean = jnp.mean(scaled * hidden, axis=-1, keepdims=True)
        dz = inverse * scaled - hidden * (inverse * inverse * inverse * mean)
        dz = (g_s[at].astype(F32) + dz).astype(BF)
        if i < lines:
            face_out[0, i] = y_s[at]
            face_grad[0, i] = dz
        else:
            edge_s[edges + start - faces : edges + start - faces + size] = dz
    edge_s[:edges] = y_s[faces:]
    gain_part[...] = jnp.broadcast_to(gain_sum, gain_part.shape)
    cosine = turn_ref[:, 0:1]
    sine = turn_ref[:, 1:2]
    first = edge_s[:, :half].astype(F32)
    second = edge_s[:, half:].astype(F32)
    turned_first = (cosine * first + sine * second).astype(BF)
    turned_second = (cosine * second - sine * first).astype(BF)
    picked = one_hot(back_index_ref, 2 * edges)
    back_ref[:, :half] = nn(picked, turned_first).astype(BF)
    back_ref[:, half:] = nn(picked, turned_second).astype(BF)

    x_bit = scal_ref[lines]
    y_bit = scal_ref[lines + 1]

    @pl.when(x_bit == 0)
    def _():
        keep_a[...] = stk_s[:, :width]
        send_a[...] = stk_s[:, width : 2 * width]

    @pl.when(x_bit != 0)
    def _():
        send_a[...] = stk_s[:, :width]
        keep_a[...] = stk_s[:, width : 2 * width]

    @pl.when(y_bit == 0)
    def _():
        keep_b[...] = stk_s[:, 2 * width :]
        send_b[...] = mix_s[...]

    @pl.when(y_bit != 0)
    def _():
        send_b[...] = stk_s[:, 2 * width :]
        keep_b[...] = mix_s[...]


def weight_kernel(runs, parities, blocks, count, adds, pieces, column, scal_ref, *refs):
    operands = refs[:count]
    add_refs = refs[count : count + adds]
    outs = refs[count + adds : -3]
    lhs_s, lhs_t, rhs_s = refs[-3:]
    step = pl.program_id(0)
    depth, width = rhs_s.shape
    rows = depth // len(runs)
    part = width // 2
    size = part // blocks
    tile = width // (2 * pieces)

    def fill(at, src):
        for n, own in enumerate(parities):
            first = scal_ref[0] == (0 if own else 1)
            for b in range(blocks):
                left = src[:, 2 * b * size : (2 * b + 1) * size]
                right = src[:, (2 * b + 1) * size : (2 * b + 2) * size]
                to = n * part + b * size
                lhs_s[at : at + src.shape[0], to : to + size] = jnp.where(first, left, right)

    def load(swapped):
        for i, (faces, edges, chunk, late) in enumerate(runs):
            late_rows = operands[late][...]
            edge = operands[edges[swapped]][...]
            front = rows - edge.shape[0]
            face = operands[faces[swapped]][chunk * front : (chunk + 1) * front]
            at = i * rows
            if swapped:
                fill(at, late_rows)
                rhs_s[at : at + front] = face
                rhs_s[at + front : at + rows] = edge
            else:
                fill(at, face)
                fill(at + front, edge)
                rhs_s[at : at + rows] = late_rows

    @pl.when((step == 0) & (scal_ref[1] == 0))
    def _():
        load(0)

    @pl.when((step == 0) & (scal_ref[1] != 0))
    def _():
        load(1)

    @pl.when(step == 0)
    def _():
        for n in range(0, lhs_t.shape[0], 128):
            lhs_t[n : n + 128] = lhs_s[:, n : n + 128].T

    col = column(step, scal_ref)
    total = nn(lhs_t[...], rhs_s[:, pl.ds(pl.multiple_of(col * tile, tile), tile)])
    for ref in add_refs:
        total = total + ref[...]
    if len(outs) == 1:
        outs[0][...] = total
    else:
        for n, out in enumerate(outs):

            @pl.when(step == n)
            def _(out=out):
                out[...] = total


def weight_part(scal, runs, parities, blocks, operands, adds, pieces, halved, deps, tracked):
    width = operands[-1].shape[1]
    tile = width // (2 * pieces)
    rows = len(parities) * (width // 2)
    depth = len(runs) * operands[runs[0][3]].shape[0]

    def column(j, s):
        if not halved:
            return j
        second = j // pieces
        return ((1 - s[2]) + second * (2 * s[2] - 1)) * pieces + j % pieces

    def kernel(scal_ref, *refs):
        refs = refs[: len(operands) + len(adds)] + refs[len(operands) + len(adds) + len(deps) :]
        weight_kernel(
            runs, parities, blocks, len(operands), len(adds), pieces, column, scal_ref, *refs
        )

    whole = [pl.BlockSpec(o.shape, lambda j, s: (0, 0)) for o in operands]
    add_specs = [
        pl.BlockSpec((rows, tile), lambda j, s, at=at: (at, column(j, s))) for _, at in adds
    ]
    if halved:
        out_specs = [pl.BlockSpec((rows, tile), lambda j, s: (0, 0))] * (2 * pieces)
        out_shape = [jax.ShapeDtypeStruct((rows, tile), F32)] * (2 * pieces)
    else:
        out_specs = [pl.BlockSpec((rows, tile), lambda j, s: (0, j))]
        out_shape = [jax.ShapeDtypeStruct((rows, width), F32)]
    return pl.pallas_call(
        kernel,
        grid_spec=pltpu.PrefetchScalarGridSpec(
            num_scalar_prefetch=1,
            grid=(2 * pieces,),
            in_specs=whole + add_specs + [pl.BlockSpec(memory_space=pl.ANY)] * len(deps),
            out_specs=out_specs,
            scratch_shapes=[
                pltpu.VMEM((depth, rows), BF),
                pltpu.VMEM((rows, depth), BF),
                pltpu.VMEM((depth, width), BF),
            ],
        ),
        out_shape=out_shape,
        compiler_params=pltpu.CompilerParams(vmem_limit_bytes=VMEM_BYTES),
        cost_estimate=pl.CostEstimate(
            flops=2 * rows * depth * width, bytes_accessed=tracked, transcendentals=0
        ),
        name="weight_part",
    )(scal, *operands, *[a for a, _ in adds], *deps)


def block_kernel(blocks, count, scal_ref, *refs):
    groups = (refs[:count], refs[count : 2 * count])
    outs = refs[2 * count :]
    columns = groups[0][0].shape[1]
    size = groups[0][0].shape[0] // blocks
    for o, out in enumerate(outs):
        at = pl.ds(pl.multiple_of((scal_ref[0] ^ o) * size, size), size)
        for n, parts in enumerate(groups):
            total = parts[0][at]
            for p in parts[1:]:
                total = total + p[at]
            out[:, n * columns : (n + 1) * columns] = total


def sum_kernel(factor, scal_ref, *refs):
    total = refs[0][...]
    for ref in refs[1:-1]:
        total = total + ref[...]
    refs[-1][...] = total * factor


def place_kernel(pieces, devices, scal_ref, *refs):
    qkv_ref, out_ref = refs[-2], refs[-1]
    width = out_ref.shape[1]
    bits = devices.bit_length() - 1
    for n in range(pieces):
        for o in range(devices):
            src = refs[n * devices + o]
            part = src.shape[1] // 2
            device = scal_ref[0] ^ o
            for group in range(2):
                value = slice(group * part, (group + 1) * part)
                rest = [b for b in range(bits) if b != group]
                at = ((device >> rest[0]) & 1) * (width // 2) + n * (width // 2 // pieces)
                unit = width // 2 // pieces
                for b in rest[1:]:
                    unit = unit // 2
                    at = at + ((device >> b) & 1) * unit
                which = (device >> group) & 1
                if group == 0:
                    at = pl.multiple_of(at + which * width, part)
                    qkv_ref[:, pl.ds(at, part)] = src[:, value]
                else:

                    @pl.when(which == 0)
                    def _(src=src, value=value, at=at, part=part):
                        cols = pl.ds(pl.multiple_of(at + 2 * width, part), part)
                        qkv_ref[:, cols] = src[:, value]

                    @pl.when(which != 0)
                    def _(src=src, value=value, at=at, part=part):
                        out_ref[:, pl.ds(pl.multiple_of(at, part), part)] = src[:, value]


def exchange(x, axis, bits, size):
    return lax.ppermute(x, axis, [(i, i ^ bits) for i in range(size)])


def whole_call(kernel, name, scal, out_shape, operands, deps=(), scratch=(), flops=0):
    def body(scal_ref, *refs):
        kernel(scal_ref, *refs[: len(operands)], *refs[len(operands) + len(deps) :])

    def spec(shape):
        return pl.BlockSpec(shape, lambda i, s: (0,) * len(shape))

    moved = sum(int(np.prod(o.shape)) * o.dtype.itemsize for o in [*operands, *out_shape])
    return pl.pallas_call(
        body,
        grid_spec=pltpu.PrefetchScalarGridSpec(
            num_scalar_prefetch=1,
            grid=(1,),
            in_specs=[spec(o.shape) for o in operands]
            + [pl.BlockSpec(memory_space=pl.ANY)] * len(deps),
            out_specs=[spec(o.shape) for o in out_shape],
            scratch_shapes=list(scratch),
        ),
        out_shape=out_shape,
        compiler_params=pltpu.CompilerParams(vmem_limit_bytes=VMEM_BYTES),
        cost_estimate=pl.CostEstimate(flops=flops, bytes_accessed=moved, transcendentals=0),
        name=name,
    )(scal, *operands, *deps)


def local(
    face_tokens,
    edge_tokens,
    face_cotangent,
    edge_cotangent,
    rotation,
    counts,
    norm_gain,
    qkv_weight,
    out_weight,
):
    T = lax.axis_size("tile")
    D = lax.axis_size("dp")
    me_t = lax.axis_index("tile")
    me_d = lax.axis_index("dp")
    LD, FL, width = face_tokens.shape[1:]
    K = edge_tokens.shape[1]
    EL = K * T
    NLG = edge_tokens.shape[2]
    length = FL + EL
    chunks = 2
    lines = LD // chunks
    RB = lines * K
    packed = T * 2 * RB
    factor = float(D * T * LD * length) ** (-0.5)
    x_bit = (me_d % 2).astype(jnp.int32)
    y_bit = ((me_d // 2) % 2).astype(jnp.int32)
    gain = norm_gain.reshape(1, width)

    def struct(*shape, dtype=BF):
        return jax.ShapeDtypeStruct(shape, dtype)

    order = np.zeros((chunks, T, 2, lines, K), np.int32)
    for c in range(chunks):
        for w in range(2):
            t, l, k = np.meshgrid(np.arange(T), np.arange(lines), np.arange(K), indexing="ij")
            order[c, :, w] = w * K * NLG + k * NLG + t * LD + c * lines + l
    sent = whole_call(
        lambda s, *refs: pack_kernel(*refs),
        "pack",
        y_bit.reshape(1),
        [struct(packed, width)] * chunks,
        [
            edge_tokens.reshape(K * NLG, width),
            edge_cotangent.reshape(K * NLG, width),
            jnp.asarray(order.reshape(-1, 1)),
        ],
        scratch=[pltpu.VMEM((2 * K * NLG, width), BF)],
    )
    arrived = [lax.all_to_all(s, "tile", split_axis=0, concat_axis=0, tiled=True) for s in sent]

    face_rows = face_tokens.reshape(LD * FL, width)
    face_cots = face_cotangent.reshape(LD * FL, width)
    face_normed, face_early = whole_call(
        face_kernel,
        "face_norm",
        y_bit.reshape(1),
        [struct(LD * FL, width)] * 2,
        [face_rows, face_cots, gain],
    )
    got_face_a = exchange(face_normed, "dp", 1, D)
    got_face_b = exchange(face_early, "dp", 2, D)

    my_turns = lax.dynamic_slice_in_dim(rotation, me_t * LD, LD)
    my_counts = lax.dynamic_slice_in_dim(counts, me_t * LD, LD)
    spos = np.arange(EL)
    edge_parts, results, got_edges, got_late = [], [], [], []
    faces = None
    for c in range(chunks):
        turns = my_turns[c * lines : (c + 1) * lines]
        flip = turns >= 2
        pos = jnp.where(flip[:, None], EL - 1 - spos[None, :], spos[None, :])
        row = (pos // K) * (2 * RB) + jnp.arange(lines)[:, None] * K + pos % K
        index = jnp.concatenate([row, row + RB], axis=0).reshape(-1, 1).astype(jnp.int32)
        cosine = (turns == 0).astype(F32) - (turns == 2).astype(F32)
        sine = (turns == 1).astype(F32) - (turns == 3).astype(F32)
        turn = jnp.stack([cosine, sine], axis=-1)
        turn = jnp.broadcast_to(turn[None, :, None, :], (2, lines, EL, 2)).reshape(-1, 2)
        sk = np.arange(T)[:, None, None, None] * K + np.arange(K)[None, None, None, :]
        bk = jnp.where(flip[None, None, :, None], EL - 1 - sk, sk)
        back_index = (
            jnp.arange(2)[None, :, None, None] * (lines * EL)
            + jnp.arange(lines)[None, None, :, None] * EL
            + bk
        )
        back_index = back_index.reshape(-1, 1).astype(jnp.int32)
        scal = jnp.concatenate([my_counts[c * lines : (c + 1) * lines], jnp.stack([x_bit, y_bit])])
        edges = lines * EL
        z_edge, g_edge, normed_edge, early_edge = whole_call(
            edge_kernel,
            "edge_norm",
            y_bit.reshape(1),
            [struct(edges, width)] * 4,
            [arrived[c], index, turn, gain],
        )
        edge_parts.append((normed_edge, g_edge))
        got_edges.append((exchange(normed_edge, "dp", 1, D), exchange(early_edge, "dp", 2, D)))
        rows_all = lines * length
        row_shape = (rows_all, width)
        face_spec = pl.BlockSpec((1, lines, FL, width), lambda i, s, c=c: (0, c, 0, 0))
        normed_spec = pl.BlockSpec((lines * FL, width), lambda i, s, c=c: (c, 0))

        def full(shape):
            return pl.BlockSpec(shape, lambda i, s: (0,) * len(shape))

        operands = [
            face_tokens,
            face_cotangent,
            z_edge,
            g_edge,
            face_normed,
            normed_edge,
            back_index,
            turn,
            gain,
            qkv_weight,
            out_weight,
        ]
        in_specs = [face_spec, face_spec] + [full(o.shape) for o in operands[2:]]
        in_specs[4] = normed_spec
        if faces is not None:
            in_specs += [pl.BlockSpec(memory_space=pl.ANY)] * 2
            operands += list(faces)
        outs = pl.pallas_call(
            functools.partial(layer_kernel, lines, faces is not None),
            grid_spec=pltpu.PrefetchScalarGridSpec(
                num_scalar_prefetch=1,
                grid=(1,),
                in_specs=in_specs,
                out_specs=[face_spec, face_spec, full((packed, width))]
                + [full(row_shape)] * 4
                + [full((8, width))],
                scratch_shapes=[
                    pltpu.VMEM(row_shape, BF),
                    pltpu.VMEM(row_shape, BF),
                    pltpu.VMEM(row_shape, BF),
                    pltpu.VMEM((rows_all, 3 * width), BF),
                    pltpu.VMEM(row_shape, BF),
                    pltpu.VMEM(row_shape, BF),
                    pltpu.VMEM((rows_all, 3 * width), BF),
                    pltpu.VMEM(row_shape, F32),
                    pltpu.VMEM(row_shape, BF),
                    pltpu.VMEM((2 * edges, width), BF),
                ],
            ),
            out_shape=[struct(*face_tokens.shape)] * 2
            + [struct(packed, width)]
            + [struct(*row_shape)] * 4
            + [struct(8, width, dtype=F32)],
            input_output_aliases={12: 0, 13: 1} if faces is not None else {},
            compiler_params=pltpu.CompilerParams(vmem_limit_bytes=VMEM_BYTES),
            cost_estimate=pl.CostEstimate(
                flops=2 * rows_all * width * width * 8 * 2, bytes_accessed=1 << 24, transcendentals=0
            ),
            name="layer",
        )(scal, *operands)
        faces = outs[:2]
        results.append(outs[2:])
        got_late.append((exchange(outs[4], "dp", 1, D), exchange(outs[6], "dp", 2, D)))
    returned = [
        lax.all_to_all(r[0], "tile", split_axis=0, concat_axis=0, tiled=True) for r in results
    ]

    gain_sum = sum(r[5] for r in results)
    for b in range(D.bit_length() - 1):
        gain_sum = gain_sum + exchange(gain_sum, "dp", 1 << b, D)
    for b in range(T.bit_length() - 1):
        gain_sum = gain_sum + exchange(gain_sum, "tile", 1 << b, T)

    blocks = T // 2
    chip = (me_t // 2).astype(jnp.int32)
    core = (me_t % 2).astype(jnp.int32)
    pieces = 2
    size = width // T
    bits = D.bit_length() - 1
    groups = []
    for group in range(2):
        first = [b for b in range(bits) if b != group][0]
        swap = y_bit if group else jnp.zeros_like(y_bit)
        scal = jnp.stack([core, swap, ((me_d >> first) & 1).astype(jnp.int32)])
        late = [r[1 + 2 * group] for r in results]
        got_face = (got_face_a, got_face_b)[group]
        normed_e, g_e = [e[0] for e in edge_parts], [e[1] for e in edge_parts]
        got_e = [e[group] for e in got_edges]
        got_l = [e[group] for e in got_late]
        operands = [face_normed, face_cots, *normed_e, *g_e, got_face, got_e[0], late[0], late[1], got_l[0]]
        runs = [((0, 1), (2, 4), 0, 8), ((0, 1), (3, 5), 1, 9), ((6, 6), (7, 7), 0, 10)]
        start = weight_part(
            scal, runs, (False, True), blocks, operands, [], pieces, False,
            [returned[0]] if group == 0 else [], 8 << 20,
        )[0]
        groups.append((scal, [got_face, got_e[1], got_l[1]], start, first))
    theirs = []
    runs = [((0, 0), (1, 1), 1, 2)]
    for scal, operands, start, first in groups:
        send = weight_part(
            scal, runs, (False,), blocks, operands, [(start, 0)], pieces, False, [], 8 << 20
        )[0]
        theirs.append(exchange(send, "tile", 1, T))
    halves = []
    for group, (scal, operands, start, first) in enumerate(groups):
        outs = weight_part(
            scal, runs, (True,), blocks, operands, [(start, 1), (theirs[group], 0)], pieces, True,
            [], 8 << 20,
        )
        parts = []
        for n in range(pieces):
            both = [outs[pieces + n], exchange(outs[n], "dp", 1 << first, D)]
            for b in range(bits):
                if b in (group, first):
                    continue
                columns = both[0].shape[1] // 2
                mine = (me_d >> b) & 1
                keep = [lax.dynamic_slice_in_dim(p, mine * columns, columns, 1) for p in both]
                give = [lax.dynamic_slice_in_dim(p, (1 - mine) * columns, columns, 1) for p in both]
                both = [sum(keep), exchange(sum(give), "dp", 1 << b, D)]
            parts.append(both)
        halves.append(parts)
    placed = []
    for n in range(pieces):
        parts = [*halves[0][n], *halves[1][n]]
        columns = 2 * parts[0].shape[1]
        outs = whole_call(
            functools.partial(block_kernel, blocks, 2),
            "row_blocks",
            chip.reshape(1),
            [struct(size, columns, dtype=F32)] * blocks,
            parts,
            deps=[returned[1], gain_sum] if n == 0 else [],
        )
        got = [exchange(outs[o], "tile", 2 * o, T) for o in range(1, blocks)]
        (mine,) = whole_call(
            functools.partial(sum_kernel, factor),
            "block_sum",
            chip.reshape(1),
            [struct(size, columns, dtype=F32)],
            [outs[0], *got],
        )
        placed += [mine] + [exchange(mine, "dp", o, D) for o in range(1, D)]

    back_order = np.zeros((2, K, NLG), np.int32)
    for w in range(2):
        k, t, c, l = np.meshgrid(
            np.arange(K), np.arange(T), np.arange(chunks), np.arange(lines), indexing="ij"
        )
        back_order[w] = (c * packed + t * 2 * RB + w * RB + l * K + k).reshape(K, NLG)
    edge_output, edge_grad = whole_call(
        lambda s, *refs: unpack_kernel(chunks, *refs),
        "unpack",
        chip.reshape(1),
        [struct(K * NLG, width)] * 2,
        [*returned, jnp.asarray(back_order.reshape(-1, 1))],
        scratch=[pltpu.VMEM((chunks * packed, width), BF)],
    )
    qkv_grad, out_grad = whole_call(
        functools.partial(place_kernel, pieces, D),
        "place",
        me_d.astype(jnp.int32).reshape(1),
        [struct(size, 3 * width, dtype=F32), struct(size, width, dtype=F32)],
        placed,
    )
    gain_grad = lax.dynamic_slice_in_dim(gain_sum[0], me_t * size, size) * factor
    shape = edge_tokens.shape
    return (
        faces[0],
        edge_output.reshape(shape),
        faces[1],
        edge_grad.reshape(shape),
        qkv_grad,
        out_grad,
        gain_grad,
    )


def solution(mesh):
    return jax.shard_map(
        local,
        mesh=mesh,
        in_specs=(
            P("dp", "tile", None, None),
            P("dp", "tile", None, None),
            P("dp", "tile", None, None),
            P("dp", "tile", None, None),
            P(),
            P(),
            P(),
            P(),
            P(),
        ),
        out_specs=(
            P("dp", "tile", None, None),
            P("dp", "tile", None, None),
            P("dp", "tile", None, None),
            P("dp", "tile", None, None),
            P("tile", None),
            P("tile", None),
            P("tile"),
        ),
        check_vma=False,
    )
```

```python
import functools

import jax
import jax.numpy as jnp
import numpy as np
from jax import lax
from jax.experimental import pallas as pl
from jax.experimental.pallas import tpu as pltpu
from jax.sharding import PartitionSpec as P

HEADS = 16
BF = jnp.bfloat16
F32 = jnp.float32
VMEM_BYTES = 60 * 1024 * 1024


def nn(a, b):
    return lax.dot_general(a, b, (((1,), (0,)), ((), ())), preferred_element_type=F32)


def nt(a, b):
    return lax.dot_general(a, b, (((1,), (1,)), ((), ())), preferred_element_type=F32)


def tn(a, b):
    return lax.dot_general(a, b, (((0,), (0,)), ((), ())), preferred_element_type=F32)


def one_hot(index_ref, width):
    rows = index_ref.shape[0]
    columns = lax.broadcasted_iota(jnp.int32, (rows, width), 1)
    return jnp.where(columns == index_ref[...], 1.0, 0.0).astype(BF)


def pack_kernel(tok_ref, cot_ref, index_ref, *refs):
    both = refs[-1]
    rows = tok_ref.shape[0]
    both[:rows] = tok_ref[...]
    both[rows:] = cot_ref[...]
    take = index_ref.shape[0] // (len(refs) - 1)
    for c, out in enumerate(refs[:-1]):
        columns = lax.broadcasted_iota(jnp.int32, (take, 2 * rows), 1)
        picked = jnp.where(columns == index_ref[c * take : (c + 1) * take], 1.0, 0.0).astype(BF)
        out[...] = nn(picked, both[...]).astype(BF)


def unpack_kernel(chunks, *refs):
    backs, index_ref, out_tok, out_cot, both = refs[:chunks], refs[chunks], refs[-3], refs[-2], refs[-1]
    take = backs[0].shape[0]
    for c, back in enumerate(backs):
        both[c * take : (c + 1) * take] = back[...]
    rows = out_tok.shape[0]
    for w, out in enumerate((out_tok, out_cot)):
        columns = lax.broadcasted_iota(jnp.int32, (rows, chunks * take), 1)
        picked = jnp.where(columns == index_ref[w * rows : (w + 1) * rows], 1.0, 0.0).astype(BF)
        out[...] = nn(picked, both[...]).astype(BF)


def face_kernel(scal_ref, face_ref, fcot_ref, gain_ref, normed_ref, early_ref):
    hidden = face_ref[...].astype(F32)
    inverse = lax.rsqrt(jnp.mean(hidden * hidden, axis=-1, keepdims=True) + 1e-06)
    normed = (hidden * inverse * gain_ref[...]).astype(BF)
    normed_ref[...] = normed
    early_ref[...] = jnp.where(scal_ref[0] == 0, fcot_ref[...], normed)


def flips(line_ref, rotation_ref, base, lines):
    line = line_ref[:, 2:3]
    flip = jnp.zeros_like(line)
    for l in range(lines):
        turned = (rotation_ref[base + l] >= 2).astype(jnp.int32)
        flip = jnp.where(line == l, turned, flip)
    return jnp.where(flip != 0, line_ref[:, 1:2], line_ref[:, 0:1])


def turn_pair(rotation_ref, at):
    turn = rotation_ref[at]
    cosine = (turn == 0).astype(F32) - (turn == 2).astype(F32)
    sine = (turn == 1).astype(F32) - (turn == 3).astype(F32)
    return cosine, sine


def one_hot_rows(index, width):
    columns = lax.broadcasted_iota(jnp.int32, (index.shape[0], width), 1)
    return jnp.where(columns == index, 1.0, 0.0).astype(BF)


def edge_kernel(
    lines,
    scal_ref,
    rotation_ref,
    counts_ref,
    arrived_ref,
    index_ref,
    gain_ref,
    z_ref,
    g_ref,
    normed_ref,
    early_ref,
):
    half = z_ref.shape[1] // 2
    edges = z_ref.shape[0]
    edge_len = edges // lines
    base = scal_ref[0]
    index = flips(index_ref, rotation_ref, base, lines)
    picked = one_hot_rows(index, arrived_ref.shape[0])
    first = nn(picked, arrived_ref[:, :half])
    second = nn(picked, arrived_ref[:, half:])
    for l in range(lines):
        cosine, sine = turn_pair(rotation_ref, base + l)

        def turned(at):
            u, v = first[at : at + edge_len], second[at : at + edge_len]
            return jnp.concatenate([cosine * u - sine * v, sine * u + cosine * v], axis=1)

        rows = slice(l * edge_len, (l + 1) * edge_len)
        hidden = turned(l * edge_len)
        g = turned(edges + l * edge_len).astype(BF)
        z_ref[rows] = hidden.astype(BF)
        g_ref[rows] = g
        inverse = lax.rsqrt(jnp.mean(hidden * hidden, axis=-1, keepdims=True) + 1e-06)
        normed = (hidden * inverse * gain_ref[...]).astype(BF)
        normed_ref[rows] = normed
        early_ref[rows] = jnp.where(scal_ref[2] == 0, g, normed)


def layer_kernel(
    lines,
    aliased,
    drop,
    scal_ref,
    rotation_ref,
    counts_ref,
    face_ref,
    fcot_ref,
    z_edge_ref,
    g_edge_ref,
    normed_face_ref,
    normed_edge_ref,
    back_index_ref,
    gain_ref,
    wqkv_ref,
    wo_ref,
    *refs,
):
    refs = refs[drop + (2 if aliased else 0) :]
    base = scal_ref[0]
    (
        face_out,
        face_grad,
        back_ref,
        keep_a,
        send_a,
        keep_b,
        send_b,
        gain_part,
        z_s,
        g_s,
        norm_s,
        qkv_s,
        dm_s,
        mix_s,
        stk_s,
        dn_s,
        y_s,
        edge_s,
    ) = refs
    width = z_s.shape[1]
    half = width // 2
    face_len = face_ref.shape[2]
    edges = z_edge_ref.shape[0]
    edge_len = edges // lines
    length = face_len + edge_len
    faces = lines * face_len
    head_dim = width // HEADS
    scale = head_dim ** (-0.5)
    gain = gain_ref[...]

    for l in range(lines):
        z_s[l * face_len : (l + 1) * face_len] = face_ref[0, l]
        g_s[l * face_len : (l + 1) * face_len] = fcot_ref[0, l]
    z_s[faces:] = z_edge_ref[...]
    g_s[faces:] = g_edge_ref[...]
    norm_s[:faces] = normed_face_ref[...]
    norm_s[faces:] = normed_edge_ref[...]

    tile = 512

    @pl.loop(0, 3 * width // tile)
    def _(j):
        cols = pl.ds(pl.multiple_of(j * tile, tile), tile)
        qkv_s[:, cols] = nn(norm_s[...], wqkv_ref[:, cols]).astype(BF)

    @pl.loop(0, width // tile)
    def _(j):
        cols = pl.ds(pl.multiple_of(j * tile, tile), tile)
        dm_s[:, cols] = nt(g_s[...], wo_ref[cols, :]).astype(BF)

    pair = 2 * head_dim
    low = lax.broadcasted_iota(jnp.int32, (length, pair), 1) < head_dim
    key_row = lax.broadcasted_iota(jnp.int32, (length, length), 0)

    def split(x):
        zero = jnp.zeros_like(x)
        return jnp.concatenate([jnp.where(low, x, zero), jnp.where(low, zero, x)], axis=0)

    @pl.loop(0, lines)
    def _(l):
        top = pl.ds(pl.multiple_of(l * face_len, face_len), face_len)
        bottom = pl.ds(pl.multiple_of(faces + l * edge_len, edge_len), edge_len)
        live = key_row < counts_ref[base + l] + face_len

        def load(ref, at):
            return jnp.concatenate([ref[top, at : at + pair], ref[bottom, at : at + pair]], axis=0)

        def store(ref, at, value):
            ref[top, at : at + pair] = value[:face_len].astype(BF)
            ref[bottom, at : at + pair] = value[face_len:].astype(BF)

        for p in range(HEADS // 2):
            at = p * pair
            q = load(qkv_s, at)
            k2 = split(load(qkv_s, width + at))
            v2 = split(load(qkv_s, 2 * width + at))
            dm = load(dm_s, at)
            scores = nt(k2, q) * scale
            d_probs = nt(v2, dm)
            probs_b, d_scores = [], []
            for h in range(2):
                part = slice(h * length, (h + 1) * length)
                s = jnp.where(live, scores[part], -1e30)
                e = jnp.exp(s - jnp.max(s, axis=0, keepdims=True))
                probs = e * (1.0 / jnp.sum(e, axis=0, keepdims=True))
                d = d_probs[part]
                inner = jnp.sum(probs * d, axis=0, keepdims=True)
                probs_b.append(probs.astype(BF))
                d_scores.append((probs * (d - inner) * scale).astype(BF))
            pb = jnp.concatenate(probs_b, axis=0)
            ds = jnp.concatenate(d_scores, axis=0)
            store(mix_s, at, tn(pb, v2))
            dv = nn(pb, dm)
            store(stk_s, 2 * width + at, jnp.where(low, dv[:length], dv[length:]))
            store(stk_s, at, tn(ds, k2))
            dk = nn(ds, q)
            store(stk_s, width + at, jnp.where(low, dk[:length], dk[length:]))

    @pl.loop(0, width // tile)
    def _(j):
        cols = pl.ds(pl.multiple_of(j * tile, tile), tile)
        y_s[:, cols] = (nn(mix_s[...], wo_ref[:, cols]) + z_s[:, cols].astype(F32)).astype(BF)
        dn_s[:, cols] = nt(stk_s[...], wqkv_ref[cols, :])

    gain_sum = jnp.zeros((1, width), F32)
    for i in range(2 * lines):
        size = face_len if i < lines else edge_len
        start = i * face_len if i < lines else faces + (i - lines) * edge_len
        at = slice(start, start + size)
        hidden = z_s[at].astype(F32)
        inverse = lax.rsqrt(jnp.mean(hidden * hidden, axis=-1, keepdims=True) + 1e-06)
        d_normed = dn_s[at]
        gain_sum = gain_sum + jnp.sum(d_normed * hidden * inverse, axis=0, keepdims=True)
        scaled = d_normed * gain
        mean = jnp.mean(scaled * hidden, axis=-1, keepdims=True)
        dz = inverse * scaled - hidden * (inverse * inverse * inverse * mean)
        dz = (g_s[at].astype(F32) + dz).astype(BF)
        if i < lines:
            face_out[0, i] = y_s[at]
            face_grad[0, i] = dz
        else:
            edge_s[edges + start - faces : edges + start - faces + size] = dz
    edge_s[:edges] = y_s[faces:]
    lanes = gain_part.shape[1]
    for i in range(width // lanes):
        gain_part[i : i + 1] = gain_sum[:, i * lanes : (i + 1) * lanes]
    for i in range(2 * lines):
        cosine, sine = turn_pair(rotation_ref, base + i % lines)
        rows = slice(i * edge_len, (i + 1) * edge_len)
        u, v = edge_s[rows, :half].astype(F32), edge_s[rows, half:].astype(F32)
        edge_s[rows, :half] = (cosine * u + sine * v).astype(BF)
        edge_s[rows, half:] = (cosine * v - sine * u).astype(BF)
    picked = one_hot_rows(flips(back_index_ref, rotation_ref, base, lines), 2 * edges)
    back_ref[...] = nn(picked, edge_s[...]).astype(BF)

    x_bit = scal_ref[1]
    y_bit = scal_ref[2]

    @pl.when(x_bit == 0)
    def _():
        keep_a[...] = stk_s[:, :width]
        send_a[...] = stk_s[:, width : 2 * width]

    @pl.when(x_bit != 0)
    def _():
        send_a[...] = stk_s[:, :width]
        keep_a[...] = stk_s[:, width : 2 * width]

    @pl.when(y_bit == 0)
    def _():
        keep_b[...] = stk_s[:, 2 * width :]
        send_b[...] = mix_s[...]

    @pl.when(y_bit != 0)
    def _():
        send_b[...] = stk_s[:, 2 * width :]
        keep_b[...] = mix_s[...]


def weight_kernel(runs, parities, blocks, count, adds, gains, halved, scal_ref, *refs):
    operands = refs[:count]
    add_refs = refs[count : count + adds]
    gain_refs = refs[count + adds : count + adds + gains]
    outs = refs[count + adds + gains :]
    pieces = max(1, len(outs) // 2)
    width = operands[-1].shape[1]
    part = width // 2
    size = part // blocks
    tile = outs[0].shape[1]
    rows = len(parities) * part

    def pick(src):
        kept = []
        for own in parities:
            first = scal_ref[0] == (0 if own else 1)
            for b in range(blocks):
                left = src[:, 2 * b * size : (2 * b + 1) * size]
                right = src[:, (2 * b + 1) * size : (2 * b + 2) * size]
                kept.append(jnp.where(first, left, right))
        return jnp.concatenate(kept, axis=1)

    def run(swapped):
        early, late = [], []
        for faces, edges, chunk, late_at in runs:
            edge = operands[edges[swapped]]
            front = operands[late_at].shape[0] - edge.shape[0]
            early += [operands[faces[swapped]][chunk * front : (chunk + 1) * front], edge[...]]
            late.append(operands[late_at][...])
        early, late = jnp.concatenate(early, axis=0), jnp.concatenate(late, axis=0)
        lhs, rhs = (late, early) if swapped else (early, late)
        lhs = pick(lhs)
        if not halved:
            total = tn(lhs, rhs)
            for ref in add_refs:
                total = total + ref[:rows]
            outs[0][:rows] = total
            return
        for half in range(2):
            mine = (scal_ref[2] if half else 1 - scal_ref[2]) == 0
            cols = jnp.where(mine, rhs[:, :part], rhs[:, part:])
            total = tn(lhs, cols)
            for ref in add_refs:
                total = total + jnp.where(mine, ref[:rows, :part], ref[:rows, part:])
            for n in range(pieces):
                outs[half * pieces + n][:rows] = total[:, n * tile : (n + 1) * tile]

    @pl.when(scal_ref[1] == 0)
    def _():
        run(0)

    @pl.when(scal_ref[1] != 0)
    def _():
        run(1)

    if gains:
        total = gain_refs[0][...]
        for ref in gain_refs[1:]:
            total = total + ref[...]
        lanes = total.shape[1]
        if halved:
            total = total + add_refs[-1][rows:, :lanes]
        for out in outs:
            if out.shape[0] > rows:
                for n in range(tile // lanes):
                    out[rows:, n * lanes : (n + 1) * lanes] = total


def weight_part(scal, runs, parities, blocks, operands, adds, pieces, halved, gains, deps):
    width = operands[-1].shape[1]
    part = width // 2
    rows = len(parities) * part
    depth = len(runs) * operands[runs[0][3]].shape[0]
    extra = gains[0].shape[0] if gains else 0
    used = len(operands) + len(adds) + len(gains)

    def kernel(scal_ref, *refs):
        refs = refs[:used] + refs[used + len(deps) :]
        weight_kernel(
            runs, parities, blocks, len(operands), len(adds), len(gains), halved, scal_ref, *refs
        )

    def spec(shape, at=0):
        return pl.BlockSpec(shape, lambda i, s: (at, 0))

    add_specs = [
        spec(a.shape) if at is None else spec((rows, width), at) for a, at in adds
    ]
    if halved:
        tile = part // pieces
        shapes = [
            (rows + (extra if n % pieces == 0 else 0), tile) for n in range(2 * pieces)
        ]
    else:
        shapes = [(rows + extra, width)]
    return pl.pallas_call(
        kernel,
        grid_spec=pltpu.PrefetchScalarGridSpec(
            num_scalar_prefetch=1,
            grid=(1,),
            in_specs=[spec(o.shape) for o in operands]
            + add_specs
            + [spec(g.shape) for g in gains]
            + [pl.BlockSpec(memory_space=pl.ANY)] * len(deps),
            out_specs=[spec(s) for s in shapes],
        ),
        out_shape=[jax.ShapeDtypeStruct(s, F32) for s in shapes],
        compiler_params=pltpu.CompilerParams(vmem_limit_bytes=VMEM_BYTES),
        cost_estimate=pl.CostEstimate(
            flops=1 << 33 if len(runs) > 1 else 1024, bytes_accessed=1024, transcendentals=0
        ),
        name="weight_part",
    )(scal, *operands, *[a for a, _ in adds], *gains, *deps)


def block_kernel(blocks, count, scal_ref, *refs):
    groups = (refs[:count], refs[count : 2 * count])
    outs = refs[2 * count :]
    columns = groups[0][0].shape[1]
    size = groups[1][0].shape[0] // blocks
    whole = blocks * size
    for o, out in enumerate(outs):
        at = pl.ds(pl.multiple_of((scal_ref[0] ^ o) * size, size), size)
        for n, parts in enumerate(groups):
            total = parts[0][at]
            for p in parts[1:]:
                total = total + p[at]
            out[:size, n * columns : (n + 1) * columns] = total
        if out.shape[0] > size:
            total = groups[0][0][whole:]
            for p in groups[0][1:]:
                total = total + p[whole:]
            out[size:, :columns] = total
            out[size:, columns:] = total


def sum_kernel(factor, scal_ref, *refs):
    total = refs[0][...]
    for ref in refs[1:-1]:
        total = total + ref[...]
    refs[-1][...] = total * factor


def place_kernel(pieces, devices, scal_ref, *refs):
    qkv_ref, out_ref = refs[-2], refs[-1]
    width = out_ref.shape[1]
    bits = devices.bit_length() - 1
    for n in range(pieces):
        for o in range(devices):
            src = refs[n * devices + o]
            part = src.shape[1] // 2
            size = out_ref.shape[0]
            device = scal_ref[0] ^ o
            for group in range(2):
                value = (slice(0, size), slice(group * part, (group + 1) * part))
                rest = [b for b in range(bits) if b != group]
                at = ((device >> rest[0]) & 1) * (width // 2) + n * (width // 2 // pieces)
                unit = width // 2 // pieces
                for b in rest[1:]:
                    unit = unit // 2
                    at = at + ((device >> b) & 1) * unit
                which = (device >> group) & 1
                if group == 0:
                    at = pl.multiple_of(at + which * width, part)
                    qkv_ref[:, pl.ds(at, part)] = src[value]
                else:

                    @pl.when(which == 0)
                    def _(src=src, value=value, at=at, part=part):
                        cols = pl.ds(pl.multiple_of(at + 2 * width, part), part)
                        qkv_ref[:, cols] = src[value]

                    @pl.when(which != 0)
                    def _(src=src, value=value, at=at, part=part):
                        out_ref[:, pl.ds(pl.multiple_of(at, part), part)] = src[value]


def exchange(x, axis, bits, size):
    return lax.ppermute(x, axis, [(i, i ^ bits) for i in range(size)])


def whole_call(kernel, name, scal, out_shape, operands, deps=(), scratch=(), flops=0):
    scal = scal if isinstance(scal, tuple) else (scal,)

    def body(*refs):
        used = len(scal) + len(operands)
        kernel(*refs[:used], *refs[used + len(deps) :])

    def spec(shape):
        return pl.BlockSpec(shape, lambda i, *s: (0,) * len(shape))

    moved = sum(int(np.prod(o.shape)) * o.dtype.itemsize for o in [*operands, *out_shape])
    return pl.pallas_call(
        body,
        grid_spec=pltpu.PrefetchScalarGridSpec(
            num_scalar_prefetch=len(scal),
            grid=(1,),
            in_specs=[spec(o.shape) for o in operands]
            + [pl.BlockSpec(memory_space=pl.ANY)] * len(deps),
            out_specs=[spec(o.shape) for o in out_shape],
            scratch_shapes=list(scratch),
        ),
        out_shape=out_shape,
        compiler_params=pltpu.CompilerParams(vmem_limit_bytes=VMEM_BYTES),
        cost_estimate=pl.CostEstimate(flops=1024, bytes_accessed=1024, transcendentals=0),
        name=name,
    )(*scal, *operands, *deps)


def local(
    face_tokens,
    edge_tokens,
    face_cotangent,
    edge_cotangent,
    rotation,
    counts,
    norm_gain,
    qkv_weight,
    out_weight,
):
    T = lax.axis_size("tile")
    D = lax.axis_size("dp")
    me_t = lax.axis_index("tile")
    me_d = lax.axis_index("dp")
    LD, FL, width = face_tokens.shape[1:]
    K = edge_tokens.shape[1]
    EL = K * T
    NLG = edge_tokens.shape[2]
    length = FL + EL
    chunks = 2
    lines = LD // chunks
    RB = lines * K
    packed = T * 2 * RB
    factor = float(D * T * LD * length) ** (-0.5)
    x_bit = (me_d % 2).astype(jnp.int32)
    y_bit = ((me_d // 2) % 2).astype(jnp.int32)
    gain = norm_gain.reshape(1, width)

    def struct(*shape, dtype=BF):
        return jax.ShapeDtypeStruct(shape, dtype)

    order = np.zeros((chunks, T, 2, lines, K), np.int32)
    for c in range(chunks):
        for w in range(2):
            t, l, k = np.meshgrid(np.arange(T), np.arange(lines), np.arange(K), indexing="ij")
            order[c, :, w] = w * K * NLG + k * NLG + t * LD + c * lines + l
    sent = whole_call(
        lambda s, *refs: pack_kernel(*refs),
        "pack",
        y_bit.reshape(1),
        [struct(packed, width)] * chunks,
        [
            edge_tokens.reshape(K * NLG, width),
            edge_cotangent.reshape(K * NLG, width),
            jnp.asarray(order.reshape(-1, 1)),
        ],
        scratch=[pltpu.VMEM((2 * K * NLG, width), BF)],
    )
    arrived = [lax.all_to_all(s, "tile", split_axis=0, concat_axis=0, tiled=True) for s in sent]

    face_rows = face_tokens.reshape(LD * FL, width)
    face_cots = face_cotangent.reshape(LD * FL, width)
    face_normed, face_early = whole_call(
        face_kernel,
        "face_norm",
        y_bit.reshape(1),
        [struct(LD * FL, width)] * 2,
        [face_rows, face_cots, gain],
    )
    got_face_a = exchange(face_normed, "dp", 1, D)
    got_face_b = exchange(face_early, "dp", 2, D)

    edges = lines * EL
    l, p = np.meshgrid(np.arange(lines), np.arange(EL), indexing="ij")
    table = []
    for pos in (p, EL - 1 - p):
        row = (pos // K) * (2 * RB) + l * K + pos % K
        table.append(np.stack([row, row + RB]))
    table.append(np.stack([l, l]))
    index = jnp.asarray(np.stack(table, axis=-1).reshape(-1, 3).astype(np.int32))
    t, w, l, k = np.meshgrid(
        np.arange(T), np.arange(2), np.arange(lines), np.arange(K), indexing="ij"
    )
    pos = t * K + k
    table = [w * edges + l * EL + pos, w * edges + l * EL + EL - 1 - pos, l]
    back_index = jnp.asarray(np.stack(table, axis=-1).reshape(-1, 3).astype(np.int32))
    edge_parts, results, got_edges, got_late = [], [], [], []
    faces = None
    for c in range(chunks):
        base = (me_t * LD + c * lines).astype(jnp.int32)
        scal = (jnp.stack([base, x_bit, y_bit]), rotation, counts)
        z_edge, g_edge, normed_edge, early_edge = whole_call(
            functools.partial(edge_kernel, lines),
            "edge_norm",
            scal,
            [struct(edges, width)] * 4,
            [arrived[c], index, gain],
        )
        edge_parts.append((normed_edge, g_edge))
        got_edges.append((exchange(normed_edge, "dp", 1, D), exchange(early_edge, "dp", 2, D)))
        rows_all = lines * length
        row_shape = (rows_all, width)
        face_spec = pl.BlockSpec((1, lines, FL, width), lambda i, *s, c=c: (0, c, 0, 0))
        normed_spec = pl.BlockSpec((lines * FL, width), lambda i, *s, c=c: (c, 0))

        def full(shape):
            return pl.BlockSpec(shape, lambda i, *s: (0,) * len(shape))

        operands = [
            face_tokens,
            face_cotangent,
            z_edge,
            g_edge,
            face_normed,
            normed_edge,
            back_index,
            gain,
            qkv_weight,
            out_weight,
        ]
        in_specs = [face_spec, face_spec] + [full(o.shape) for o in operands[2:]]
        in_specs[4] = normed_spec
        held = [got_face_a, got_face_b, *got_edges[0]] if c else []
        if faces is not None:
            operands += list(faces)
        operands += held
        in_specs += [pl.BlockSpec(memory_space=pl.ANY)] * (len(operands) - len(in_specs))
        outs = pl.pallas_call(
            functools.partial(layer_kernel, lines, faces is not None, len(held)),
            grid_spec=pltpu.PrefetchScalarGridSpec(
                num_scalar_prefetch=3,
                grid=(1,),
                in_specs=in_specs,
                out_specs=[face_spec, face_spec, full((packed, width))]
                + [full(row_shape)] * 4
                + [full((8, width // 8))],
                scratch_shapes=[
                    pltpu.VMEM(row_shape, BF),
                    pltpu.VMEM(row_shape, BF),
                    pltpu.VMEM(row_shape, BF),
                    pltpu.VMEM((rows_all, 3 * width), BF),
                    pltpu.VMEM(row_shape, BF),
                    pltpu.VMEM(row_shape, BF),
                    pltpu.VMEM((rows_all, 3 * width), BF),
                    pltpu.VMEM(row_shape, F32),
                    pltpu.VMEM(row_shape, BF),
                    pltpu.VMEM((2 * edges, width), BF),
                ],
            ),
            out_shape=[struct(*face_tokens.shape)] * 2
            + [struct(packed, width)]
            + [struct(*row_shape)] * 4
            + [struct(8, width // 8, dtype=F32)],
            input_output_aliases={13: 0, 14: 1} if faces is not None else {},
            compiler_params=pltpu.CompilerParams(vmem_limit_bytes=VMEM_BYTES),
            cost_estimate=pl.CostEstimate(flops=1 << 35, bytes_accessed=1 << 20, transcendentals=0),
            name="layer",
        )(*scal, *operands)
        faces = outs[:2]
        results.append(outs[2:])
        got_late.append((exchange(outs[4], "dp", 1, D), exchange(outs[6], "dp", 2, D)))
    returned = [
        lax.all_to_all(r[0], "tile", split_axis=0, concat_axis=0, tiled=True) for r in results
    ]

    blocks = T // 2
    chip = (me_t // 2).astype(jnp.int32)
    core = (me_t % 2).astype(jnp.int32)
    pieces = 2
    size = width // T
    bits = D.bit_length() - 1
    groups = []
    for group in range(2):
        first = [b for b in range(bits) if b != group][0]
        swap = y_bit if group else jnp.zeros_like(y_bit)
        scal = jnp.stack([core, swap, ((me_d >> first) & 1).astype(jnp.int32)])
        late = [r[1 + 2 * group] for r in results]
        got_face = (got_face_a, got_face_b)[group]
        normed_e, g_e = [e[0] for e in edge_parts], [e[1] for e in edge_parts]
        got_e = [e[group] for e in got_edges]
        got_l = [e[group] for e in got_late]
        operands = [face_normed, face_cots, *normed_e, *g_e, got_face, got_e[0], late[0], late[1], got_l[0]]
        runs = [((0, 1), (2, 4), 0, 8), ((0, 1), (3, 5), 1, 9), ((6, 6), (7, 7), 0, 10)]
        start = weight_part(
            scal, runs, (False, True), blocks, operands, [], pieces, False, [],
            [returned[0], *got_edges[1], *got_late[0]] if group == 0 else [],
        )[0]
        groups.append((scal, [got_face, got_e[1], got_l[1]], start, first))
    theirs = []
    runs = [((0, 0), (1, 1), 1, 2)]
    gains = [[r[5] for r in results], []]
    for group, (scal, operands, start, first) in enumerate(groups):
        send = weight_part(
            scal, runs, (False,), blocks, operands, [(start, 0)], pieces, False, gains[group], [returned[1]] if group else []
        )[0]
        theirs.append(exchange(send, "tile", 1, T))
    halves = []
    for group, (scal, operands, start, first) in enumerate(groups):
        outs = weight_part(
            scal, runs, (True,), blocks, operands, [(start, 1), (theirs[group], None)], pieces, True,
            gains[group], [],
        )
        parts = []
        for n in range(pieces):
            both = [outs[pieces + n], exchange(outs[n], "dp", 1 << first, D)]
            for b in range(bits):
                if b in (group, first):
                    continue
                columns = both[0].shape[1] // 2
                mine = (me_d >> b) & 1
                keep = [lax.dynamic_slice_in_dim(p, mine * columns, columns, 1) for p in both]
                give = [lax.dynamic_slice_in_dim(p, (1 - mine) * columns, columns, 1) for p in both]
                both = [sum(keep), exchange(sum(give), "dp", 1 << b, D)]
            parts.append(both)
        halves.append(parts)
    placed = []
    for n in range(pieces):
        parts = [*halves[0][n], *halves[1][n]]
        columns = 2 * parts[0].shape[1]
        outs = whole_call(
            functools.partial(block_kernel, blocks, 2),
            "row_blocks",
            chip.reshape(1),
            [struct(size + (8 if n == 0 else 0), columns, dtype=F32)] * blocks,
            parts,
        )
        got = [exchange(outs[o], "tile", 2 * o, T) for o in range(1, blocks)]
        (mine,) = whole_call(
            functools.partial(sum_kernel, factor),
            "block_sum",
            chip.reshape(1),
            [struct(*outs[0].shape, dtype=F32)],
            [outs[0], *got],
        )
        placed += [mine] + [exchange(mine, "dp", o, D) for o in range(1, D)]

    back_order = np.zeros((2, K, NLG), np.int32)
    for w in range(2):
        k, t, c, l = np.meshgrid(
            np.arange(K), np.arange(T), np.arange(chunks), np.arange(lines), indexing="ij"
        )
        back_order[w] = (c * packed + t * 2 * RB + w * RB + l * K + k).reshape(K, NLG)
    edge_output, edge_grad = whole_call(
        lambda s, *refs: unpack_kernel(chunks, *refs),
        "unpack",
        chip.reshape(1),
        [struct(K * NLG, width)] * 2,
        [*returned, jnp.asarray(back_order.reshape(-1, 1))],
        scratch=[pltpu.VMEM((chunks * packed, width), BF)],
    )
    qkv_grad, out_grad = whole_call(
        functools.partial(place_kernel, pieces, D),
        "place",
        me_d.astype(jnp.int32).reshape(1),
        [struct(size, 3 * width, dtype=F32), struct(size, width, dtype=F32)],
        placed,
    )
    gain_sum = (placed[0] + placed[1])[size:, : width // 8].reshape(width)
    gain_grad = lax.dynamic_slice_in_dim(gain_sum, me_t * size, size)
    shape = edge_tokens.shape
    return (
        faces[0],
        edge_output.reshape(shape),
        faces[1],
        edge_grad.reshape(shape),
        qkv_grad,
        out_grad,
        gain_grad,
    )


def solution(mesh):
    return jax.shard_map(
        local,
        mesh=mesh,
        in_specs=(
            P("dp", "tile", None, None),
            P("dp", "tile", None, None),
            P("dp", "tile", None, None),
            P("dp", "tile", None, None),
            P(),
            P(),
            P(),
            P(),
            P(),
        ),
        out_specs=(
            P("dp", "tile", None, None),
            P("dp", "tile", None, None),
            P("dp", "tile", None, None),
            P("dp", "tile", None, None),
            P("tile", None),
            P("tile", None),
            P("tile"),
        ),
        check_vma=False,
    )
```

```python
import functools

import jax
import jax.numpy as jnp
import numpy as np
from jax import lax
from jax.experimental import pallas as pl
from jax.experimental.pallas import tpu as pltpu
from jax.sharding import PartitionSpec as P

HEADS = 16
BF = jnp.bfloat16
F32 = jnp.float32
VMEM_BYTES = 60 * 1024 * 1024
SMALL_BYTES = 28 * 1024 * 1024
WEIGHT_BYTES = 54 * 1024 * 1024


def nn(a, b):
    return lax.dot_general(a, b, (((1,), (0,)), ((), ())), preferred_element_type=F32)


def nt(a, b):
    return lax.dot_general(a, b, (((1,), (1,)), ((), ())), preferred_element_type=F32)


def tn(a, b):
    return lax.dot_general(a, b, (((0,), (0,)), ((), ())), preferred_element_type=F32)


def one_hot(index_ref, width):
    rows = index_ref.shape[0]
    columns = lax.broadcasted_iota(jnp.int32, (rows, width), 1)
    return jnp.where(columns == index_ref[...], 1.0, 0.0).astype(BF)


def pack_kernel(tok_ref, cot_ref, index_ref, *refs):
    both = refs[-1]
    rows = tok_ref.shape[0]
    both[:rows] = tok_ref[...]
    both[rows:] = cot_ref[...]
    take = index_ref.shape[0] // (len(refs) - 1)
    for c, out in enumerate(refs[:-1]):
        columns = lax.broadcasted_iota(jnp.int32, (take, 2 * rows), 1)
        picked = jnp.where(columns == index_ref[c * take : (c + 1) * take], 1.0, 0.0).astype(BF)
        out[...] = nn(picked, both[...]).astype(BF)


def unpack_kernel(chunks, *refs):
    backs, index_ref, out_tok, out_cot, both = refs[:chunks], refs[chunks], refs[-3], refs[-2], refs[-1]
    take = backs[0].shape[0]
    for c, back in enumerate(backs):
        both[c * take : (c + 1) * take] = back[...]
    rows = out_tok.shape[0]
    for w, out in enumerate((out_tok, out_cot)):
        columns = lax.broadcasted_iota(jnp.int32, (rows, chunks * take), 1)
        picked = jnp.where(columns == index_ref[w * rows : (w + 1) * rows], 1.0, 0.0).astype(BF)
        out[...] = nn(picked, both[...]).astype(BF)


def face_kernel(scal_ref, face_ref, fcot_ref, gain_ref, normed_ref, early_ref):
    hidden = face_ref[...].astype(F32)
    inverse = lax.rsqrt(jnp.mean(hidden * hidden, axis=-1, keepdims=True) + 1e-06)
    normed = (hidden * inverse * gain_ref[...]).astype(BF)
    normed_ref[...] = normed
    early_ref[...] = jnp.where(scal_ref[0] == 0, fcot_ref[...], normed)


def flips(line_ref, rotation_ref, base, lines):
    line = line_ref[:, 2:3]
    flip = jnp.zeros_like(line)
    for l in range(lines):
        turned = (rotation_ref[base + l] >= 2).astype(jnp.int32)
        flip = jnp.where(line == l, turned, flip)
    return jnp.where(flip != 0, line_ref[:, 1:2], line_ref[:, 0:1])


def turn_pair(rotation_ref, at):
    turn = rotation_ref[at]
    cosine = (turn == 0).astype(F32) - (turn == 2).astype(F32)
    sine = (turn == 1).astype(F32) - (turn == 3).astype(F32)
    return cosine, sine


def one_hot_rows(index, width):
    columns = lax.broadcasted_iota(jnp.int32, (index.shape[0], width), 1)
    return jnp.where(columns == index, 1.0, 0.0).astype(BF)


def edge_kernel(
    lines,
    scal_ref,
    rotation_ref,
    counts_ref,
    arrived_ref,
    index_ref,
    gain_ref,
    z_ref,
    g_ref,
    normed_ref,
    early_ref,
):
    half = z_ref.shape[1] // 2
    edges = z_ref.shape[0]
    edge_len = edges // lines
    base = scal_ref[0]
    index = flips(index_ref, rotation_ref, base, lines)
    picked = one_hot_rows(index, arrived_ref.shape[0])
    first = nn(picked, arrived_ref[:, :half])
    second = nn(picked, arrived_ref[:, half:])
    for l in range(lines):
        cosine, sine = turn_pair(rotation_ref, base + l)

        def turned(at):
            u, v = first[at : at + edge_len], second[at : at + edge_len]
            return jnp.concatenate([cosine * u - sine * v, sine * u + cosine * v], axis=1)

        rows = slice(l * edge_len, (l + 1) * edge_len)
        hidden = turned(l * edge_len)
        g = turned(edges + l * edge_len).astype(BF)
        z_ref[rows] = hidden.astype(BF)
        g_ref[rows] = g
        inverse = lax.rsqrt(jnp.mean(hidden * hidden, axis=-1, keepdims=True) + 1e-06)
        normed = (hidden * inverse * gain_ref[...]).astype(BF)
        normed_ref[rows] = normed
        early_ref[rows] = jnp.where(scal_ref[2] == 0, g, normed)


def layer_kernel(
    lines, first_chunk, drop, scal_ref, rotation_ref, counts_ref, face_ref, fcot_ref, *refs
):
    base = scal_ref[0]
    if first_chunk:
        arrived_ref, index_ref, normed_face_ref, gain_ref, wqkv_ref, wo_ref = refs[:6]
        refs = refs[6 + drop :]
        send_a, send_b = refs[4], refs[6]
        g_edge_ref, normed_edge_ref = refs[8:10]
        z_edge_ref = refs[-1]
        refs = (*refs[:8], *refs[10:-1])
        late_rows = refs[3].shape[0]
        edge_rows = z_edge_ref.shape[0]
        edge_kernel(
            lines,
            scal_ref,
            rotation_ref,
            counts_ref,
            arrived_ref,
            index_ref,
            gain_ref,
            z_edge_ref,
            g_edge_ref,
            normed_edge_ref,
            send_b.at[pl.ds(late_rows, edge_rows)],
        )
        send_a[late_rows:] = normed_edge_ref[...]
    else:
        z_edge_ref, g_edge_ref, normed_edge_ref = refs[:3]
        normed_face_ref, gain_ref, wqkv_ref, wo_ref, back_index_ref, before_ref = refs[3:9]
        refs = refs[9 + drop :]
    (
        face_out,
        face_grad,
        back_ref,
        keep_a,
        send_a,
        keep_b,
        send_b,
        gain_part,
        z_s,
        g_s,
        norm_s,
        qkv_s,
        dm_s,
        mix_s,
        stk_s,
        dn_s,
        y_s,
        edge_s,
    ) = refs
    width = z_s.shape[1]
    half = width // 2
    face_len = face_ref.shape[2]
    edges = z_edge_ref.shape[0]
    edge_len = edges // lines
    length = face_len + edge_len
    faces = lines * face_len
    head_dim = width // HEADS
    scale = head_dim ** (-0.5)
    gain = gain_ref[...]

    for l in range(lines):
        z_s[l * face_len : (l + 1) * face_len] = face_ref[0, l]
        g_s[l * face_len : (l + 1) * face_len] = fcot_ref[0, l]
    z_s[faces:] = z_edge_ref[...]
    g_s[faces:] = g_edge_ref[...]
    norm_s[:faces] = normed_face_ref[...]
    norm_s[faces:] = normed_edge_ref[...]

    tile = 512

    @pl.loop(0, 3 * width // tile)
    def _(j):
        cols = pl.ds(pl.multiple_of(j * tile, tile), tile)
        qkv_s[:, cols] = nn(norm_s[...], wqkv_ref[:, cols]).astype(BF)

    @pl.loop(0, width // tile)
    def _(j):
        cols = pl.ds(pl.multiple_of(j * tile, tile), tile)
        dm_s[:, cols] = nt(g_s[...], wo_ref[cols, :]).astype(BF)

    pair = 2 * head_dim
    low = lax.broadcasted_iota(jnp.int32, (length, pair), 1) < head_dim
    key_row = lax.broadcasted_iota(jnp.int32, (length, length), 0)

    def split(x):
        zero = jnp.zeros_like(x)
        return jnp.concatenate([jnp.where(low, x, zero), jnp.where(low, zero, x)], axis=0)

    @pl.loop(0, lines)
    def _(l):
        top = pl.ds(pl.multiple_of(l * face_len, face_len), face_len)
        bottom = pl.ds(pl.multiple_of(faces + l * edge_len, edge_len), edge_len)
        live = key_row < counts_ref[base + l] + face_len

        def load(ref, at):
            return jnp.concatenate([ref[top, at : at + pair], ref[bottom, at : at + pair]], axis=0)

        def store(ref, at, value):
            ref[top, at : at + pair] = value[:face_len].astype(BF)
            ref[bottom, at : at + pair] = value[face_len:].astype(BF)

        for p in range(HEADS // 2):
            at = p * pair
            q = load(qkv_s, at)
            k2 = split(load(qkv_s, width + at))
            v2 = split(load(qkv_s, 2 * width + at))
            dm = load(dm_s, at)
            scores = nt(k2, q) * scale
            d_probs = nt(v2, dm)
            probs_b, d_scores = [], []
            for h in range(2):
                part = slice(h * length, (h + 1) * length)
                s = jnp.where(live, scores[part], -1e30)
                e = jnp.exp(s - jnp.max(s, axis=0, keepdims=True))
                probs = e * (1.0 / jnp.sum(e, axis=0, keepdims=True))
                d = d_probs[part]
                inner = jnp.sum(probs * d, axis=0, keepdims=True)
                probs_b.append(probs.astype(BF))
                d_scores.append((probs * (d - inner) * scale).astype(BF))
            pb = jnp.concatenate(probs_b, axis=0)
            ds = jnp.concatenate(d_scores, axis=0)
            store(mix_s, at, tn(pb, v2))
            dv = nn(pb, dm)
            store(stk_s, 2 * width + at, jnp.where(low, dv[:length], dv[length:]))
            store(stk_s, at, tn(ds, k2))
            dk = nn(ds, q)
            store(stk_s, width + at, jnp.where(low, dk[:length], dk[length:]))

    @pl.loop(0, width // tile)
    def _(j):
        cols = pl.ds(pl.multiple_of(j * tile, tile), tile)
        y_s[:, cols] = (nn(mix_s[...], wo_ref[:, cols]) + z_s[:, cols].astype(F32)).astype(BF)
        dn_s[:, cols] = nt(stk_s[...], wqkv_ref[cols, :])

    gain_sum = jnp.zeros((1, width), F32)
    off = 0 if first_chunk else 2 * edges
    for i in range(2 * lines):
        size = face_len if i < lines else edge_len
        start = i * face_len if i < lines else faces + (i - lines) * edge_len
        at = slice(start, start + size)
        hidden = z_s[at].astype(F32)
        inverse = lax.rsqrt(jnp.mean(hidden * hidden, axis=-1, keepdims=True) + 1e-06)
        d_normed = dn_s[at]
        gain_sum = gain_sum + jnp.sum(d_normed * hidden * inverse, axis=0, keepdims=True)
        scaled = d_normed * gain
        mean = jnp.mean(scaled * hidden, axis=-1, keepdims=True)
        dz = inverse * scaled - hidden * (inverse * inverse * inverse * mean)
        dz = (g_s[at].astype(F32) + dz).astype(BF)
        if i < lines:
            face_out[0, i] = y_s[at]
            face_grad[0, i] = dz
        else:
            at = off + edges + start - faces
            edge_s[at : at + size] = dz
    edge_s[off : off + edges] = y_s[faces:]
    lanes = gain_part.shape[1]
    for i in range(width // lanes):
        gain_part[i : i + 1] = gain_sum[:, i * lanes : (i + 1) * lanes]
    for i in range(2 * lines):
        cosine, sine = turn_pair(rotation_ref, base + i % lines)
        rows = slice(off + i * edge_len, off + (i + 1) * edge_len)
        u, v = edge_s[rows, :half].astype(F32), edge_s[rows, half:].astype(F32)
        edge_s[rows, :half] = (cosine * u + sine * v).astype(BF)
        edge_s[rows, half:] = (cosine * v - sine * u).astype(BF)
    if first_chunk:
        back_ref[...] = edge_s[...]
    else:
        edge_s[:off] = before_ref[...]
        picked = one_hot_rows(
            flips(back_index_ref, rotation_ref, base - lines, 2 * lines), 4 * edges
        )
        back_ref[...] = nn(picked, edge_s[...]).astype(BF)

    total_rows = z_s.shape[0]
    x_bit = scal_ref[1]
    y_bit = scal_ref[2]

    @pl.when(x_bit == 0)
    def _():
        keep_a[...] = stk_s[:, :width]
        send_a[:total_rows] = stk_s[:, width : 2 * width]

    @pl.when(x_bit != 0)
    def _():
        send_a[:total_rows] = stk_s[:, :width]
        keep_a[...] = stk_s[:, width : 2 * width]

    @pl.when(y_bit == 0)
    def _():
        keep_b[...] = stk_s[:, 2 * width :]
        send_b[:total_rows] = mix_s[...]

    @pl.when(y_bit != 0)
    def _():
        send_b[:total_rows] = stk_s[:, 2 * width :]
        keep_b[...] = mix_s[...]


def weight_kernel(runs, parities, blocks, count, adds, gains, halved, scal_ref, *refs):
    operands = refs[:count]
    add_refs = refs[count : count + adds]
    gain_refs = refs[count + adds : count + adds + gains]
    outs = refs[count + adds + gains :]
    pieces = max(1, len(outs) // 2)
    width = operands[-1].shape[1]
    part = width // 2
    size = part // blocks
    tile = outs[0].shape[1]
    rows = len(parities) * part

    def pick(src):
        kept = []
        for own in parities:
            first = scal_ref[0] == (0 if own else 1)
            for b in range(blocks):
                left = src[:, 2 * b * size : (2 * b + 1) * size]
                right = src[:, (2 * b + 1) * size : (2 * b + 2) * size]
                kept.append(jnp.where(first, left, right))
        return jnp.concatenate(kept, axis=1)

    def run(swapped):
        early, late = [], []
        for faces, edges, chunk, late_at in runs:
            edge = operands[edges[swapped]]
            front = operands[late_at].shape[0] - edge.shape[0]
            early += [operands[faces[swapped]][chunk * front : (chunk + 1) * front], edge[...]]
            late.append(operands[late_at][...])
        early, late = jnp.concatenate(early, axis=0), jnp.concatenate(late, axis=0)
        lhs, rhs = (late, early) if swapped else (early, late)
        lhs = pick(lhs)
        if not halved:
            total = tn(lhs, rhs)
            for ref in add_refs:
                total = total + ref[:rows]
            for n, out in enumerate(outs):
                out[:part] = total[n * part : (n + 1) * part]
            return
        for half in range(2):
            mine = (scal_ref[2] if half else 1 - scal_ref[2]) == 0
            cols = jnp.where(mine, rhs[:, :part], rhs[:, part:])
            total = tn(lhs, cols)
            for ref in add_refs:
                total = total + jnp.where(mine, ref[:rows, :part], ref[:rows, part:])
            for n in range(pieces):
                outs[half * pieces + n][:rows] = total[:, n * tile : (n + 1) * tile]

    @pl.when(scal_ref[1] == 0)
    def _():
        run(0)

    @pl.when(scal_ref[1] != 0)
    def _():
        run(1)

    if gains:
        total = gain_refs[0][...]
        for ref in gain_refs[1:]:
            total = total + ref[...]
        lanes = total.shape[1]
        if halved:
            total = total + add_refs[-1][rows:, :lanes]
        for out in outs:
            if out.shape[0] > rows:
                for n in range(tile // lanes):
                    out[rows:, n * lanes : (n + 1) * lanes] = total


def weight_part(
    scal, runs, parities, blocks, operands, adds, pieces, halved, gains, deps, held=()
):
    pieces_of = [o if isinstance(o, tuple) else (o, o.shape[0], 0) for o in operands]
    operands = [o for o, _, _ in pieces_of]
    width = operands[-1].shape[1]
    part = width // 2
    rows = len(parities) * part
    depth = len(runs) * pieces_of[runs[0][3]][1]
    extra = gains[0].shape[0] if gains else 0
    used = len(operands) + len(adds) + len(gains)

    def kernel(scal_ref, *refs):
        refs = refs[:used] + refs[used + len(deps) :]
        weight_kernel(
            runs, parities, blocks, len(operands), len(adds), len(gains), halved, scal_ref, *refs
        )

    def spec(shape):
        return pl.BlockSpec(shape, lambda i, s: (0, 0))

    near = pl.BlockSpec(memory_space=pltpu.VMEM)
    if halved:
        tile = part // pieces
        shapes = [
            (rows + (extra if n % pieces == 0 else 0), tile) for n in range(2 * pieces)
        ]
    else:
        shapes = [(part + extra, width)] * len(parities)
    return pl.pallas_call(
        kernel,
        grid_spec=pltpu.PrefetchScalarGridSpec(
            num_scalar_prefetch=1,
            grid=(1,),
            in_specs=[
                near
                if n in held
                else pl.BlockSpec((size, width), lambda i, s, at=at: (at, 0))
                for n, (_, size, at) in enumerate(pieces_of)
            ]
            + [near] * len(adds)
            + [spec(g.shape) for g in gains]
            + [pl.BlockSpec(memory_space=pl.ANY)] * len(deps),
            out_specs=[near] * len(shapes),
        ),
        out_shape=[jax.ShapeDtypeStruct(s, F32) for s in shapes],
        compiler_params=pltpu.CompilerParams(vmem_limit_bytes=SMALL_BYTES if len(runs) == 1 else WEIGHT_BYTES),
        cost_estimate=pl.CostEstimate(
            flops=1 << 33 if len(runs) > 1 else 1024, bytes_accessed=1024, transcendentals=0
        ),
        name="weight_part",
    )(scal, *operands, *adds, *gains, *deps)


def block_kernel(blocks, count, scal_ref, *refs):
    groups = (refs[:count], refs[count : 2 * count])
    outs = refs[2 * count :]
    columns = groups[0][0].shape[1]
    size = groups[1][0].shape[0] // blocks
    whole = blocks * size
    for o, out in enumerate(outs):
        at = pl.ds(pl.multiple_of((scal_ref[0] ^ o) * size, size), size)
        for n, parts in enumerate(groups):
            total = parts[0][at]
            for p in parts[1:]:
                total = total + p[at]
            out[:size, n * columns : (n + 1) * columns] = total
        if out.shape[0] > size:
            total = groups[0][0][whole:]
            for p in groups[0][1:]:
                total = total + p[whole:]
            out[size:, :columns] = total
            out[size:, columns:] = total


def sum_kernel(factor, scal_ref, *refs):
    total = refs[0][...]
    for ref in refs[1:-1]:
        total = total + ref[...]
    refs[-1][...] = total * factor


def place_kernel(pieces, devices, scal_ref, *refs):
    qkv_ref, out_ref = refs[-2], refs[-1]
    width = out_ref.shape[1]
    bits = devices.bit_length() - 1
    for n in range(pieces):
        for o in range(devices):
            src = refs[n * devices + o]
            part = src.shape[1] // 2
            size = out_ref.shape[0]
            device = scal_ref[0] ^ o
            for group in range(2):
                value = (slice(0, size), slice(group * part, (group + 1) * part))
                rest = [b for b in range(bits) if b != group]
                at = ((device >> rest[0]) & 1) * (width // 2) + n * (width // 2 // pieces)
                unit = width // 2 // pieces
                for b in rest[1:]:
                    unit = unit // 2
                    at = at + ((device >> b) & 1) * unit
                which = (device >> group) & 1
                if group == 0:
                    at = pl.multiple_of(at + which * width, part)
                    qkv_ref[:, pl.ds(at, part)] = src[value]
                else:

                    @pl.when(which == 0)
                    def _(src=src, value=value, at=at, part=part):
                        cols = pl.ds(pl.multiple_of(at + 2 * width, part), part)
                        qkv_ref[:, cols] = src[value]

                    @pl.when(which != 0)
                    def _(src=src, value=value, at=at, part=part):
                        out_ref[:, pl.ds(pl.multiple_of(at, part), part)] = src[value]


def exchange(x, axis, bits, size):
    return lax.ppermute(x, axis, [(i, i ^ bits) for i in range(size)])


def whole_call(kernel, name, scal, out_shape, operands, deps=(), scratch=(), flops=0, limit=SMALL_BYTES, near=(False, False)):
    scal = scal if isinstance(scal, tuple) else (scal,)

    def body(*refs):
        used = len(scal) + len(operands)
        kernel(*refs[:used], *refs[used + len(deps) :])

    def spec(shape):
        return pl.BlockSpec(shape, lambda i, *s: (0,) * len(shape))

    vmem = pl.BlockSpec(memory_space=pltpu.VMEM)
    moved = sum(int(np.prod(o.shape)) * o.dtype.itemsize for o in [*operands, *out_shape])
    return pl.pallas_call(
        body,
        grid_spec=pltpu.PrefetchScalarGridSpec(
            num_scalar_prefetch=len(scal),
            grid=(1,),
            in_specs=[vmem if near[0] else spec(o.shape) for o in operands]
            + [pl.BlockSpec(memory_space=pl.ANY)] * len(deps),
            out_specs=[vmem if near[1] else spec(o.shape) for o in out_shape],
            scratch_shapes=list(scratch),
        ),
        out_shape=out_shape,
        compiler_params=pltpu.CompilerParams(vmem_limit_bytes=limit),
        cost_estimate=pl.CostEstimate(flops=1024, bytes_accessed=1024, transcendentals=0),
        name=name,
    )(*scal, *operands, *deps)


def local(
    face_tokens,
    edge_tokens,
    face_cotangent,
    edge_cotangent,
    rotation,
    counts,
    norm_gain,
    qkv_weight,
    out_weight,
):
    T = lax.axis_size("tile")
    D = lax.axis_size("dp")
    me_t = lax.axis_index("tile")
    me_d = lax.axis_index("dp")
    LD, FL, width = face_tokens.shape[1:]
    K = edge_tokens.shape[1]
    EL = K * T
    NLG = edge_tokens.shape[2]
    length = FL + EL
    chunks = 2
    lines = LD // chunks
    RB = lines * K
    packed = T * 2 * RB
    factor = float(D * T * LD * length) ** (-0.5)
    x_bit = (me_d % 2).astype(jnp.int32)
    y_bit = ((me_d // 2) % 2).astype(jnp.int32)
    gain = norm_gain.reshape(1, width)

    def struct(*shape, dtype=BF):
        return jax.ShapeDtypeStruct(shape, dtype)

    order = np.zeros((chunks, T, 2, lines, K), np.int32)
    for c in range(chunks):
        for w in range(2):
            t, l, k = np.meshgrid(np.arange(T), np.arange(lines), np.arange(K), indexing="ij")
            order[c, :, w] = w * K * NLG + k * NLG + t * LD + c * lines + l
    sent = whole_call(
        lambda s, *refs: pack_kernel(*refs),
        "pack",
        y_bit.reshape(1),
        [struct(packed, width)] * chunks,
        [
            edge_tokens.reshape(K * NLG, width),
            edge_cotangent.reshape(K * NLG, width),
            jnp.asarray(order.reshape(-1, 1)),
        ],
        scratch=[pltpu.VMEM((2 * K * NLG, width), BF)],
        limit=VMEM_BYTES,
    )
    arrived = [lax.all_to_all(s, "tile", split_axis=0, concat_axis=0, tiled=True) for s in sent]

    face_rows = face_tokens.reshape(LD * FL, width)
    face_cots = face_cotangent.reshape(LD * FL, width)
    face_normed, face_early = whole_call(
        face_kernel,
        "face_norm",
        y_bit.reshape(1),
        [struct(LD * FL, width)] * 2,
        [face_rows, face_cots, gain],
        limit=VMEM_BYTES,
    )
    got_face_a = exchange(face_normed, "dp", 1, D)
    got_face_b = exchange(face_early, "dp", 2, D)

    edges = lines * EL
    l, p = np.meshgrid(np.arange(lines), np.arange(EL), indexing="ij")
    table = []
    for pos in (p, EL - 1 - p):
        row = (pos // K) * (2 * RB) + l * K + pos % K
        table.append(np.stack([row, row + RB]))
    table.append(np.stack([l, l]))
    index = jnp.asarray(np.stack(table, axis=-1).reshape(-1, 3).astype(np.int32))
    t, c, w, l, k = np.meshgrid(
        np.arange(T),
        np.arange(chunks),
        np.arange(2),
        np.arange(lines),
        np.arange(K),
        indexing="ij",
    )
    at = 2 * c * edges + w * edges + l * EL
    pos = t * K + k
    table = [at + pos, at + EL - 1 - pos, c * lines + l]
    back_index = jnp.asarray(np.stack(table, axis=-1).reshape(-1, 3).astype(np.int32))
    edge_parts, results, got_edges, got_late = [], [], [], []
    faces = None
    for c in range(chunks):
        base = (me_t * LD + c * lines).astype(jnp.int32)
        scal = (jnp.stack([base, x_bit, y_bit]), rotation, counts)
        rows_all = lines * length
        row_shape = (rows_all, width)
        face_spec = pl.BlockSpec((1, lines, FL, width), lambda i, *s, c=c: (0, c, 0, 0))
        normed_spec = pl.BlockSpec((lines * FL, width), lambda i, *s, c=c: (c, 0))

        def full(shape):
            return pl.BlockSpec(shape, lambda i, *s: (0,) * len(shape))

        if c == 0:
            operands = [face_tokens, face_cotangent, arrived[c], index]
            operands += [face_normed, gain, qkv_weight, out_weight]
            tail = []
        else:
            z_edge, g_edge, normed_edge, early_edge = whole_call(
                functools.partial(edge_kernel, lines),
                "edge_norm",
                scal,
                [struct(edges, width)] * 4,
                [arrived[c], index, gain],
                deps=[results[0][5]],
                limit=VMEM_BYTES,
            )
            operands = [face_tokens, face_cotangent, z_edge, g_edge, normed_edge]
            operands += [face_normed, gain, qkv_weight, out_weight, back_index, results[0][0]]
            tail = [*faces, got_face_a, got_face_b]
        in_specs = [
            face_spec if n < 2 else normed_spec if o is face_normed else full(o.shape)
            for n, o in enumerate(operands)
        ]
        in_specs += [pl.BlockSpec(memory_space=pl.ANY)] * len(tail)
        aliases = {} if c == 0 else {3 + len(operands): 0, 4 + len(operands): 1}
        operands += tail
        back_rows = 2 * edges if c == 0 else packed * chunks
        edge_outs = [(edges, width)] * 2 if c == 0 else []
        send_shape = (rows_all + (edges if c == 0 else 0), width)
        outs = pl.pallas_call(
            functools.partial(layer_kernel, lines, c == 0, len(tail)),
            grid_spec=pltpu.PrefetchScalarGridSpec(
                num_scalar_prefetch=3,
                grid=(1,),
                in_specs=in_specs,
                out_specs=[face_spec, face_spec, full((back_rows, width))]
                + [full(row_shape), full(send_shape)] * 2
                + [full((8, width // 8))]
                + [full(e) for e in edge_outs],
                scratch_shapes=[
                    pltpu.VMEM(row_shape, BF),
                    pltpu.VMEM(row_shape, BF),
                    pltpu.VMEM(row_shape, BF),
                    pltpu.VMEM((rows_all, 3 * width), BF),
                    pltpu.VMEM(row_shape, BF),
                    pltpu.VMEM(row_shape, BF),
                    pltpu.VMEM((rows_all, 3 * width), BF),
                    pltpu.VMEM(row_shape, F32),
                    pltpu.VMEM(row_shape, BF),
                    pltpu.VMEM((2 * edges * (c + 1), width), BF),
                ]
                + ([pltpu.VMEM((edges, width), BF)] if c == 0 else []),
            ),
            out_shape=[struct(*face_tokens.shape)] * 2
            + [struct(back_rows, width)]
            + [struct(*row_shape), struct(*send_shape)] * 2
            + [struct(8, width // 8, dtype=F32)]
            + [struct(*e) for e in edge_outs],
            input_output_aliases=aliases,
            compiler_params=pltpu.CompilerParams(vmem_limit_bytes=VMEM_BYTES),
            cost_estimate=pl.CostEstimate(flops=1 << 35, bytes_accessed=1 << 20, transcendentals=0),
            name="layer",
        )(*scal, *operands)
        faces = outs[:2]
        results.append(outs[2:])
        late_a, late_b = exchange(outs[4], "dp", 1, D), exchange(outs[6], "dp", 2, D)
        if c == 0:
            g_edge, normed_edge = outs[8:]
            edges_a, edges_b = (late_a, edges, rows_all // edges), (late_b, edges, rows_all // edges)
            late_a, late_b = (late_a, rows_all, 0), (late_b, rows_all, 0)
        else:
            edges_a = exchange(normed_edge, "dp", 1, D)
            edges_b = exchange(early_edge, "dp", 2, D)
        edge_parts.append((normed_edge, g_edge))
        got_edges.append((edges_a, edges_b))
        got_late.append((late_a, late_b))
    returned = lax.all_to_all(results[1][0], "tile", split_axis=0, concat_axis=0, tiled=True)

    blocks = T // 2
    chip = (me_t // 2).astype(jnp.int32)
    core = (me_t % 2).astype(jnp.int32)
    pieces = 2
    size = width // T
    bits = D.bit_length() - 1
    groups = []
    for group in range(2):
        first = [b for b in range(bits) if b != group][0]
        swap = y_bit if group else jnp.zeros_like(y_bit)
        scal = jnp.stack([core, swap, ((me_d >> first) & 1).astype(jnp.int32)])
        late = [r[1 + 2 * group] for r in results]
        got_face = (got_face_a, got_face_b)[group]
        normed_e, g_e = [e[0] for e in edge_parts], [e[1] for e in edge_parts]
        got_e = [e[group] for e in got_edges]
        got_l = [e[group] for e in got_late]
        operands = [face_normed, face_cots, *normed_e, *g_e, got_face, got_e[0], late[0], late[1], got_l[0]]
        runs = [((0, 1), (2, 4), 0, 8), ((0, 1), (3, 5), 1, 9), ((6, 6), (7, 7), 0, 10)]
        start = weight_part(
            scal, runs, (False, True), blocks, operands, [], pieces, False, [],
            [*got_edges[1], got_late[0][0][0], got_late[0][1][0]],
        )
        groups.append((scal, [got_face, got_e[1], got_l[1]], start, first))
    theirs = []
    runs = [((0, 0), (1, 1), 1, 2)]
    gains = [[r[5] for r in results], []]
    starts = [g[2] for g in groups]
    for group, (scal, operands, start, first) in enumerate(groups):
        send = weight_part(
            scal, runs, (False,), blocks, operands, [start[0]], pieces, False, gains[group],
            [] if group else [starts[1][0]],
            held=(2,),
        )[0]
        theirs.append(exchange(send, "tile", 1, T))
    halves = []
    for group, (scal, operands, start, first) in enumerate(groups):
        outs = weight_part(
            scal, runs, (True,), blocks, operands, [start[1], theirs[group]], pieces, True,
            gains[group], [], held=(2,),
        )
        parts = []
        for n in range(pieces):
            both = [outs[pieces + n], exchange(outs[n], "dp", 1 << first, D)]
            for b in range(bits):
                if b in (group, first):
                    continue
                columns = both[0].shape[1] // 2
                mine = (me_d >> b) & 1
                keep = [lax.dynamic_slice_in_dim(p, mine * columns, columns, 1) for p in both]
                give = [lax.dynamic_slice_in_dim(p, (1 - mine) * columns, columns, 1) for p in both]
                both = [sum(keep), exchange(sum(give), "dp", 1 << b, D)]
            parts.append(both)
        halves.append(parts)
    placed = []
    for n in range(pieces):
        parts = [*halves[0][n], *halves[1][n]]
        columns = 2 * parts[0].shape[1]
        outs = whole_call(
            functools.partial(block_kernel, blocks, 2),
            "row_blocks",
            chip.reshape(1),
            [struct(size + (8 if n == 0 else 0), columns, dtype=F32)] * blocks,
            parts,
            near=(True, True),
            deps=[returned] if n == 0 else [],
        )
        got = [exchange(outs[o], "tile", 2 * o, T) for o in range(1, blocks)]
        (mine,) = whole_call(
            functools.partial(sum_kernel, factor),
            "block_sum",
            chip.reshape(1),
            [struct(*outs[0].shape, dtype=F32)],
            [outs[0], *got],
            near=(True, True),
        )
        placed += [mine] + [exchange(mine, "dp", o, D) for o in range(1, D)]

    back_order = np.zeros((2, K, NLG), np.int32)
    for w in range(2):
        k, t, c, l = np.meshgrid(
            np.arange(K), np.arange(T), np.arange(chunks), np.arange(lines), indexing="ij"
        )
        back_order[w] = ((t * chunks + c) * 2 * RB + w * RB + l * K + k).reshape(K, NLG)
    edge_output, edge_grad = whole_call(
        lambda s, *refs: unpack_kernel(1, *refs),
        "unpack",
        chip.reshape(1),
        [struct(K * NLG, width)] * 2,
        [returned, jnp.asarray(back_order.reshape(-1, 1))],
        scratch=[pltpu.VMEM((chunks * packed, width), BF)],
    )
    qkv_grad, out_grad = whole_call(
        functools.partial(place_kernel, pieces, D),
        "place",
        me_d.astype(jnp.int32).reshape(1),
        [struct(size, 3 * width, dtype=F32), struct(size, width, dtype=F32)],
        placed,
        near=(True, False),
    )
    gain_sum = (placed[0] + placed[1])[size:, : width // 8].reshape(width)
    gain_grad = lax.dynamic_slice_in_dim(gain_sum, me_t * size, size)
    shape = edge_tokens.shape
    return (
        faces[0],
        edge_output.reshape(shape),
        faces[1],
        edge_grad.reshape(shape),
        qkv_grad,
        out_grad,
        gain_grad,
    )


def solution(mesh):
    return jax.shard_map(
        local,
        mesh=mesh,
        in_specs=(
            P("dp", "tile", None, None),
            P("dp", "tile", None, None),
            P("dp", "tile", None, None),
            P("dp", "tile", None, None),
            P(),
            P(),
            P(),
            P(),
            P(),
        ),
        out_specs=(
            P("dp", "tile", None, None),
            P("dp", "tile", None, None),
            P("dp", "tile", None, None),
            P("dp", "tile", None, None),
            P("tile", None),
            P("tile", None),
            P("tile"),
        ),
        check_vma=False,
    )
```

```python
import functools

import jax
import jax.numpy as jnp
import numpy as np
from jax import lax
from jax.experimental import pallas as pl
from jax.experimental.pallas import tpu as pltpu
from jax.sharding import PartitionSpec as P

HEADS = 16
BF = jnp.bfloat16
F32 = jnp.float32
VMEM_BYTES = 60 * 1024 * 1024
SMALL_BYTES = 28 * 1024 * 1024
WEIGHT_BYTES = 54 * 1024 * 1024


def nn(a, b):
    return lax.dot_general(a, b, (((1,), (0,)), ((), ())), preferred_element_type=F32)


def nt(a, b):
    return lax.dot_general(a, b, (((1,), (1,)), ((), ())), preferred_element_type=F32)


def tn(a, b):
    return lax.dot_general(a, b, (((0,), (0,)), ((), ())), preferred_element_type=F32)


def one_hot(index_ref, width):
    rows = index_ref.shape[0]
    columns = lax.broadcasted_iota(jnp.int32, (rows, width), 1)
    return jnp.where(columns == index_ref[...], 1.0, 0.0).astype(BF)


def pack_kernel(tok_ref, cot_ref, index_ref, *refs):
    both = refs[-1]
    rows = tok_ref.shape[0]
    both[:rows] = tok_ref[...]
    both[rows:] = cot_ref[...]
    take = index_ref.shape[0] // (len(refs) - 1)
    for c, out in enumerate(refs[:-1]):
        columns = lax.broadcasted_iota(jnp.int32, (take, 2 * rows), 1)
        picked = jnp.where(columns == index_ref[c * take : (c + 1) * take], 1.0, 0.0).astype(BF)
        out[...] = nn(picked, both[...]).astype(BF)


def unpack_kernel(chunks, *refs):
    backs, index_ref, out_tok, out_cot, both = refs[:chunks], refs[chunks], refs[-3], refs[-2], refs[-1]
    take = backs[0].shape[0]
    for c, back in enumerate(backs):
        both[c * take : (c + 1) * take] = back[...]
    rows = out_tok.shape[0]
    for w, out in enumerate((out_tok, out_cot)):
        columns = lax.broadcasted_iota(jnp.int32, (rows, chunks * take), 1)
        picked = jnp.where(columns == index_ref[w * rows : (w + 1) * rows], 1.0, 0.0).astype(BF)
        out[...] = nn(picked, both[...]).astype(BF)


def face_kernel(scal_ref, face_ref, fcot_ref, gain_ref, normed_ref, early_ref):
    hidden = face_ref[...].astype(F32)
    inverse = lax.rsqrt(jnp.mean(hidden * hidden, axis=-1, keepdims=True) + 1e-06)
    normed = (hidden * inverse * gain_ref[...]).astype(BF)
    normed_ref[...] = normed
    early_ref[...] = jnp.where(scal_ref[0] == 0, fcot_ref[...], normed)


def flips(line_ref, rotation_ref, base, lines):
    line = line_ref[:, 2:3]
    flip = jnp.zeros_like(line)
    for l in range(lines):
        turned = (rotation_ref[base + l] >= 2).astype(jnp.int32)
        flip = jnp.where(line == l, turned, flip)
    return jnp.where(flip != 0, line_ref[:, 1:2], line_ref[:, 0:1])


def turn_pair(rotation_ref, at):
    turn = rotation_ref[at]
    cosine = (turn == 0).astype(F32) - (turn == 2).astype(F32)
    sine = (turn == 1).astype(F32) - (turn == 3).astype(F32)
    return cosine, sine


def one_hot_rows(index, width):
    columns = lax.broadcasted_iota(jnp.int32, (index.shape[0], width), 1)
    return jnp.where(columns == index, 1.0, 0.0).astype(BF)


def edge_kernel(
    lines,
    scal_ref,
    rotation_ref,
    counts_ref,
    arrived_ref,
    index_ref,
    gain_ref,
    z_ref,
    g_ref,
    normed_ref,
    early_ref,
):
    half = z_ref.shape[1] // 2
    edges = z_ref.shape[0]
    edge_len = edges // lines
    base = scal_ref[0]
    index = flips(index_ref, rotation_ref, base, lines)
    picked = one_hot_rows(index, arrived_ref.shape[0])
    first = nn(picked, arrived_ref[:, :half])
    second = nn(picked, arrived_ref[:, half:])
    for l in range(lines):
        cosine, sine = turn_pair(rotation_ref, base + l)

        def turned(at):
            u, v = first[at : at + edge_len], second[at : at + edge_len]
            return jnp.concatenate([cosine * u - sine * v, sine * u + cosine * v], axis=1)

        rows = slice(l * edge_len, (l + 1) * edge_len)
        hidden = turned(l * edge_len)
        g = turned(edges + l * edge_len).astype(BF)
        z_ref[rows] = hidden.astype(BF)
        g_ref[rows] = g
        inverse = lax.rsqrt(jnp.mean(hidden * hidden, axis=-1, keepdims=True) + 1e-06)
        normed = (hidden * inverse * gain_ref[...]).astype(BF)
        normed_ref[rows] = normed
        early_ref[rows] = jnp.where(scal_ref[2] == 0, g, normed)


def layer_kernel(
    lines, first_chunk, drop, scal_ref, rotation_ref, counts_ref, face_ref, fcot_ref, *refs
):
    base = scal_ref[0]
    wqkv_hbm, wo_hbm = (refs[4:6]) if first_chunk else refs[5:7]
    wqkv_ref, wo_ref, in_sems, out_sems = refs[-4:]
    refs = refs[:-4]
    tile = 512

    def fetch(j):
        cols = pl.ds(j * tile if isinstance(j, int) else pl.multiple_of(j * tile, tile), tile)
        return pltpu.make_async_copy(wqkv_hbm.at[:, cols], wqkv_ref.at[:, cols], in_sems.at[j])

    tiles = wqkv_ref.shape[1] // tile
    fetch_out = pltpu.make_async_copy(wo_hbm, wo_ref, in_sems.at[tiles])
    for j in range(tiles):
        fetch(j).start()
    fetch_out.start()
    moves = []
    if first_chunk:
        arrived_ref, index_ref, normed_face_ref, gain_ref = refs[:4]
        refs = refs[6 + drop :]
        send_a, send_b = refs[4], refs[6]
        g_edge_ref, normed_edge_ref = refs[8:10]
        early_ref, z_edge_ref = refs[-2:]
        refs = (*refs[:8], *refs[10:-2])
        late_rows = refs[3].shape[0]
        edge_rows = z_edge_ref.shape[0]
        edge_kernel(
            lines,
            scal_ref,
            rotation_ref,
            counts_ref,
            arrived_ref,
            index_ref,
            gain_ref,
            z_edge_ref,
            g_edge_ref,
            normed_edge_ref,
            early_ref,
        )
        for n, (src, dst) in enumerate(((normed_edge_ref, send_a), (early_ref, send_b))):
            to = dst.at[pl.ds(late_rows, edge_rows)]
            moves.append(pltpu.make_async_copy(src, to, out_sems.at[4 + n]))
            moves[-1].start()
    else:
        z_edge_ref, g_edge_ref, normed_edge_ref = refs[:3]
        normed_face_ref, gain_ref = refs[3:5]
        back_index_ref, before_ref = refs[7:9]
        refs = refs[9 + drop :]
    (
        face_out,
        face_grad,
        back_ref,
        keep_a,
        send_a,
        keep_b,
        send_b,
        gain_part,
        z_s,
        g_s,
        norm_s,
        qkv_s,
        dm_s,
        mix_s,
        stk_s,
        dn_s,
        y_s,
        edge_s,
    ) = refs
    width = z_s.shape[1]
    half = width // 2
    face_len = face_ref.shape[2]
    edges = z_edge_ref.shape[0]
    edge_len = edges // lines
    length = face_len + edge_len
    faces = lines * face_len
    head_dim = width // HEADS
    scale = head_dim ** (-0.5)
    gain = gain_ref[...]

    for l in range(lines):
        z_s[l * face_len : (l + 1) * face_len] = face_ref[0, l]
        g_s[l * face_len : (l + 1) * face_len] = fcot_ref[0, l]
    z_s[faces:] = z_edge_ref[...]
    g_s[faces:] = g_edge_ref[...]
    norm_s[:faces] = normed_face_ref[...]
    norm_s[faces:] = normed_edge_ref[...]

    @pl.loop(0, tiles)
    def _(j):
        cols = pl.ds(pl.multiple_of(j * tile, tile), tile)
        fetch(j).wait()
        qkv_s[:, cols] = nn(norm_s[...], wqkv_ref[:, cols]).astype(BF)

    fetch_out.wait()

    @pl.loop(0, width // tile)
    def _(j):
        cols = pl.ds(pl.multiple_of(j * tile, tile), tile)
        dm_s[:, cols] = nt(g_s[...], wo_ref[cols, :]).astype(BF)

    pair = 2 * head_dim
    low = lax.broadcasted_iota(jnp.int32, (length, pair), 1) < head_dim
    key_row = lax.broadcasted_iota(jnp.int32, (length, length), 0)

    def split(x):
        zero = jnp.zeros_like(x)
        return jnp.concatenate([jnp.where(low, x, zero), jnp.where(low, zero, x)], axis=0)

    @pl.loop(0, lines)
    def _(l):
        top = pl.ds(pl.multiple_of(l * face_len, face_len), face_len)
        bottom = pl.ds(pl.multiple_of(faces + l * edge_len, edge_len), edge_len)
        live = key_row < counts_ref[base + l] + face_len

        def load(ref, at):
            return jnp.concatenate([ref[top, at : at + pair], ref[bottom, at : at + pair]], axis=0)

        def store(ref, at, value):
            ref[top, at : at + pair] = value[:face_len].astype(BF)
            ref[bottom, at : at + pair] = value[face_len:].astype(BF)

        for p in range(HEADS // 2):
            at = p * pair
            q = load(qkv_s, at)
            k2 = split(load(qkv_s, width + at))
            v2 = split(load(qkv_s, 2 * width + at))
            dm = load(dm_s, at)
            scores = nt(k2, q * jnp.asarray(scale, BF))
            d_probs = nt(v2, dm)
            probs_b, d_scores = [], []
            for h in range(2):
                part = slice(h * length, (h + 1) * length)
                s = jnp.where(live, scores[part], -1e30)
                e = jnp.exp(s - jnp.max(s, axis=0, keepdims=True))
                probs = e * (1.0 / jnp.sum(e, axis=0, keepdims=True))
                d = d_probs[part]
                inner = jnp.sum(probs * d, axis=0, keepdims=True)
                probs_b.append(probs.astype(BF))
                d_scores.append((probs * (d - inner)).astype(BF))
            pb = jnp.concatenate(probs_b, axis=0)
            ds = jnp.concatenate(d_scores, axis=0)
            store(mix_s, at, tn(pb, v2))
            dv = nn(pb, dm)
            store(stk_s, 2 * width + at, jnp.where(low, dv[:length], dv[length:]))
            store(stk_s, at, tn(ds, k2) * scale)
            dk = nn(ds, q)
            store(stk_s, width + at, jnp.where(low, dk[:length], dk[length:]) * scale)

    total_rows = z_s.shape[0]
    targets = (keep_a, send_a, keep_b, send_b)
    third = [stk_s.at[:, pl.ds(n * width, width)] for n in range(3)]
    sources = (third[0], third[1], third[2], mix_s)

    def ship(at, order):
        for n, src in enumerate(order):
            dst = targets[at + n].at[pl.ds(0, total_rows)]
            pltpu.make_async_copy(sources[src], dst, out_sems.at[at + n]).start()

    for at, bit in ((0, scal_ref[1]), (2, scal_ref[2])):

        @pl.when(bit == 0)
        def _(at=at):
            ship(at, (at, at + 1))

        @pl.when(bit != 0)
        def _(at=at):
            ship(at, (at + 1, at))

    @pl.loop(0, width // tile)
    def _(j):
        cols = pl.ds(pl.multiple_of(j * tile, tile), tile)
        y_s[:, cols] = (nn(mix_s[...], wo_ref[:, cols]) + z_s[:, cols].astype(F32)).astype(BF)
        dn_s[:, cols] = nt(stk_s[...], wqkv_ref[cols, :])

    gain_sum = jnp.zeros((1, width), F32)
    off = 0 if first_chunk else 2 * edges
    for i in range(2 * lines):
        size = face_len if i < lines else edge_len
        start = i * face_len if i < lines else faces + (i - lines) * edge_len
        at = slice(start, start + size)
        hidden = z_s[at].astype(F32)
        inverse = lax.rsqrt(jnp.mean(hidden * hidden, axis=-1, keepdims=True) + 1e-06)
        d_normed = dn_s[at]
        gain_sum = gain_sum + jnp.sum(d_normed * hidden * inverse, axis=0, keepdims=True)
        scaled = d_normed * gain
        mean = jnp.mean(scaled * hidden, axis=-1, keepdims=True)
        dz = inverse * scaled - hidden * (inverse * inverse * inverse * mean)
        dz = (g_s[at].astype(F32) + dz).astype(BF)
        if i < lines:
            face_out[0, i] = y_s[at]
            face_grad[0, i] = dz
        else:
            at = off + edges + start - faces
            edge_s[at : at + size] = dz
    edge_s[off : off + edges] = y_s[faces:]
    lanes = gain_part.shape[1]
    for i in range(width // lanes):
        gain_part[i : i + 1] = gain_sum[:, i * lanes : (i + 1) * lanes]
    for i in range(2 * lines):
        cosine, sine = turn_pair(rotation_ref, base + i % lines)
        rows = slice(off + i * edge_len, off + (i + 1) * edge_len)
        u, v = edge_s[rows, :half].astype(F32), edge_s[rows, half:].astype(F32)
        edge_s[rows, :half] = (cosine * u + sine * v).astype(BF)
        edge_s[rows, half:] = (cosine * v - sine * u).astype(BF)
    if first_chunk:
        back_ref[...] = edge_s[...]
    else:
        edge_s[:off] = before_ref[...]
        picked = one_hot_rows(
            flips(back_index_ref, rotation_ref, base - lines, 2 * lines), 4 * edges
        )
        back_ref[...] = nn(picked, edge_s[...]).astype(BF)

    for n, dst in enumerate(targets):
        pltpu.make_async_copy(sources[n], dst.at[pl.ds(0, total_rows)], out_sems.at[n]).wait()
    for move in moves:
        move.wait()


def weight_kernel(runs, parities, blocks, count, adds, gains, halved, scal_ref, *refs):
    operands = refs[:count]
    add_refs = refs[count : count + adds]
    gain_refs = refs[count + adds : count + adds + gains]
    outs = refs[count + adds + gains :]
    pieces = max(1, len(outs) // 2)
    width = operands[-1].shape[1]
    part = width // 2
    size = part // blocks
    tile = outs[0].shape[1]
    rows = len(parities) * part

    def pick(src):
        kept = []
        for own in parities:
            first = scal_ref[0] == (0 if own else 1)
            for b in range(blocks):
                left = src[:, 2 * b * size : (2 * b + 1) * size]
                right = src[:, (2 * b + 1) * size : (2 * b + 2) * size]
                kept.append(jnp.where(first, left, right))
        return jnp.concatenate(kept, axis=1)

    def run(swapped):
        early, late = [], []
        for faces, edges, chunk, late_at in runs:
            edge = operands[edges[swapped]]
            front = operands[late_at].shape[0] - edge.shape[0]
            early += [operands[faces[swapped]][chunk * front : (chunk + 1) * front], edge[...]]
            late.append(operands[late_at][...])
        early, late = jnp.concatenate(early, axis=0), jnp.concatenate(late, axis=0)
        lhs, rhs = (late, early) if swapped else (early, late)
        lhs = pick(lhs)
        if not halved:
            total = tn(lhs, rhs)
            for ref in add_refs:
                total = total + ref[:rows]
            for n, out in enumerate(outs):
                out[:part] = total[n * part : (n + 1) * part]
            return
        for half in range(2):
            mine = (scal_ref[2] if half else 1 - scal_ref[2]) == 0
            cols = jnp.where(mine, rhs[:, :part], rhs[:, part:])
            total = tn(lhs, cols)
            for ref in add_refs:
                total = total + jnp.where(mine, ref[:rows, :part], ref[:rows, part:])
            for n in range(pieces):
                outs[half * pieces + n][:rows] = total[:, n * tile : (n + 1) * tile]

    @pl.when(scal_ref[1] == 0)
    def _():
        run(0)

    @pl.when(scal_ref[1] != 0)
    def _():
        run(1)

    if gains:
        total = gain_refs[0][...]
        for ref in gain_refs[1:]:
            total = total + ref[...]
        lanes = total.shape[1]
        if halved:
            total = total + add_refs[-1][rows:, :lanes]
        for out in outs:
            if out.shape[0] > rows:
                for n in range(tile // lanes):
                    out[rows:, n * lanes : (n + 1) * lanes] = total


def weight_part(
    scal, runs, parities, blocks, operands, adds, pieces, halved, gains, deps, held=()
):
    pieces_of = [o if isinstance(o, tuple) else (o, o.shape[0], 0) for o in operands]
    operands = [o for o, _, _ in pieces_of]
    width = operands[-1].shape[1]
    part = width // 2
    rows = len(parities) * part
    depth = len(runs) * pieces_of[runs[0][3]][1]
    extra = gains[0].shape[0] if gains else 0
    used = len(operands) + len(adds) + len(gains)

    def kernel(scal_ref, *refs):
        refs = refs[:used] + refs[used + len(deps) :]
        weight_kernel(
            runs, parities, blocks, len(operands), len(adds), len(gains), halved, scal_ref, *refs
        )

    def spec(shape):
        return pl.BlockSpec(shape, lambda i, s: (0, 0))

    near = pl.BlockSpec(memory_space=pltpu.VMEM)
    if halved:
        tile = part // pieces
        shapes = [
            (rows + (extra if n % pieces == 0 else 0), tile) for n in range(2 * pieces)
        ]
    else:
        shapes = [(part + extra, width)] * len(parities)
    return pl.pallas_call(
        kernel,
        grid_spec=pltpu.PrefetchScalarGridSpec(
            num_scalar_prefetch=1,
            grid=(1,),
            in_specs=[
                near
                if n in held
                else pl.BlockSpec((size, width), lambda i, s, at=at: (at, 0))
                for n, (_, size, at) in enumerate(pieces_of)
            ]
            + [near] * len(adds)
            + [spec(g.shape) for g in gains]
            + [pl.BlockSpec(memory_space=pl.ANY)] * len(deps),
            out_specs=[near] * len(shapes),
        ),
        out_shape=[jax.ShapeDtypeStruct(s, F32) for s in shapes],
        compiler_params=pltpu.CompilerParams(vmem_limit_bytes=SMALL_BYTES if len(runs) == 1 else WEIGHT_BYTES),
        cost_estimate=pl.CostEstimate(
            flops=1 << 33 if len(runs) > 1 else 1024, bytes_accessed=1024, transcendentals=0
        ),
        name="weight_part",
    )(scal, *operands, *adds, *gains, *deps)


def block_kernel(blocks, count, scal_ref, *refs):
    groups = (refs[:count], refs[count : 2 * count])
    outs = refs[2 * count :]
    columns = groups[0][0].shape[1]
    size = groups[1][0].shape[0] // blocks
    whole = blocks * size
    for o, out in enumerate(outs):
        at = pl.ds(pl.multiple_of((scal_ref[0] ^ o) * size, size), size)
        for n, parts in enumerate(groups):
            total = parts[0][at]
            for p in parts[1:]:
                total = total + p[at]
            out[:size, n * columns : (n + 1) * columns] = total
        if out.shape[0] > size:
            total = groups[0][0][whole:]
            for p in groups[0][1:]:
                total = total + p[whole:]
            out[size:, :columns] = total
            out[size:, columns:] = total


def sum_kernel(factor, scal_ref, *refs):
    total = refs[0][...]
    for ref in refs[1:-1]:
        total = total + ref[...]
    refs[-1][...] = total * factor


def place_kernel(pieces, devices, scal_ref, *refs):
    qkv_ref, out_ref = refs[-2], refs[-1]
    width = out_ref.shape[1]
    bits = devices.bit_length() - 1
    for n in range(pieces):
        for o in range(devices):
            src = refs[n * devices + o]
            part = src.shape[1] // 2
            size = out_ref.shape[0]
            device = scal_ref[0] ^ o
            for group in range(2):
                value = (slice(0, size), slice(group * part, (group + 1) * part))
                rest = [b for b in range(bits) if b != group]
                at = ((device >> rest[0]) & 1) * (width // 2) + n * (width // 2 // pieces)
                unit = width // 2 // pieces
                for b in rest[1:]:
                    unit = unit // 2
                    at = at + ((device >> b) & 1) * unit
                which = (device >> group) & 1
                if group == 0:
                    at = pl.multiple_of(at + which * width, part)
                    qkv_ref[:, pl.ds(at, part)] = src[value]
                else:

                    @pl.when(which == 0)
                    def _(src=src, value=value, at=at, part=part):
                        cols = pl.ds(pl.multiple_of(at + 2 * width, part), part)
                        qkv_ref[:, cols] = src[value]

                    @pl.when(which != 0)
                    def _(src=src, value=value, at=at, part=part):
                        out_ref[:, pl.ds(pl.multiple_of(at, part), part)] = src[value]


def exchange(x, axis, bits, size):
    return lax.ppermute(x, axis, [(i, i ^ bits) for i in range(size)])


def whole_call(kernel, name, scal, out_shape, operands, deps=(), scratch=(), flops=0, limit=SMALL_BYTES, near=(False, False)):
    scal = scal if isinstance(scal, tuple) else (scal,)

    def body(*refs):
        used = len(scal) + len(operands)
        kernel(*refs[:used], *refs[used + len(deps) :])

    def spec(shape):
        return pl.BlockSpec(shape, lambda i, *s: (0,) * len(shape))

    vmem = pl.BlockSpec(memory_space=pltpu.VMEM)
    moved = sum(int(np.prod(o.shape)) * o.dtype.itemsize for o in [*operands, *out_shape])
    return pl.pallas_call(
        body,
        grid_spec=pltpu.PrefetchScalarGridSpec(
            num_scalar_prefetch=len(scal),
            grid=(1,),
            in_specs=[vmem if near[0] else spec(o.shape) for o in operands]
            + [pl.BlockSpec(memory_space=pl.ANY)] * len(deps),
            out_specs=[vmem if near[1] else spec(o.shape) for o in out_shape],
            scratch_shapes=list(scratch),
        ),
        out_shape=out_shape,
        compiler_params=pltpu.CompilerParams(vmem_limit_bytes=limit),
        cost_estimate=pl.CostEstimate(flops=1024, bytes_accessed=1024, transcendentals=0),
        name=name,
    )(*scal, *operands, *deps)


def local(
    face_tokens,
    edge_tokens,
    face_cotangent,
    edge_cotangent,
    rotation,
    counts,
    norm_gain,
    qkv_weight,
    out_weight,
):
    T = lax.axis_size("tile")
    D = lax.axis_size("dp")
    me_t = lax.axis_index("tile")
    me_d = lax.axis_index("dp")
    LD, FL, width = face_tokens.shape[1:]
    K = edge_tokens.shape[1]
    EL = K * T
    NLG = edge_tokens.shape[2]
    length = FL + EL
    chunks = 2
    lines = LD // chunks
    RB = lines * K
    packed = T * 2 * RB
    factor = float(D * T * LD * length) ** (-0.5)
    x_bit = (me_d % 2).astype(jnp.int32)
    y_bit = ((me_d // 2) % 2).astype(jnp.int32)
    gain = norm_gain.reshape(1, width)

    def struct(*shape, dtype=BF):
        return jax.ShapeDtypeStruct(shape, dtype)

    order = np.zeros((chunks, T, 2, lines, K), np.int32)
    for c in range(chunks):
        for w in range(2):
            t, l, k = np.meshgrid(np.arange(T), np.arange(lines), np.arange(K), indexing="ij")
            order[c, :, w] = w * K * NLG + k * NLG + t * LD + c * lines + l
    sent = whole_call(
        lambda s, *refs: pack_kernel(*refs),
        "pack",
        y_bit.reshape(1),
        [struct(packed, width)] * chunks,
        [
            edge_tokens.reshape(K * NLG, width),
            edge_cotangent.reshape(K * NLG, width),
            jnp.asarray(order.reshape(-1, 1)),
        ],
        scratch=[pltpu.VMEM((2 * K * NLG, width), BF)],
        limit=VMEM_BYTES,
    )
    arrived = [lax.all_to_all(s, "tile", split_axis=0, concat_axis=0, tiled=True) for s in sent]

    face_rows = face_tokens.reshape(LD * FL, width)
    face_cots = face_cotangent.reshape(LD * FL, width)
    face_normed, face_early = whole_call(
        face_kernel,
        "face_norm",
        y_bit.reshape(1),
        [struct(LD * FL, width)] * 2,
        [face_rows, face_cots, gain],
        limit=VMEM_BYTES,
    )
    got_face_a = exchange(face_normed, "dp", 1, D)
    got_face_b = exchange(face_early, "dp", 2, D)

    edges = lines * EL
    l, p = np.meshgrid(np.arange(lines), np.arange(EL), indexing="ij")
    table = []
    for pos in (p, EL - 1 - p):
        row = (pos // K) * (2 * RB) + l * K + pos % K
        table.append(np.stack([row, row + RB]))
    table.append(np.stack([l, l]))
    index = jnp.asarray(np.stack(table, axis=-1).reshape(-1, 3).astype(np.int32))
    t, c, w, l, k = np.meshgrid(
        np.arange(T),
        np.arange(chunks),
        np.arange(2),
        np.arange(lines),
        np.arange(K),
        indexing="ij",
    )
    at = 2 * c * edges + w * edges + l * EL
    pos = t * K + k
    table = [at + pos, at + EL - 1 - pos, c * lines + l]
    back_index = jnp.asarray(np.stack(table, axis=-1).reshape(-1, 3).astype(np.int32))
    edge_parts, results, got_edges, got_late = [], [], [], []
    faces = None
    for c in range(chunks):
        base = (me_t * LD + c * lines).astype(jnp.int32)
        scal = (jnp.stack([base, x_bit, y_bit]), rotation, counts)
        rows_all = lines * length
        row_shape = (rows_all, width)
        face_spec = pl.BlockSpec((1, lines, FL, width), lambda i, *s, c=c: (0, c, 0, 0))
        normed_spec = pl.BlockSpec((lines * FL, width), lambda i, *s, c=c: (c, 0))

        def full(shape):
            return pl.BlockSpec(shape, lambda i, *s: (0,) * len(shape))

        if c == 0:
            operands = [face_tokens, face_cotangent, arrived[c], index]
            operands += [face_normed, gain, qkv_weight, out_weight]
            tail = []
        else:
            z_edge, g_edge, normed_edge, early_edge = whole_call(
                functools.partial(edge_kernel, lines),
                "edge_norm",
                scal,
                [struct(edges, width)] * 4,
                [arrived[c], index, gain],
                deps=[results[0][5]],
                limit=VMEM_BYTES,
            )
            operands = [face_tokens, face_cotangent, z_edge, g_edge, normed_edge]
            operands += [face_normed, gain, qkv_weight, out_weight, back_index, results[0][0]]
            tail = [*faces, got_face_a, got_face_b]
        in_specs = [
            face_spec
            if n < 2
            else normed_spec
            if o is face_normed
            else pl.BlockSpec(memory_space=pl.ANY)
            if o is qkv_weight or o is out_weight
            else full(o.shape)
            for n, o in enumerate(operands)
        ]
        in_specs += [pl.BlockSpec(memory_space=pl.ANY)] * len(tail)
        aliases = {} if c == 0 else {3 + len(operands): 0, 4 + len(operands): 1}
        operands += tail
        back_rows = 2 * edges if c == 0 else packed * chunks
        edge_outs = [(edges, width)] * 2 if c == 0 else []
        send_shape = (rows_all + (edges if c == 0 else 0), width)
        outs = pl.pallas_call(
            functools.partial(layer_kernel, lines, c == 0, len(tail)),
            grid_spec=pltpu.PrefetchScalarGridSpec(
                num_scalar_prefetch=3,
                grid=(1,),
                in_specs=in_specs,
                out_specs=[face_spec, face_spec, full((back_rows, width))]
                + [pl.BlockSpec(memory_space=pl.ANY)] * 4
                + [full((8, width // 8))]
                + [full(e) for e in edge_outs],
                scratch_shapes=[
                    pltpu.VMEM(row_shape, BF),
                    pltpu.VMEM(row_shape, BF),
                    pltpu.VMEM(row_shape, BF),
                    pltpu.VMEM((rows_all, 3 * width), BF),
                    pltpu.VMEM(row_shape, BF),
                    pltpu.VMEM(row_shape, BF),
                    pltpu.VMEM((rows_all, 3 * width), BF),
                    pltpu.VMEM(row_shape, F32),
                    pltpu.VMEM(row_shape, BF),
                    pltpu.VMEM((2 * edges * (c + 1), width), BF),
                ]
                + ([pltpu.VMEM((edges, width), BF)] * 2 if c == 0 else [])
                + [
                    pltpu.VMEM(qkv_weight.shape, BF),
                    pltpu.VMEM(out_weight.shape, BF),
                    pltpu.SemaphoreType.DMA((3 * width // 512 + 1,)),
                    pltpu.SemaphoreType.DMA((6,)),
                ],
            ),
            out_shape=[struct(*face_tokens.shape)] * 2
            + [struct(back_rows, width)]
            + [struct(*row_shape), struct(*send_shape)] * 2
            + [struct(8, width // 8, dtype=F32)]
            + [struct(*e) for e in edge_outs],
            input_output_aliases=aliases,
            compiler_params=pltpu.CompilerParams(vmem_limit_bytes=VMEM_BYTES),
            cost_estimate=pl.CostEstimate(flops=1 << 35, bytes_accessed=1 << 20, transcendentals=0),
            name="layer",
        )(*scal, *operands)
        faces = outs[:2]
        results.append(outs[2:])
        late_a, late_b = exchange(outs[4], "dp", 1, D), exchange(outs[6], "dp", 2, D)
        if c == 0:
            g_edge, normed_edge = outs[8:]
            edges_a, edges_b = (late_a, edges, rows_all // edges), (late_b, edges, rows_all // edges)
            late_a, late_b = (late_a, rows_all, 0), (late_b, rows_all, 0)
        else:
            edges_a = exchange(normed_edge, "dp", 1, D)
            edges_b = exchange(early_edge, "dp", 2, D)
        edge_parts.append((normed_edge, g_edge))
        got_edges.append((edges_a, edges_b))
        got_late.append((late_a, late_b))
    returned = lax.all_to_all(results[1][0], "tile", split_axis=0, concat_axis=0, tiled=True)

    blocks = T // 2
    chip = (me_t // 2).astype(jnp.int32)
    core = (me_t % 2).astype(jnp.int32)
    pieces = 2
    size = width // T
    bits = D.bit_length() - 1
    groups = []
    for group in range(2):
        first = [b for b in range(bits) if b != group][0]
        swap = y_bit if group else jnp.zeros_like(y_bit)
        scal = jnp.stack([core, swap, ((me_d >> first) & 1).astype(jnp.int32)])
        late = [r[1 + 2 * group] for r in results]
        got_face = (got_face_a, got_face_b)[group]
        normed_e, g_e = [e[0] for e in edge_parts], [e[1] for e in edge_parts]
        got_e = [e[group] for e in got_edges]
        got_l = [e[group] for e in got_late]
        operands = [face_normed, face_cots, *normed_e, *g_e, got_face, got_e[0], late[0], late[1], got_l[0]]
        runs = [((0, 1), (2, 4), 0, 8), ((0, 1), (3, 5), 1, 9), ((6, 6), (7, 7), 0, 10)]
        start = weight_part(
            scal, runs, (False, True), blocks, operands, [], pieces, False, [],
            [*got_edges[1], got_late[0][0][0], got_late[0][1][0]],
        )
        groups.append((scal, [got_face, got_e[1], got_l[1]], start, first))
    theirs = []
    runs = [((0, 0), (1, 1), 1, 2)]
    gains = [[r[5] for r in results], []]
    starts = [g[2] for g in groups]
    for group, (scal, operands, start, first) in enumerate(groups):
        send = weight_part(
            scal, runs, (False,), blocks, operands, [start[0]], pieces, False, gains[group],
            [] if group else [starts[1][0]],
            held=(2,),
        )[0]
        theirs.append(exchange(send, "tile", 1, T))
    halves = []
    for group, (scal, operands, start, first) in enumerate(groups):
        outs = weight_part(
            scal, runs, (True,), blocks, operands, [start[1], theirs[group]], pieces, True,
            gains[group], [], held=(2,),
        )
        parts = []
        for n in range(pieces):
            both = [outs[pieces + n], exchange(outs[n], "dp", 1 << first, D)]
            for b in range(bits):
                if b in (group, first):
                    continue
                columns = both[0].shape[1] // 2
                mine = (me_d >> b) & 1
                keep = [lax.dynamic_slice_in_dim(p, mine * columns, columns, 1) for p in both]
                give = [lax.dynamic_slice_in_dim(p, (1 - mine) * columns, columns, 1) for p in both]
                both = [sum(keep), exchange(sum(give), "dp", 1 << b, D)]
            parts.append(both)
        halves.append(parts)
    placed = []
    for n in range(pieces):
        parts = [*halves[0][n], *halves[1][n]]
        columns = 2 * parts[0].shape[1]
        outs = whole_call(
            functools.partial(block_kernel, blocks, 2),
            "row_blocks",
            chip.reshape(1),
            [struct(size + (8 if n == 0 else 0), columns, dtype=F32)] * blocks,
            parts,
            near=(True, True),
            deps=[returned] if n == 0 else [],
        )
        got = [exchange(outs[o], "tile", 2 * o, T) for o in range(1, blocks)]
        (mine,) = whole_call(
            functools.partial(sum_kernel, factor),
            "block_sum",
            chip.reshape(1),
            [struct(*outs[0].shape, dtype=F32)],
            [outs[0], *got],
            near=(True, True),
        )
        placed += [mine] + [exchange(mine, "dp", o, D) for o in range(1, D)]

    back_order = np.zeros((2, K, NLG), np.int32)
    for w in range(2):
        k, t, c, l = np.meshgrid(
            np.arange(K), np.arange(T), np.arange(chunks), np.arange(lines), indexing="ij"
        )
        back_order[w] = ((t * chunks + c) * 2 * RB + w * RB + l * K + k).reshape(K, NLG)
    edge_output, edge_grad = whole_call(
        lambda s, *refs: unpack_kernel(1, *refs),
        "unpack",
        chip.reshape(1),
        [struct(K * NLG, width)] * 2,
        [returned, jnp.asarray(back_order.reshape(-1, 1))],
        scratch=[pltpu.VMEM((chunks * packed, width), BF)],
    )
    qkv_grad, out_grad = whole_call(
        functools.partial(place_kernel, pieces, D),
        "place",
        me_d.astype(jnp.int32).reshape(1),
        [struct(size, 3 * width, dtype=F32), struct(size, width, dtype=F32)],
        placed,
        near=(True, False),
    )
    gain_sum = (placed[0] + placed[1])[size:, : width // 8].reshape(width)
    gain_grad = lax.dynamic_slice_in_dim(gain_sum, me_t * size, size)
    shape = edge_tokens.shape
    return (
        faces[0],
        edge_output.reshape(shape),
        faces[1],
        edge_grad.reshape(shape),
        qkv_grad,
        out_grad,
        gain_grad,
    )


def solution(mesh):
    return jax.shard_map(
        local,
        mesh=mesh,
        in_specs=(
            P("dp", "tile", None, None),
            P("dp", "tile", None, None),
            P("dp", "tile", None, None),
            P("dp", "tile", None, None),
            P(),
            P(),
            P(),
            P(),
            P(),
        ),
        out_specs=(
            P("dp", "tile", None, None),
            P("dp", "tile", None, None),
            P("dp", "tile", None, None),
            P("dp", "tile", None, None),
            P("tile", None),
            P("tile", None),
            P("tile"),
        ),
        check_vma=False,
    )
```

```python
import functools

import jax
import jax.numpy as jnp
import numpy as np
from jax import lax
from jax.experimental import pallas as pl
from jax.experimental.pallas import tpu as pltpu
from jax.sharding import PartitionSpec as P

HEADS = 16
BF = jnp.bfloat16
F32 = jnp.float32
VMEM_BYTES = 60 * 1024 * 1024
SMALL_BYTES = 28 * 1024 * 1024
WEIGHT_BYTES = 54 * 1024 * 1024


def nn(a, b):
    return lax.dot_general(a, b, (((1,), (0,)), ((), ())), preferred_element_type=F32)


def nt(a, b):
    return lax.dot_general(a, b, (((1,), (1,)), ((), ())), preferred_element_type=F32)


def tn(a, b):
    return lax.dot_general(a, b, (((0,), (0,)), ((), ())), preferred_element_type=F32)


def one_hot(index_ref, width):
    rows = index_ref.shape[0]
    columns = lax.broadcasted_iota(jnp.int32, (rows, width), 1)
    return jnp.where(columns == index_ref[...], 1.0, 0.0).astype(BF)


def pack_kernel(tok_ref, cot_ref, index_ref, *refs):
    both = refs[-1]
    rows = tok_ref.shape[0]
    both[:rows] = tok_ref[...]
    both[rows:] = cot_ref[...]
    take = index_ref.shape[0] // (len(refs) - 1)
    for c, out in enumerate(refs[:-1]):
        columns = lax.broadcasted_iota(jnp.int32, (take, 2 * rows), 1)
        picked = jnp.where(columns == index_ref[c * take : (c + 1) * take], 1.0, 0.0).astype(BF)
        out[...] = nn(picked, both[...]).astype(BF)


def unpack_kernel(chunks, *refs):
    backs, index_ref, out_tok, out_cot, both = refs[:chunks], refs[chunks], refs[-3], refs[-2], refs[-1]
    take = backs[0].shape[0]
    for c, back in enumerate(backs):
        both[c * take : (c + 1) * take] = back[...]
    rows = out_tok.shape[0]
    for w, out in enumerate((out_tok, out_cot)):
        columns = lax.broadcasted_iota(jnp.int32, (rows, chunks * take), 1)
        picked = jnp.where(columns == index_ref[w * rows : (w + 1) * rows], 1.0, 0.0).astype(BF)
        out[...] = nn(picked, both[...]).astype(BF)


def face_kernel(scal_ref, face_ref, fcot_ref, gain_ref, normed_ref, early_ref):
    hidden = face_ref[...].astype(F32)
    inverse = lax.rsqrt(jnp.mean(hidden * hidden, axis=-1, keepdims=True) + 1e-06)
    normed = (hidden * inverse * gain_ref[...]).astype(BF)
    normed_ref[...] = normed
    early_ref[...] = jnp.where(scal_ref[0] == 0, fcot_ref[...], normed)


def flips(line_ref, rotation_ref, base, lines):
    line = line_ref[:, 2:3]
    flip = jnp.zeros_like(line)
    for l in range(lines):
        turned = (rotation_ref[base + l] >= 2).astype(jnp.int32)
        flip = jnp.where(line == l, turned, flip)
    return jnp.where(flip != 0, line_ref[:, 1:2], line_ref[:, 0:1])


def turn_pair(rotation_ref, at):
    turn = rotation_ref[at]
    cosine = (turn == 0).astype(F32) - (turn == 2).astype(F32)
    sine = (turn == 1).astype(F32) - (turn == 3).astype(F32)
    return cosine, sine


def one_hot_rows(index, width):
    columns = lax.broadcasted_iota(jnp.int32, (index.shape[0], width), 1)
    return jnp.where(columns == index, 1.0, 0.0).astype(BF)


def edge_kernel(
    lines,
    scal_ref,
    rotation_ref,
    counts_ref,
    arrived_ref,
    index_ref,
    gain_ref,
    z_ref,
    g_ref,
    normed_ref,
    early_ref,
):
    half = z_ref.shape[1] // 2
    edges = z_ref.shape[0]
    edge_len = edges // lines
    base = scal_ref[0]
    index = flips(index_ref, rotation_ref, base, lines)
    picked = one_hot_rows(index, arrived_ref.shape[0])
    first = nn(picked, arrived_ref[:, :half])
    second = nn(picked, arrived_ref[:, half:])
    for l in range(lines):
        cosine, sine = turn_pair(rotation_ref, base + l)

        def turned(at):
            u, v = first[at : at + edge_len], second[at : at + edge_len]
            return jnp.concatenate([cosine * u - sine * v, sine * u + cosine * v], axis=1)

        rows = slice(l * edge_len, (l + 1) * edge_len)
        hidden = turned(l * edge_len)
        g = turned(edges + l * edge_len).astype(BF)
        z_ref[rows] = hidden.astype(BF)
        g_ref[rows] = g
        inverse = lax.rsqrt(jnp.mean(hidden * hidden, axis=-1, keepdims=True) + 1e-06)
        normed = (hidden * inverse * gain_ref[...]).astype(BF)
        normed_ref[rows] = normed
        early_ref[rows] = jnp.where(scal_ref[2] == 0, g, normed)


def layer_kernel(
    lines, first_chunk, drop, scal_ref, rotation_ref, counts_ref, face_ref, fcot_ref, *refs
):
    base = scal_ref[0]
    wqkv_hbm, wo_hbm = (refs[4:6]) if first_chunk else refs[5:7]
    wqkv_ref, wo_ref, in_sems, out_sems = refs[-4:]
    refs = refs[:-4]
    tile = 1024

    def fetch(j):
        cols = pl.ds(j * tile if isinstance(j, int) else pl.multiple_of(j * tile, tile), tile)
        return pltpu.make_async_copy(wqkv_hbm.at[:, cols], wqkv_ref.at[:, cols], in_sems.at[j])

    tiles = wqkv_ref.shape[1] // tile
    fetch_out = pltpu.make_async_copy(wo_hbm, wo_ref, in_sems.at[tiles])
    for j in range(tiles):
        fetch(j).start()
    fetch_out.start()
    moves = []
    if first_chunk:
        arrived_ref, index_ref, normed_face_ref, gain_ref = refs[:4]
        refs = refs[6 + drop :]
        send_a, send_b = refs[4], refs[6]
        g_edge_ref, normed_edge_ref = refs[8:10]
        early_ref, z_edge_ref = refs[-2:]
        refs = (*refs[:8], *refs[10:-2])
        late_rows = refs[3].shape[0]
        edge_rows = z_edge_ref.shape[0]
        edge_kernel(
            lines,
            scal_ref,
            rotation_ref,
            counts_ref,
            arrived_ref,
            index_ref,
            gain_ref,
            z_edge_ref,
            g_edge_ref,
            normed_edge_ref,
            early_ref,
        )
        for n, (src, dst) in enumerate(((normed_edge_ref, send_a), (early_ref, send_b))):
            to = dst.at[pl.ds(late_rows, edge_rows)]
            moves.append(pltpu.make_async_copy(src, to, out_sems.at[4 + n]))
            moves[-1].start()
    else:
        z_edge_ref, g_edge_ref, normed_edge_ref = refs[:3]
        normed_face_ref, gain_ref = refs[3:5]
        back_index_ref, before_ref = refs[7:9]
        refs = refs[9 + drop :]
    (
        face_out,
        face_grad,
        back_ref,
        keep_a,
        send_a,
        keep_b,
        send_b,
        gain_part,
        z_s,
        g_s,
        norm_s,
        qkv_s,
        dm_s,
        mix_s,
        stk_s,
        dn_s,
        y_s,
        edge_s,
    ) = refs
    width = z_s.shape[1]
    half = width // 2
    face_len = face_ref.shape[2]
    edges = z_edge_ref.shape[0]
    edge_len = edges // lines
    length = face_len + edge_len
    faces = lines * face_len
    head_dim = width // HEADS
    scale = head_dim ** (-0.5)
    gain = gain_ref[...]

    for l in range(lines):
        z_s[l * face_len : (l + 1) * face_len] = face_ref[0, l]
        g_s[l * face_len : (l + 1) * face_len] = fcot_ref[0, l]
    z_s[faces:] = z_edge_ref[...]
    g_s[faces:] = g_edge_ref[...]
    norm_s[:faces] = normed_face_ref[...]
    norm_s[faces:] = normed_edge_ref[...]

    @pl.loop(0, tiles)
    def _(j):
        cols = pl.ds(pl.multiple_of(j * tile, tile), tile)
        fetch(j).wait()
        qkv_s[:, cols] = nn(norm_s[...], wqkv_ref[:, cols]).astype(BF)

    fetch_out.wait()

    @pl.loop(0, width // tile)
    def _(j):
        cols = pl.ds(pl.multiple_of(j * tile, tile), tile)
        dm_s[:, cols] = nt(g_s[...], wo_ref[cols, :]).astype(BF)

    pair = 2 * head_dim
    low = lax.broadcasted_iota(jnp.int32, (length, pair), 1) < head_dim
    key_row = lax.broadcasted_iota(jnp.int32, (length, length), 0)

    def split(x):
        zero = jnp.zeros_like(x)
        return jnp.concatenate([jnp.where(low, x, zero), jnp.where(low, zero, x)], axis=0)

    @pl.loop(0, lines)
    def _(l):
        top = pl.ds(pl.multiple_of(l * face_len, face_len), face_len)
        bottom = pl.ds(pl.multiple_of(faces + l * edge_len, edge_len), edge_len)
        live = key_row < counts_ref[base + l] + face_len

        def load(ref, at):
            return jnp.concatenate([ref[top, at : at + pair], ref[bottom, at : at + pair]], axis=0)

        def store(ref, at, value):
            ref[top, at : at + pair] = value[:face_len].astype(BF)
            ref[bottom, at : at + pair] = value[face_len:].astype(BF)

        for p in range(HEADS // 2):
            at = p * pair
            q = load(qkv_s, at)
            k2 = split(load(qkv_s, width + at))
            v2 = split(load(qkv_s, 2 * width + at))
            dm = load(dm_s, at)
            scores = nt(k2, q * jnp.asarray(scale, BF))
            d_probs = nt(v2, dm)
            probs_b, d_scores = [], []
            for h in range(2):
                part = slice(h * length, (h + 1) * length)
                s = jnp.where(live, scores[part], -1e30)
                e = jnp.exp(s - jnp.max(s, axis=0, keepdims=True))
                probs = e * (1.0 / jnp.sum(e, axis=0, keepdims=True))
                d = d_probs[part]
                inner = jnp.sum(probs * d, axis=0, keepdims=True)
                probs_b.append(probs.astype(BF))
                d_scores.append((probs * (d - inner)).astype(BF))
            pb = jnp.concatenate(probs_b, axis=0)
            ds = jnp.concatenate(d_scores, axis=0)
            store(mix_s, at, tn(pb, v2))
            dv = nn(pb, dm)
            store(stk_s, 2 * width + at, jnp.where(low, dv[:length], dv[length:]))
            store(stk_s, at, tn(ds, k2) * scale)
            dk = nn(ds, q)
            store(stk_s, width + at, jnp.where(low, dk[:length], dk[length:]) * scale)

    total_rows = z_s.shape[0]
    targets = (keep_a, send_a, keep_b, send_b)
    third = [stk_s.at[:, pl.ds(n * width, width)] for n in range(3)]
    sources = (third[0], third[1], third[2], mix_s)

    def ship(at, order):
        for n, src in enumerate(order):
            dst = targets[at + n].at[pl.ds(0, total_rows)]
            pltpu.make_async_copy(sources[src], dst, out_sems.at[at + n]).start()

    for at, bit in ((0, scal_ref[1]), (2, scal_ref[2])):

        @pl.when(bit == 0)
        def _(at=at):
            ship(at, (at, at + 1))

        @pl.when(bit != 0)
        def _(at=at):
            ship(at, (at + 1, at))

    @pl.loop(0, width // tile)
    def _(j):
        cols = pl.ds(pl.multiple_of(j * tile, tile), tile)
        y_s[:, cols] = (nn(mix_s[...], wo_ref[:, cols]) + z_s[:, cols].astype(F32)).astype(BF)
        dn_s[:, cols] = nt(stk_s[...], wqkv_ref[cols, :])

    gain_sum = jnp.zeros((1, width), F32)
    off = 0 if first_chunk else 2 * edges
    for i in range(2 * lines):
        size = face_len if i < lines else edge_len
        start = i * face_len if i < lines else faces + (i - lines) * edge_len
        at = slice(start, start + size)
        hidden = z_s[at].astype(F32)
        inverse = lax.rsqrt(jnp.mean(hidden * hidden, axis=-1, keepdims=True) + 1e-06)
        d_normed = dn_s[at]
        gain_sum = gain_sum + jnp.sum(d_normed * hidden * inverse, axis=0, keepdims=True)
        scaled = d_normed * gain
        mean = jnp.mean(scaled * hidden, axis=-1, keepdims=True)
        dz = inverse * scaled - hidden * (inverse * inverse * inverse * mean)
        dz = (g_s[at].astype(F32) + dz).astype(BF)
        if i < lines:
            face_out[0, i] = y_s[at]
            face_grad[0, i] = dz
        else:
            at = off + edges + start - faces
            edge_s[at : at + size] = dz
    edge_s[off : off + edges] = y_s[faces:]
    lanes = gain_part.shape[1]
    for i in range(width // lanes):
        gain_part[i : i + 1] = gain_sum[:, i * lanes : (i + 1) * lanes]
    for i in range(2 * lines):
        cosine, sine = turn_pair(rotation_ref, base + i % lines)
        rows = slice(off + i * edge_len, off + (i + 1) * edge_len)
        u, v = edge_s[rows, :half].astype(F32), edge_s[rows, half:].astype(F32)
        edge_s[rows, :half] = (cosine * u + sine * v).astype(BF)
        edge_s[rows, half:] = (cosine * v - sine * u).astype(BF)
    if first_chunk:
        back_ref[...] = edge_s[...]
    else:
        edge_s[:off] = before_ref[...]
        picked = one_hot_rows(
            flips(back_index_ref, rotation_ref, base - lines, 2 * lines), 4 * edges
        )
        back_ref[...] = nn(picked, edge_s[...]).astype(BF)

    for n, dst in enumerate(targets):
        pltpu.make_async_copy(sources[n], dst.at[pl.ds(0, total_rows)], out_sems.at[n]).wait()
    for move in moves:
        move.wait()


def weight_kernel(runs, parities, blocks, count, adds, gains, halved, scal_ref, *refs):
    operands = refs[:count]
    add_refs = refs[count : count + adds]
    gain_refs = refs[count + adds : count + adds + gains]
    outs = refs[count + adds + gains :]
    width = operands[-1].shape[1]
    part = width // 2
    size = part // blocks
    rows = len(parities) * part

    def pick(src):
        kept = []
        for own in parities:
            first = scal_ref[0] == (0 if own else 1)
            for b in range(blocks):
                left = src[:, 2 * b * size : (2 * b + 1) * size]
                right = src[:, (2 * b + 1) * size : (2 * b + 2) * size]
                kept.append(jnp.where(first, left, right))
        return jnp.concatenate(kept, axis=1)

    def run(swapped):
        early, late = [], []
        for faces, edges, chunk, late_at in runs:
            edge = operands[edges[swapped]]
            front = operands[late_at].shape[0] - edge.shape[0]
            early += [operands[faces[swapped]][chunk * front : (chunk + 1) * front], edge[...]]
            late.append(operands[late_at][...])
        early, late = jnp.concatenate(early, axis=0), jnp.concatenate(late, axis=0)
        lhs, rhs = (late, early) if swapped else (early, late)
        lhs = pick(lhs)
        if not halved:
            total = tn(lhs, rhs)
            for ref in add_refs:
                total = total + ref[:rows]
            for n, out in enumerate(outs):
                out[:part] = total[n * part : (n + 1) * part]
            return
        for half in range(2):
            mine = (scal_ref[2] if half else 1 - scal_ref[2]) == 0
            left = slice(halved[0], halved[0] + halved[1])
            right = slice(part + halved[0], part + halved[0] + halved[1])
            total = tn(lhs, jnp.where(mine, rhs[:, left], rhs[:, right]))
            for ref in add_refs:
                total = total + jnp.where(mine, ref[:rows, left], ref[:rows, right])
            outs[half][:rows] = total

    @pl.when(scal_ref[1] == 0)
    def _():
        run(0)

    @pl.when(scal_ref[1] != 0)
    def _():
        run(1)

    if gains:
        total = gain_refs[0][...]
        for ref in gain_refs[1:]:
            total = total + ref[...]
        lanes = total.shape[1]
        if halved:
            total = total + add_refs[-1][rows:, :lanes]
        for out in outs:
            if out.shape[0] > rows:
                for n in range(out.shape[1] // lanes):
                    out[rows:, n * lanes : (n + 1) * lanes] = total


def weight_part(
    scal, runs, parities, blocks, operands, adds, halved, gains, deps, held=()
):
    pieces_of = [o if isinstance(o, tuple) else (o, o.shape[0], 0) for o in operands]
    operands = [o for o, _, _ in pieces_of]
    width = operands[-1].shape[1]
    part = width // 2
    rows = len(parities) * part
    depth = len(runs) * pieces_of[runs[0][3]][1]
    extra = gains[0].shape[0] if gains else 0
    used = len(operands) + len(adds) + len(gains)

    def kernel(scal_ref, *refs):
        refs = refs[:used] + refs[used + len(deps) :]
        weight_kernel(
            runs, parities, blocks, len(operands), len(adds), len(gains), halved, scal_ref, *refs
        )

    def spec(shape):
        return pl.BlockSpec(shape, lambda i, s: (0, 0))

    near = pl.BlockSpec(memory_space=pltpu.VMEM)
    if halved:
        shapes = [(rows + extra, halved[1])] * 2
    else:
        shapes = [(part + extra, width)] * len(parities)
    return pl.pallas_call(
        kernel,
        grid_spec=pltpu.PrefetchScalarGridSpec(
            num_scalar_prefetch=1,
            grid=(1,),
            in_specs=[
                near
                if n in held
                else pl.BlockSpec((size, width), lambda i, s, at=at: (at, 0))
                for n, (_, size, at) in enumerate(pieces_of)
            ]
            + [near] * len(adds)
            + [spec(g.shape) for g in gains]
            + [pl.BlockSpec(memory_space=pl.ANY)] * len(deps),
            out_specs=[near] * len(shapes),
        ),
        out_shape=[jax.ShapeDtypeStruct(s, F32) for s in shapes],
        compiler_params=pltpu.CompilerParams(vmem_limit_bytes=SMALL_BYTES if len(runs) == 1 else WEIGHT_BYTES),
        cost_estimate=pl.CostEstimate(
            flops=1 << 33 if len(runs) > 1 else 1024, bytes_accessed=1024, transcendentals=0
        ),
        name="weight_part",
    )(scal, *operands, *adds, *gains, *deps)


def block_kernel(blocks, count, scal_ref, *refs):
    groups = (refs[:count], refs[count : 2 * count])
    outs = refs[2 * count :]
    columns = groups[0][0].shape[1]
    size = groups[1][0].shape[0] // blocks
    whole = blocks * size
    for o, out in enumerate(outs):
        at = pl.ds(pl.multiple_of((scal_ref[0] ^ o) * size, size), size)
        for n, parts in enumerate(groups):
            total = parts[0][at]
            for p in parts[1:]:
                total = total + p[at]
            out[:size, n * columns : (n + 1) * columns] = total
        if out.shape[0] > size:
            total = groups[0][0][whole:]
            for p in groups[0][1:]:
                total = total + p[whole:]
            out[size:, :columns] = total
            out[size:, columns:] = total


def sum_kernel(factor, scal_ref, *refs):
    total = refs[0][...]
    for ref in refs[1:-1]:
        total = total + ref[...]
    refs[-1][...] = total * factor


def place_kernel(pieces, devices, scal_ref, *refs):
    qkv_ref, out_ref = refs[-2], refs[-1]
    size, width = out_ref.shape
    bits = devices.bit_length() - 1
    for m, src in enumerate(refs[:-2]):
        n, o = m // devices, m % devices
        part = src.shape[1] // 2
        device = scal_ref[0] ^ o
        for group in range(2):
            value = (slice(0, size), slice(group * part, (group + 1) * part))
            rest = [b for b in range(bits) if b != group]
            at = ((device >> rest[0]) & 1) * (width // 2) + sum(pieces[:n])
            unit = pieces[n]
            for b in rest[1:]:
                unit = unit // 2
                at = at + ((device >> b) & 1) * unit
            which = (device >> group) & 1
            if group == 0:
                cols = pl.ds(pl.multiple_of(at + which * width, 128), part)
                qkv_ref[:, cols] = src[value]
            else:

                @pl.when(which == 0)
                def _(src=src, value=value, at=at, part=part):
                    cols = pl.ds(pl.multiple_of(at + 2 * width, 128), part)
                    qkv_ref[:, cols] = src[value]

                @pl.when(which != 0)
                def _(src=src, value=value, at=at, part=part):
                    out_ref[:, pl.ds(pl.multiple_of(at, 128), part)] = src[value]


def exchange(x, axis, bits, size):
    return lax.ppermute(x, axis, [(i, i ^ bits) for i in range(size)])


def whole_call(kernel, name, scal, out_shape, operands, deps=(), scratch=(), flops=0, limit=SMALL_BYTES, near=(False, False)):
    scal = scal if isinstance(scal, tuple) else (scal,)

    def body(*refs):
        used = len(scal) + len(operands)
        kernel(*refs[:used], *refs[used + len(deps) :])

    def spec(shape):
        return pl.BlockSpec(shape, lambda i, *s: (0,) * len(shape))

    vmem = pl.BlockSpec(memory_space=pltpu.VMEM)
    moved = sum(int(np.prod(o.shape)) * o.dtype.itemsize for o in [*operands, *out_shape])
    return pl.pallas_call(
        body,
        grid_spec=pltpu.PrefetchScalarGridSpec(
            num_scalar_prefetch=len(scal),
            grid=(1,),
            in_specs=[vmem if near[0] else spec(o.shape) for o in operands]
            + [pl.BlockSpec(memory_space=pl.ANY)] * len(deps),
            out_specs=[vmem if near[1] else spec(o.shape) for o in out_shape],
            scratch_shapes=list(scratch),
        ),
        out_shape=out_shape,
        compiler_params=pltpu.CompilerParams(vmem_limit_bytes=limit),
        cost_estimate=pl.CostEstimate(flops=1024, bytes_accessed=1024, transcendentals=0),
        name=name,
    )(*scal, *operands, *deps)


def local(
    face_tokens,
    edge_tokens,
    face_cotangent,
    edge_cotangent,
    rotation,
    counts,
    norm_gain,
    qkv_weight,
    out_weight,
):
    T = lax.axis_size("tile")
    D = lax.axis_size("dp")
    me_t = lax.axis_index("tile")
    me_d = lax.axis_index("dp")
    LD, FL, width = face_tokens.shape[1:]
    K = edge_tokens.shape[1]
    EL = K * T
    NLG = edge_tokens.shape[2]
    length = FL + EL
    chunks = 2
    lines = LD // chunks
    RB = lines * K
    packed = T * 2 * RB
    factor = float(D * T * LD * length) ** (-0.5)
    x_bit = (me_d % 2).astype(jnp.int32)
    y_bit = ((me_d // 2) % 2).astype(jnp.int32)
    gain = norm_gain.reshape(1, width)

    def struct(*shape, dtype=BF):
        return jax.ShapeDtypeStruct(shape, dtype)

    order = np.zeros((chunks, T, 2, lines, K), np.int32)
    for c in range(chunks):
        for w in range(2):
            t, l, k = np.meshgrid(np.arange(T), np.arange(lines), np.arange(K), indexing="ij")
            order[c, :, w] = w * K * NLG + k * NLG + t * LD + c * lines + l
    sent = whole_call(
        lambda s, *refs: pack_kernel(*refs),
        "pack",
        y_bit.reshape(1),
        [struct(packed, width)] * chunks,
        [
            edge_tokens.reshape(K * NLG, width),
            edge_cotangent.reshape(K * NLG, width),
            jnp.asarray(order.reshape(-1, 1)),
        ],
        scratch=[pltpu.VMEM((2 * K * NLG, width), BF)],
        limit=VMEM_BYTES,
    )
    arrived = [lax.all_to_all(s, "tile", split_axis=0, concat_axis=0, tiled=True) for s in sent]

    face_rows = face_tokens.reshape(LD * FL, width)
    face_cots = face_cotangent.reshape(LD * FL, width)
    face_normed, face_early = whole_call(
        face_kernel,
        "face_norm",
        y_bit.reshape(1),
        [struct(LD * FL, width)] * 2,
        [face_rows, face_cots, gain],
        limit=VMEM_BYTES,
    )
    got_face_a = exchange(face_normed, "dp", 1, D)
    got_face_b = exchange(face_early, "dp", 2, D)

    edges = lines * EL
    l, p = np.meshgrid(np.arange(lines), np.arange(EL), indexing="ij")
    table = []
    for pos in (p, EL - 1 - p):
        row = (pos // K) * (2 * RB) + l * K + pos % K
        table.append(np.stack([row, row + RB]))
    table.append(np.stack([l, l]))
    index = jnp.asarray(np.stack(table, axis=-1).reshape(-1, 3).astype(np.int32))
    t, c, w, l, k = np.meshgrid(
        np.arange(T),
        np.arange(chunks),
        np.arange(2),
        np.arange(lines),
        np.arange(K),
        indexing="ij",
    )
    at = 2 * c * edges + w * edges + l * EL
    pos = t * K + k
    table = [at + pos, at + EL - 1 - pos, c * lines + l]
    back_index = jnp.asarray(np.stack(table, axis=-1).reshape(-1, 3).astype(np.int32))
    edge_parts, results, got_edges, got_late = [], [], [], []
    faces = None
    for c in range(chunks):
        base = (me_t * LD + c * lines).astype(jnp.int32)
        scal = (jnp.stack([base, x_bit, y_bit]), rotation, counts)
        rows_all = lines * length
        row_shape = (rows_all, width)
        face_spec = pl.BlockSpec((1, lines, FL, width), lambda i, *s, c=c: (0, c, 0, 0))
        normed_spec = pl.BlockSpec((lines * FL, width), lambda i, *s, c=c: (c, 0))

        def full(shape):
            return pl.BlockSpec(shape, lambda i, *s: (0,) * len(shape))

        if c == 0:
            operands = [face_tokens, face_cotangent, arrived[c], index]
            operands += [face_normed, gain, qkv_weight, out_weight]
            tail = []
        else:
            z_edge, g_edge, normed_edge, early_edge = whole_call(
                functools.partial(edge_kernel, lines),
                "edge_norm",
                scal,
                [struct(edges, width)] * 4,
                [arrived[c], index, gain],
                deps=[results[0][5]],
                limit=VMEM_BYTES,
            )
            operands = [face_tokens, face_cotangent, z_edge, g_edge, normed_edge]
            operands += [face_normed, gain, qkv_weight, out_weight, back_index, results[0][0]]
            tail = [*faces, got_face_a, got_face_b]
        in_specs = [
            face_spec
            if n < 2
            else normed_spec
            if o is face_normed
            else pl.BlockSpec(memory_space=pl.ANY)
            if o is qkv_weight or o is out_weight
            else full(o.shape)
            for n, o in enumerate(operands)
        ]
        in_specs += [pl.BlockSpec(memory_space=pl.ANY)] * len(tail)
        aliases = {} if c == 0 else {3 + len(operands): 0, 4 + len(operands): 1}
        operands += tail
        back_rows = 2 * edges if c == 0 else packed * chunks
        edge_outs = [(edges, width)] * 2 if c == 0 else []
        send_shape = (rows_all + (edges if c == 0 else 0), width)
        outs = pl.pallas_call(
            functools.partial(layer_kernel, lines, c == 0, len(tail)),
            grid_spec=pltpu.PrefetchScalarGridSpec(
                num_scalar_prefetch=3,
                grid=(1,),
                in_specs=in_specs,
                out_specs=[face_spec, face_spec, full((back_rows, width))]
                + [pl.BlockSpec(memory_space=pl.ANY)] * 4
                + [full((8, width // 8))]
                + [full(e) for e in edge_outs],
                scratch_shapes=[
                    pltpu.VMEM(row_shape, BF),
                    pltpu.VMEM(row_shape, BF),
                    pltpu.VMEM(row_shape, BF),
                    pltpu.VMEM((rows_all, 3 * width), BF),
                    pltpu.VMEM(row_shape, BF),
                    pltpu.VMEM(row_shape, BF),
                    pltpu.VMEM((rows_all, 3 * width), BF),
                    pltpu.VMEM(row_shape, F32),
                    pltpu.VMEM(row_shape, BF),
                    pltpu.VMEM((2 * edges * (c + 1), width), BF),
                ]
                + ([pltpu.VMEM((edges, width), BF)] * 2 if c == 0 else [])
                + [
                    pltpu.VMEM(qkv_weight.shape, BF),
                    pltpu.VMEM(out_weight.shape, BF),
                    pltpu.SemaphoreType.DMA((3 * width // 512 + 1,)),
                    pltpu.SemaphoreType.DMA((6,)),
                ],
            ),
            out_shape=[struct(*face_tokens.shape)] * 2
            + [struct(back_rows, width)]
            + [struct(*row_shape), struct(*send_shape)] * 2
            + [struct(8, width // 8, dtype=F32)]
            + [struct(*e) for e in edge_outs],
            input_output_aliases=aliases,
            compiler_params=pltpu.CompilerParams(vmem_limit_bytes=VMEM_BYTES),
            cost_estimate=pl.CostEstimate(flops=1 << 35, bytes_accessed=1 << 20, transcendentals=0),
            name="layer",
        )(*scal, *operands)
        faces = outs[:2]
        results.append(outs[2:])
        late_a, late_b = exchange(outs[4], "dp", 1, D), exchange(outs[6], "dp", 2, D)
        if c == 0:
            g_edge, normed_edge = outs[8:]
            edges_a, edges_b = (late_a, edges, rows_all // edges), (late_b, edges, rows_all // edges)
            late_a, late_b = (late_a, rows_all, 0), (late_b, rows_all, 0)
        else:
            edges_a = exchange(normed_edge, "dp", 1, D)
            edges_b = exchange(early_edge, "dp", 2, D)
        edge_parts.append((normed_edge, g_edge))
        got_edges.append((edges_a, edges_b))
        got_late.append((late_a, late_b))
    returned = lax.all_to_all(results[1][0], "tile", split_axis=0, concat_axis=0, tiled=True)

    blocks = T // 2
    chip = (me_t // 2).astype(jnp.int32)
    core = (me_t % 2).astype(jnp.int32)
    quarter = width // 8
    pieces = (2 * quarter, 2 * quarter)
    size = width // T
    bits = D.bit_length() - 1
    groups = []
    for group in range(2):
        first = [b for b in range(bits) if b != group][0]
        swap = y_bit if group else jnp.zeros_like(y_bit)
        scal = jnp.stack([core, swap, ((me_d >> first) & 1).astype(jnp.int32)])
        late = [r[1 + 2 * group] for r in results]
        got_face = (got_face_a, got_face_b)[group]
        normed_e, g_e = [e[0] for e in edge_parts], [e[1] for e in edge_parts]
        got_e = [e[group] for e in got_edges]
        got_l = [e[group] for e in got_late]
        operands = [face_normed, face_cots, *normed_e, *g_e, got_face, got_e[0], late[0], late[1], got_l[0]]
        runs = [((0, 1), (2, 4), 0, 8), ((0, 1), (3, 5), 1, 9), ((6, 6), (7, 7), 0, 10)]
        start = weight_part(
            scal, runs, (False, True), blocks, operands, [], None, [],
            [*got_edges[1], got_late[0][0][0], got_late[0][1][0]]
            + [g[2][0] for g in groups],
        )
        groups.append((scal, [got_face, got_e[1], got_l[1]], start, first))
    theirs = []
    runs = [((0, 0), (1, 1), 1, 2)]
    gains = [[r[5] for r in results], []]
    starts = [g[2] for g in groups]
    for group, (scal, operands, start, first) in enumerate(groups):
        send = weight_part(
            scal, runs, (False,), blocks, operands, [start[0]], None, gains[group],
            last if group else [starts[1][0]],
            held=(2,),
        )[0]
        last = [send]
        theirs.append(exchange(send, "tile", 1, T))
    halves = [[], []]
    for n, cut in enumerate(pieces):
        for group, (scal, operands, start, first) in enumerate(groups):
            give, keep = weight_part(
                scal, runs, (True,), blocks, operands, [start[1], theirs[group]],
                (sum(pieces[:n]), cut), [] if n else gains[group], last, held=(2,),
            )
            last = [keep]
            both = [keep, exchange(give, "dp", 1 << first, D)]
            for b in range(bits):
                if b in (group, first):
                    continue
                columns = both[0].shape[1] // 2
                mine = (me_d >> b) & 1
                keep = [lax.dynamic_slice_in_dim(p, mine * columns, columns, 1) for p in both]
                give = [lax.dynamic_slice_in_dim(p, (1 - mine) * columns, columns, 1) for p in both]
                both = [sum(keep), exchange(sum(give), "dp", 1 << b, D)]
            halves[group].append(both)
    placed = []
    for n in range(len(pieces)):
        parts = [*halves[0][n], *halves[1][n]]
        columns = 2 * parts[0].shape[1]
        outs = whole_call(
            functools.partial(block_kernel, blocks, 2),
            "row_blocks",
            chip.reshape(1),
            [struct(size + (8 if n == 0 else 0), columns, dtype=F32)] * blocks,
            parts,
            near=(True, True),
            deps=last if n else [returned],
        )
        got = [exchange(outs[o], "tile", 2 * o, T) for o in range(1, blocks)]
        (mine,) = whole_call(
            functools.partial(sum_kernel, factor),
            "block_sum",
            chip.reshape(1),
            [struct(*outs[0].shape, dtype=F32)],
            [outs[0], *got],
            near=(True, True),
        )
        last = [outs[0]]
        placed += [mine] + [exchange(mine, "dp", o, D) for o in range(1, D)]

    back_order = np.zeros((2, K, NLG), np.int32)
    for w in range(2):
        k, t, c, l = np.meshgrid(
            np.arange(K), np.arange(T), np.arange(chunks), np.arange(lines), indexing="ij"
        )
        back_order[w] = ((t * chunks + c) * 2 * RB + w * RB + l * K + k).reshape(K, NLG)
    edge_output, edge_grad = whole_call(
        lambda s, *refs: unpack_kernel(1, *refs),
        "unpack",
        chip.reshape(1),
        [struct(K * NLG, width)] * 2,
        [returned, jnp.asarray(back_order.reshape(-1, 1))],
        scratch=[pltpu.VMEM((chunks * packed, width), BF)],
    )
    qkv_grad, out_grad = whole_call(
        functools.partial(place_kernel, pieces, D),
        "place",
        me_d.astype(jnp.int32).reshape(1),
        [struct(size, 3 * width, dtype=F32), struct(size, width, dtype=F32)],
        placed,
        near=(True, False),
    )
    gain_sum = (placed[0] + placed[1])[size:, : width // 8].reshape(width)
    gain_grad = lax.dynamic_slice_in_dim(gain_sum, me_t * size, size)
    shape = edge_tokens.shape
    return (
        faces[0],
        edge_output.reshape(shape),
        faces[1],
        edge_grad.reshape(shape),
        qkv_grad,
        out_grad,
        gain_grad,
    )


def solution(mesh):
    return jax.shard_map(
        local,
        mesh=mesh,
        in_specs=(
            P("dp", "tile", None, None),
            P("dp", "tile", None, None),
            P("dp", "tile", None, None),
            P("dp", "tile", None, None),
            P(),
            P(),
            P(),
            P(),
            P(),
        ),
        out_specs=(
            P("dp", "tile", None, None),
            P("dp", "tile", None, None),
            P("dp", "tile", None, None),
            P("dp", "tile", None, None),
            P("tile", None),
            P("tile", None),
            P("tile"),
        ),
        check_vma=False,
    )
```

```python
import functools

import jax
import jax.numpy as jnp
import numpy as np
from jax import lax
from jax.experimental import pallas as pl
from jax.experimental.pallas import tpu as pltpu
from jax.sharding import PartitionSpec as P

HEADS = 16
BF = jnp.bfloat16
F32 = jnp.float32
VMEM_BYTES = 60 * 1024 * 1024
SMALL_BYTES = 28 * 1024 * 1024
WEIGHT_BYTES = 54 * 1024 * 1024


def nn(a, b):
    return lax.dot_general(a, b, (((1,), (0,)), ((), ())), preferred_element_type=F32)


def nt(a, b):
    return lax.dot_general(a, b, (((1,), (1,)), ((), ())), preferred_element_type=F32)


def tn(a, b):
    return lax.dot_general(a, b, (((0,), (0,)), ((), ())), preferred_element_type=F32)


def one_hot(index_ref, width):
    rows = index_ref.shape[0]
    columns = lax.broadcasted_iota(jnp.int32, (rows, width), 1)
    return jnp.where(columns == index_ref[...], 1.0, 0.0).astype(BF)


def pack_kernel(tok_ref, cot_ref, index_ref, *refs):
    both = refs[-1]
    rows = tok_ref.shape[0]
    both[:rows] = tok_ref[...]
    both[rows:] = cot_ref[...]
    take = index_ref.shape[0] // (len(refs) - 1)
    for c, out in enumerate(refs[:-1]):
        columns = lax.broadcasted_iota(jnp.int32, (take, 2 * rows), 1)
        picked = jnp.where(columns == index_ref[c * take : (c + 1) * take], 1.0, 0.0).astype(BF)
        out[...] = nn(picked, both[...]).astype(BF)


def unpack_kernel(chunks, *refs):
    backs, index_ref, out_tok, out_cot, both = refs[:chunks], refs[chunks], refs[-3], refs[-2], refs[-1]
    take = backs[0].shape[0]
    for c, back in enumerate(backs):
        both[c * take : (c + 1) * take] = back[...]
    rows = out_tok.shape[0]
    for w, out in enumerate((out_tok, out_cot)):
        columns = lax.broadcasted_iota(jnp.int32, (rows, chunks * take), 1)
        picked = jnp.where(columns == index_ref[w * rows : (w + 1) * rows], 1.0, 0.0).astype(BF)
        out[...] = nn(picked, both[...]).astype(BF)


def face_kernel(scal_ref, face_ref, fcot_ref, gain_ref, normed_ref, early_ref):
    hidden = face_ref[...].astype(F32)
    inverse = lax.rsqrt(jnp.mean(hidden * hidden, axis=-1, keepdims=True) + 1e-06)
    normed = (hidden * inverse * gain_ref[...]).astype(BF)
    normed_ref[...] = normed
    early_ref[...] = jnp.where(scal_ref[0] == 0, fcot_ref[...], normed)


def flips(line_ref, rotation_ref, base, lines):
    line = line_ref[:, 2:3]
    flip = jnp.zeros_like(line)
    for l in range(lines):
        turned = (rotation_ref[base + l] >= 2).astype(jnp.int32)
        flip = jnp.where(line == l, turned, flip)
    return jnp.where(flip != 0, line_ref[:, 1:2], line_ref[:, 0:1])


def turn_pair(rotation_ref, at):
    turn = rotation_ref[at]
    cosine = (turn == 0).astype(F32) - (turn == 2).astype(F32)
    sine = (turn == 1).astype(F32) - (turn == 3).astype(F32)
    return cosine, sine


def one_hot_rows(index, width):
    columns = lax.broadcasted_iota(jnp.int32, (index.shape[0], width), 1)
    return jnp.where(columns == index, 1.0, 0.0).astype(BF)


def edge_kernel(
    lines,
    scal_ref,
    rotation_ref,
    counts_ref,
    arrived_ref,
    index_ref,
    gain_ref,
    z_ref,
    g_ref,
    normed_ref,
    early_ref,
):
    half = z_ref.shape[1] // 2
    edges = z_ref.shape[0]
    edge_len = edges // lines
    base = scal_ref[0]
    index = flips(index_ref, rotation_ref, base, lines)
    picked = one_hot_rows(index, arrived_ref.shape[0])
    first = nn(picked, arrived_ref[:, :half])
    second = nn(picked, arrived_ref[:, half:])
    for l in range(lines):
        cosine, sine = turn_pair(rotation_ref, base + l)

        def turned(at):
            u, v = first[at : at + edge_len], second[at : at + edge_len]
            return jnp.concatenate([cosine * u - sine * v, sine * u + cosine * v], axis=1)

        rows = slice(l * edge_len, (l + 1) * edge_len)
        hidden = turned(l * edge_len)
        g = turned(edges + l * edge_len).astype(BF)
        z_ref[rows] = hidden.astype(BF)
        g_ref[rows] = g
        inverse = lax.rsqrt(jnp.mean(hidden * hidden, axis=-1, keepdims=True) + 1e-06)
        normed = (hidden * inverse * gain_ref[...]).astype(BF)
        normed_ref[rows] = normed
        early_ref[rows] = jnp.where(scal_ref[2] == 0, g, normed)


def layer_kernel(
    lines, first_chunk, drop, scal_ref, rotation_ref, counts_ref, face_ref, fcot_ref, *refs
):
    base = scal_ref[0]
    wqkv_hbm, wo_hbm = (refs[4:6]) if first_chunk else refs[5:7]
    wqkv_ref, wo_ref, in_sems, out_sems = refs[-4:]
    refs = refs[:-4]
    tile = 512

    def fetch(j):
        cols = pl.ds(j * tile if isinstance(j, int) else pl.multiple_of(j * tile, tile), tile)
        return pltpu.make_async_copy(wqkv_hbm.at[:, cols], wqkv_ref.at[:, cols], in_sems.at[j])

    tiles = wqkv_ref.shape[1] // tile
    fetch_out = pltpu.make_async_copy(wo_hbm, wo_ref, in_sems.at[tiles])
    for j in range(tiles):
        fetch(j).start()
    fetch_out.start()
    moves = []
    if first_chunk:
        arrived_ref, index_ref, normed_face_ref, gain_ref = refs[:4]
        refs = refs[6 + drop :]
        send_a, send_b = refs[4], refs[6]
        g_edge_ref, normed_edge_ref = refs[8:10]
        early_ref, z_edge_ref = refs[-2:]
        refs = (*refs[:8], *refs[10:-2])
        late_rows = refs[3].shape[0]
        edge_rows = z_edge_ref.shape[0]
        edge_kernel(
            lines,
            scal_ref,
            rotation_ref,
            counts_ref,
            arrived_ref,
            index_ref,
            gain_ref,
            z_edge_ref,
            g_edge_ref,
            normed_edge_ref,
            early_ref,
        )
        for n, (src, dst) in enumerate(((normed_edge_ref, send_a), (early_ref, send_b))):
            to = dst.at[pl.ds(late_rows, edge_rows)]
            moves.append(pltpu.make_async_copy(src, to, out_sems.at[4 + n]))
            moves[-1].start()
    else:
        z_edge_ref, g_edge_ref, normed_edge_ref = refs[:3]
        normed_face_ref, gain_ref = refs[3:5]
        back_index_ref, before_ref = refs[7:9]
        refs = refs[9 + drop :]
    (
        face_out,
        face_grad,
        back_ref,
        keep_a,
        send_a,
        keep_b,
        send_b,
        gain_part,
        z_s,
        g_s,
        norm_s,
        qkv_s,
        dm_s,
        mix_s,
        stk_s,
        dn_s,
        y_s,
        edge_s,
    ) = refs
    width = z_s.shape[1]
    half = width // 2
    face_len = face_ref.shape[2]
    edges = z_edge_ref.shape[0]
    edge_len = edges // lines
    length = face_len + edge_len
    faces = lines * face_len
    head_dim = width // HEADS
    scale = head_dim ** (-0.5)
    gain = gain_ref[...]

    for l in range(lines):
        z_s[l * face_len : (l + 1) * face_len] = face_ref[0, l]
        g_s[l * face_len : (l + 1) * face_len] = fcot_ref[0, l]
    z_s[faces:] = z_edge_ref[...]
    g_s[faces:] = g_edge_ref[...]
    norm_s[:faces] = normed_face_ref[...]
    norm_s[faces:] = normed_edge_ref[...]

    @pl.loop(0, tiles)
    def _(j):
        cols = pl.ds(pl.multiple_of(j * tile, tile), tile)
        fetch(j).wait()
        qkv_s[:, cols] = nn(norm_s[...], wqkv_ref[:, cols]).astype(BF)

    fetch_out.wait()

    @pl.loop(0, width // tile)
    def _(j):
        cols = pl.ds(pl.multiple_of(j * tile, tile), tile)
        dm_s[:, cols] = nt(g_s[...], wo_ref[cols, :]).astype(BF)

    pair = 2 * head_dim
    low = lax.broadcasted_iota(jnp.int32, (length, pair), 1) < head_dim
    key_row = lax.broadcasted_iota(jnp.int32, (length, length), 0)

    def split(x):
        zero = jnp.zeros_like(x)
        return jnp.concatenate([jnp.where(low, x, zero), jnp.where(low, zero, x)], axis=0)

    @pl.loop(0, lines)
    def _(l):
        top = pl.ds(pl.multiple_of(l * face_len, face_len), face_len)
        bottom = pl.ds(pl.multiple_of(faces + l * edge_len, edge_len), edge_len)
        live = key_row < counts_ref[base + l] + face_len

        def load(ref, at):
            return jnp.concatenate([ref[top, at : at + pair], ref[bottom, at : at + pair]], axis=0)

        def store(ref, at, value):
            ref[top, at : at + pair] = value[:face_len].astype(BF)
            ref[bottom, at : at + pair] = value[face_len:].astype(BF)

        for p in range(HEADS // 2):
            at = p * pair
            q = load(qkv_s, at)
            k2 = split(load(qkv_s, width + at))
            v2 = split(load(qkv_s, 2 * width + at))
            dm = load(dm_s, at)
            scores = nt(k2, q * jnp.asarray(scale, BF))
            d_probs = nt(v2, dm)
            probs_b, d_scores = [], []
            for h in range(2):
                part = slice(h * length, (h + 1) * length)
                s = jnp.where(live, scores[part], -1e30)
                e = jnp.exp(s - jnp.max(s, axis=0, keepdims=True))
                probs = e * (1.0 / jnp.sum(e, axis=0, keepdims=True))
                d = d_probs[part]
                inner = jnp.sum(probs * d, axis=0, keepdims=True)
                probs_b.append(probs.astype(BF))
                d_scores.append((probs * (d - inner)).astype(BF))
            pb = jnp.concatenate(probs_b, axis=0)
            ds = jnp.concatenate(d_scores, axis=0)
            store(mix_s, at, tn(pb, v2))
            dv = nn(pb, dm)
            store(stk_s, 2 * width + at, jnp.where(low, dv[:length], dv[length:]))
            store(stk_s, at, tn(ds, k2) * scale)
            dk = nn(ds, q)
            store(stk_s, width + at, jnp.where(low, dk[:length], dk[length:]) * scale)

    total_rows = z_s.shape[0]
    targets = (keep_a, send_a, keep_b, send_b)
    third = [stk_s.at[:, pl.ds(n * width, width)] for n in range(3)]
    sources = (third[0], third[1], third[2], mix_s)

    def ship(at, order):
        for n, src in enumerate(order):
            dst = targets[at + n].at[pl.ds(0, total_rows)]
            pltpu.make_async_copy(sources[src], dst, out_sems.at[at + n]).start()

    for at, bit in ((0, scal_ref[1]), (2, scal_ref[2])):

        @pl.when(bit == 0)
        def _(at=at):
            ship(at, (at, at + 1))

        @pl.when(bit != 0)
        def _(at=at):
            ship(at, (at + 1, at))

    @pl.loop(0, width // tile)
    def _(j):
        cols = pl.ds(pl.multiple_of(j * tile, tile), tile)
        y_s[:, cols] = (nn(mix_s[...], wo_ref[:, cols]) + z_s[:, cols].astype(F32)).astype(BF)
        dn_s[:, cols] = nt(stk_s[...], wqkv_ref[cols, :])

    gain_sum = jnp.zeros((1, width), F32)
    off = 0 if first_chunk else 2 * edges
    for i in range(2 * lines):
        size = face_len if i < lines else edge_len
        start = i * face_len if i < lines else faces + (i - lines) * edge_len
        at = slice(start, start + size)
        hidden = z_s[at].astype(F32)
        inverse = lax.rsqrt(jnp.mean(hidden * hidden, axis=-1, keepdims=True) + 1e-06)
        d_normed = dn_s[at]
        gain_sum = gain_sum + jnp.sum(d_normed * hidden * inverse, axis=0, keepdims=True)
        scaled = d_normed * gain
        mean = jnp.mean(scaled * hidden, axis=-1, keepdims=True)
        dz = inverse * scaled - hidden * (inverse * inverse * inverse * mean)
        dz = (g_s[at].astype(F32) + dz).astype(BF)
        if i < lines:
            face_out[0, i] = y_s[at]
            face_grad[0, i] = dz
        else:
            at = off + edges + start - faces
            edge_s[at : at + size] = dz
    edge_s[off : off + edges] = y_s[faces:]
    lanes = gain_part.shape[1]
    for i in range(width // lanes):
        gain_part[i : i + 1] = gain_sum[:, i * lanes : (i + 1) * lanes]
    for i in range(2 * lines):
        cosine, sine = turn_pair(rotation_ref, base + i % lines)
        rows = slice(off + i * edge_len, off + (i + 1) * edge_len)
        u, v = edge_s[rows, :half].astype(F32), edge_s[rows, half:].astype(F32)
        edge_s[rows, :half] = (cosine * u + sine * v).astype(BF)
        edge_s[rows, half:] = (cosine * v - sine * u).astype(BF)
    if first_chunk:
        back_ref[...] = edge_s[...]
    else:
        edge_s[:off] = before_ref[...]
        picked = one_hot_rows(
            flips(back_index_ref, rotation_ref, base - lines, 2 * lines), 4 * edges
        )
        back_ref[...] = nn(picked, edge_s[...]).astype(BF)

    for n, dst in enumerate(targets):
        pltpu.make_async_copy(sources[n], dst.at[pl.ds(0, total_rows)], out_sems.at[n]).wait()
    for move in moves:
        move.wait()


def weight_kernel(runs, parities, blocks, count, adds, gains, halved, scal_ref, *refs):
    operands = refs[:count]
    add_refs = refs[count : count + adds]
    gain_refs = refs[count + adds : count + adds + gains]
    outs = refs[count + adds + gains :]
    width = operands[-1].shape[1]
    part = width // 2
    size = part // blocks
    rows = len(parities) * part

    def pick(src):
        kept = []
        for own in parities:
            first = scal_ref[0] == (0 if own else 1)
            for b in range(blocks):
                left = src[:, 2 * b * size : (2 * b + 1) * size]
                right = src[:, (2 * b + 1) * size : (2 * b + 2) * size]
                kept.append(jnp.where(first, left, right))
        return jnp.concatenate(kept, axis=1)

    def run(swapped):
        early, late = [], []
        for faces, edges, chunk, late_at in runs:
            edge = operands[edges[swapped]]
            front = operands[late_at].shape[0] - edge.shape[0]
            early += [operands[faces[swapped]][chunk * front : (chunk + 1) * front], edge[...]]
            late.append(operands[late_at][...])
        early, late = jnp.concatenate(early, axis=0), jnp.concatenate(late, axis=0)
        lhs, rhs = (late, early) if swapped else (early, late)
        lhs = pick(lhs)
        if not halved:
            total = tn(lhs, rhs)
            for ref in add_refs:
                total = total + ref[:rows]
            for n, out in enumerate(outs):
                out[:part] = total[n * part : (n + 1) * part]
            return
        for half in range(2):
            mine = (scal_ref[2] if half else 1 - scal_ref[2]) == 0
            left = slice(halved[0], halved[0] + halved[1])
            right = slice(part + halved[0], part + halved[0] + halved[1])
            total = tn(lhs, jnp.where(mine, rhs[:, left], rhs[:, right]))
            for ref in add_refs:
                total = total + jnp.where(mine, ref[:rows, left], ref[:rows, right])
            outs[half][:rows] = total

    @pl.when(scal_ref[1] == 0)
    def _():
        run(0)

    @pl.when(scal_ref[1] != 0)
    def _():
        run(1)

    if gains:
        total = gain_refs[0][...]
        for ref in gain_refs[1:]:
            total = total + ref[...]
        lanes = total.shape[1]
        if halved:
            total = total + add_refs[-1][rows:, :lanes]
        for out in outs:
            if out.shape[0] > rows:
                for n in range(out.shape[1] // lanes):
                    out[rows:, n * lanes : (n + 1) * lanes] = total


def weight_part(
    scal, runs, parities, blocks, operands, adds, halved, gains, deps, held=()
):
    pieces_of = [o if isinstance(o, tuple) else (o, o.shape[0], 0) for o in operands]
    operands = [o for o, _, _ in pieces_of]
    width = operands[-1].shape[1]
    part = width // 2
    rows = len(parities) * part
    depth = len(runs) * pieces_of[runs[0][3]][1]
    extra = gains[0].shape[0] if gains else 0
    used = len(operands) + len(adds) + len(gains)

    def kernel(scal_ref, *refs):
        refs[-1][...] = jnp.zeros_like(refs[-1])
        refs = refs[:used] + refs[used + len(deps) : -1]
        weight_kernel(
            runs, parities, blocks, len(operands), len(adds), len(gains), halved, scal_ref, *refs
        )

    def spec(shape):
        return pl.BlockSpec(shape, lambda i, s: (0, 0))

    near = pl.BlockSpec(memory_space=pltpu.VMEM)
    if halved:
        shapes = [(rows + extra, halved[1])] * 2
    else:
        shapes = [(part + extra, width)] * len(parities)
    return pl.pallas_call(
        kernel,
        grid_spec=pltpu.PrefetchScalarGridSpec(
            num_scalar_prefetch=1,
            grid=(1,),
            in_specs=[
                near
                if n in held
                else pl.BlockSpec((size, width), lambda i, s, at=at: (at, 0))
                for n, (_, size, at) in enumerate(pieces_of)
            ]
            + [near] * len(adds)
            + [spec(g.shape) for g in gains]
            + [pl.BlockSpec(memory_space=pl.ANY)] * len(deps),
            out_specs=[near] * (len(shapes) + 1),
        ),
        out_shape=[jax.ShapeDtypeStruct(s, F32) for s in [*shapes, (8, 128)]],
        compiler_params=pltpu.CompilerParams(vmem_limit_bytes=SMALL_BYTES if len(runs) == 1 else WEIGHT_BYTES),
        cost_estimate=pl.CostEstimate(
            flops=1 << 33 if len(runs) > 1 else 1024, bytes_accessed=1024, transcendentals=0
        ),
        name="weight_part",
    )(scal, *operands, *adds, *gains, *deps)


def block_kernel(blocks, count, scal_ref, *refs):
    groups = (refs[:count], refs[count : 2 * count])
    outs = refs[2 * count :]
    columns = groups[0][0].shape[1]
    size = groups[1][0].shape[0] // blocks
    whole = blocks * size
    for o, out in enumerate(outs):
        at = pl.ds(pl.multiple_of((scal_ref[0] ^ o) * size, size), size)
        for n, parts in enumerate(groups):
            total = parts[0][at]
            for p in parts[1:]:
                total = total + p[at]
            out[:size, n * columns : (n + 1) * columns] = total
        if out.shape[0] > size:
            total = groups[0][0][whole:]
            for p in groups[0][1:]:
                total = total + p[whole:]
            out[size:, :columns] = total
            out[size:, columns:] = total


def sum_kernel(factor, scal_ref, *refs):
    total = refs[0][...]
    for ref in refs[1:-1]:
        total = total + ref[...]
    refs[-1][...] = total * factor


def place_kernel(pieces, devices, scal_ref, *refs):
    qkv_ref, out_ref = refs[-2], refs[-1]
    size, width = out_ref.shape
    bits = devices.bit_length() - 1
    for m, src in enumerate(refs[:-2]):
        n, o = m // devices, m % devices
        part = src.shape[1] // 2
        device = scal_ref[0] ^ o
        for group in range(2):
            value = (slice(0, size), slice(group * part, (group + 1) * part))
            rest = [b for b in range(bits) if b != group]
            at = ((device >> rest[0]) & 1) * (width // 2) + sum(pieces[:n])
            unit = pieces[n]
            for b in rest[1:]:
                unit = unit // 2
                at = at + ((device >> b) & 1) * unit
            which = (device >> group) & 1
            if group == 0:
                cols = pl.ds(pl.multiple_of(at + which * width, 128), part)
                qkv_ref[:, cols] = src[value]
            else:

                @pl.when(which == 0)
                def _(src=src, value=value, at=at, part=part):
                    cols = pl.ds(pl.multiple_of(at + 2 * width, 128), part)
                    qkv_ref[:, cols] = src[value]

                @pl.when(which != 0)
                def _(src=src, value=value, at=at, part=part):
                    out_ref[:, pl.ds(pl.multiple_of(at, 128), part)] = src[value]


def exchange(x, axis, bits, size):
    return lax.ppermute(x, axis, [(i, i ^ bits) for i in range(size)])


def whole_call(kernel, name, scal, out_shape, operands, deps=(), scratch=(), flops=0, limit=SMALL_BYTES, near=(False, False)):
    scal = scal if isinstance(scal, tuple) else (scal,)

    def body(*refs):
        used = len(scal) + len(operands)
        kernel(*refs[:used], *refs[used + len(deps) :])

    def spec(shape):
        return pl.BlockSpec(shape, lambda i, *s: (0,) * len(shape))

    vmem = pl.BlockSpec(memory_space=pltpu.VMEM)
    moved = sum(int(np.prod(o.shape)) * o.dtype.itemsize for o in [*operands, *out_shape])
    return pl.pallas_call(
        body,
        grid_spec=pltpu.PrefetchScalarGridSpec(
            num_scalar_prefetch=len(scal),
            grid=(1,),
            in_specs=[vmem if near[0] else spec(o.shape) for o in operands]
            + [pl.BlockSpec(memory_space=pl.ANY)] * len(deps),
            out_specs=[vmem if near[1] else spec(o.shape) for o in out_shape],
            scratch_shapes=list(scratch),
        ),
        out_shape=out_shape,
        compiler_params=pltpu.CompilerParams(vmem_limit_bytes=limit),
        cost_estimate=pl.CostEstimate(flops=1024, bytes_accessed=1024, transcendentals=0),
        name=name,
    )(*scal, *operands, *deps)


def local(
    face_tokens,
    edge_tokens,
    face_cotangent,
    edge_cotangent,
    rotation,
    counts,
    norm_gain,
    qkv_weight,
    out_weight,
):
    T = lax.axis_size("tile")
    D = lax.axis_size("dp")
    me_t = lax.axis_index("tile")
    me_d = lax.axis_index("dp")
    LD, FL, width = face_tokens.shape[1:]
    K = edge_tokens.shape[1]
    EL = K * T
    NLG = edge_tokens.shape[2]
    length = FL + EL
    chunks = 2
    lines = LD // chunks
    RB = lines * K
    packed = T * 2 * RB
    factor = float(D * T * LD * length) ** (-0.5)
    x_bit = (me_d % 2).astype(jnp.int32)
    y_bit = ((me_d // 2) % 2).astype(jnp.int32)
    gain = norm_gain.reshape(1, width)

    def struct(*shape, dtype=BF):
        return jax.ShapeDtypeStruct(shape, dtype)

    order = np.zeros((chunks, T, 2, lines, K), np.int32)
    for c in range(chunks):
        for w in range(2):
            t, l, k = np.meshgrid(np.arange(T), np.arange(lines), np.arange(K), indexing="ij")
            order[c, :, w] = w * K * NLG + k * NLG + t * LD + c * lines + l

    face_rows = face_tokens.reshape(LD * FL, width)
    face_cots = face_cotangent.reshape(LD * FL, width)
    face_normed, face_early = whole_call(
        face_kernel,
        "face_norm",
        y_bit.reshape(1),
        [struct(LD * FL, width)] * 2,
        [face_rows, face_cots, gain],
        limit=VMEM_BYTES,
    )
    sent = []
    for c in range(chunks):
        sent += whole_call(
            lambda s, *refs: pack_kernel(*refs),
            "pack",
            y_bit.reshape(1),
            [struct(packed, width)],
            [
                edge_tokens.reshape(K * NLG, width),
                edge_cotangent.reshape(K * NLG, width),
                jnp.asarray(order[c].reshape(-1, 1)),
            ],
            deps=[face_early] if c else [],
            scratch=[pltpu.VMEM((2 * K * NLG, width), BF)],
            limit=VMEM_BYTES,
        )
    arrived = [lax.all_to_all(s, "tile", split_axis=0, concat_axis=0, tiled=True) for s in sent]
    got_face_a = exchange(face_normed, "dp", 1, D)
    got_face_b = exchange(face_early, "dp", 2, D)

    edges = lines * EL
    l, p = np.meshgrid(np.arange(lines), np.arange(EL), indexing="ij")
    table = []
    for pos in (p, EL - 1 - p):
        row = (pos // K) * (2 * RB) + l * K + pos % K
        table.append(np.stack([row, row + RB]))
    table.append(np.stack([l, l]))
    index = jnp.asarray(np.stack(table, axis=-1).reshape(-1, 3).astype(np.int32))
    t, c, w, l, k = np.meshgrid(
        np.arange(T),
        np.arange(chunks),
        np.arange(2),
        np.arange(lines),
        np.arange(K),
        indexing="ij",
    )
    at = 2 * c * edges + w * edges + l * EL
    pos = t * K + k
    table = [at + pos, at + EL - 1 - pos, c * lines + l]
    back_index = jnp.asarray(np.stack(table, axis=-1).reshape(-1, 3).astype(np.int32))
    edge_parts, results, got_edges, got_late = [], [], [], []
    faces = None
    for c in range(chunks):
        base = (me_t * LD + c * lines).astype(jnp.int32)
        scal = (jnp.stack([base, x_bit, y_bit]), rotation, counts)
        rows_all = lines * length
        row_shape = (rows_all, width)
        face_spec = pl.BlockSpec((1, lines, FL, width), lambda i, *s, c=c: (0, c, 0, 0))
        normed_spec = pl.BlockSpec((lines * FL, width), lambda i, *s, c=c: (c, 0))

        def full(shape):
            return pl.BlockSpec(shape, lambda i, *s: (0,) * len(shape))

        if c == 0:
            operands = [face_tokens, face_cotangent, arrived[c], index]
            operands += [face_normed, gain, qkv_weight, out_weight]
            tail = []
        else:
            z_edge, g_edge, normed_edge, early_edge = whole_call(
                functools.partial(edge_kernel, lines),
                "edge_norm",
                scal,
                [struct(edges, width)] * 4,
                [arrived[c], index, gain],
                deps=[results[0][5]],
                limit=VMEM_BYTES,
            )
            operands = [face_tokens, face_cotangent, z_edge, g_edge, normed_edge]
            operands += [face_normed, gain, qkv_weight, out_weight, back_index, results[0][0]]
            tail = [*faces, got_face_a, got_face_b]
        in_specs = [
            face_spec
            if n < 2
            else normed_spec
            if o is face_normed
            else pl.BlockSpec(memory_space=pl.ANY)
            if o is qkv_weight or o is out_weight
            else full(o.shape)
            for n, o in enumerate(operands)
        ]
        in_specs += [pl.BlockSpec(memory_space=pl.ANY)] * len(tail)
        aliases = {} if c == 0 else {3 + len(operands): 0, 4 + len(operands): 1}
        operands += tail
        back_rows = 2 * edges if c == 0 else packed * chunks
        edge_outs = [(edges, width)] * 2 if c == 0 else []
        send_shape = (rows_all + (edges if c == 0 else 0), width)
        outs = pl.pallas_call(
            functools.partial(layer_kernel, lines, c == 0, len(tail)),
            grid_spec=pltpu.PrefetchScalarGridSpec(
                num_scalar_prefetch=3,
                grid=(1,),
                in_specs=in_specs,
                out_specs=[face_spec, face_spec, full((back_rows, width))]
                + [pl.BlockSpec(memory_space=pl.ANY)] * 4
                + [full((8, width // 8))]
                + [full(e) for e in edge_outs],
                scratch_shapes=[
                    pltpu.VMEM(row_shape, BF),
                    pltpu.VMEM(row_shape, BF),
                    pltpu.VMEM(row_shape, BF),
                    pltpu.VMEM((rows_all, 3 * width), BF),
                    pltpu.VMEM(row_shape, BF),
                    pltpu.VMEM(row_shape, BF),
                    pltpu.VMEM((rows_all, 3 * width), BF),
                    pltpu.VMEM(row_shape, F32),
                    pltpu.VMEM(row_shape, BF),
                    pltpu.VMEM((2 * edges * (c + 1), width), BF),
                ]
                + ([pltpu.VMEM((edges, width), BF)] * 2 if c == 0 else [])
                + [
                    pltpu.VMEM(qkv_weight.shape, BF),
                    pltpu.VMEM(out_weight.shape, BF),
                    pltpu.SemaphoreType.DMA((3 * width // 512 + 1,)),
                    pltpu.SemaphoreType.DMA((6,)),
                ],
            ),
            out_shape=[struct(*face_tokens.shape)] * 2
            + [struct(back_rows, width)]
            + [struct(*row_shape), struct(*send_shape)] * 2
            + [struct(8, width // 8, dtype=F32)]
            + [struct(*e) for e in edge_outs],
            input_output_aliases=aliases,
            compiler_params=pltpu.CompilerParams(vmem_limit_bytes=VMEM_BYTES),
            cost_estimate=pl.CostEstimate(flops=1 << 35, bytes_accessed=1 << 20, transcendentals=0),
            name="layer",
        )(*scal, *operands)
        faces = outs[:2]
        results.append(outs[2:])
        late_a, late_b = exchange(outs[4], "dp", 1, D), exchange(outs[6], "dp", 2, D)
        if c == 0:
            g_edge, normed_edge = outs[8:]
            edges_a, edges_b = (late_a, edges, rows_all // edges), (late_b, edges, rows_all // edges)
            late_a, late_b = (late_a, rows_all, 0), (late_b, rows_all, 0)
        else:
            edges_a = exchange(normed_edge, "dp", 1, D)
            edges_b = exchange(early_edge, "dp", 2, D)
        edge_parts.append((normed_edge, g_edge))
        got_edges.append((edges_a, edges_b))
        got_late.append((late_a, late_b))
    returned = lax.all_to_all(results[1][0], "tile", split_axis=0, concat_axis=0, tiled=True)

    blocks = T // 2
    chip = (me_t // 2).astype(jnp.int32)
    core = (me_t % 2).astype(jnp.int32)
    quarter = width // 8
    pieces = (2 * quarter, 2 * quarter)
    size = width // T
    bits = D.bit_length() - 1
    groups = []
    for group in range(2):
        first = [b for b in range(bits) if b != group][0]
        swap = y_bit if group else jnp.zeros_like(y_bit)
        scal = jnp.stack([core, swap, ((me_d >> first) & 1).astype(jnp.int32)])
        late = [r[1 + 2 * group] for r in results]
        got_face = (got_face_a, got_face_b)[group]
        normed_e, g_e = [e[0] for e in edge_parts], [e[1] for e in edge_parts]
        got_e = [e[group] for e in got_edges]
        got_l = [e[group] for e in got_late]
        operands = [face_normed, face_cots, *normed_e, *g_e, got_face, got_e[0], late[0], late[1], got_l[0]]
        runs = [((0, 1), (2, 4), 0, 8), ((0, 1), (3, 5), 1, 9), ((6, 6), (7, 7), 0, 10)]
        start = weight_part(
            scal, runs, (False, True), blocks, operands, [], None, [],
            [*got_edges[1], got_late[0][0][0], got_late[0][1][0]]
            + [g[2][-1] for g in groups],
        )
        groups.append((scal, [got_face, got_e[1], got_l[1]], start, first))
    theirs = []
    runs = [((0, 0), (1, 1), 1, 2)]
    gains = [[r[5] for r in results], []]
    starts = [g[2] for g in groups]
    for group, (scal, operands, start, first) in enumerate(groups):
        send, token = weight_part(
            scal, runs, (False,), blocks, operands, [start[0]], None, gains[group],
            last if group else [starts[1][-1]],
            held=(2,),
        )
        last = [token]
        theirs.append(exchange(send, "tile", 1, T))
    halves = [[], []]
    for n, cut in enumerate(pieces):
        for group, (scal, operands, start, first) in enumerate(groups):
            give, keep, token = weight_part(
                scal, runs, (True,), blocks, operands, [start[1], theirs[group]],
                (sum(pieces[:n]), cut), [] if n else gains[group], last, held=(2,),
            )
            last = [token]
            both = [keep, exchange(give, "dp", 1 << first, D)]
            for b in range(bits):
                if b in (group, first):
                    continue
                columns = both[0].shape[1] // 2
                mine = (me_d >> b) & 1
                keep = [lax.dynamic_slice_in_dim(p, mine * columns, columns, 1) for p in both]
                give = [lax.dynamic_slice_in_dim(p, (1 - mine) * columns, columns, 1) for p in both]
                both = [sum(keep), exchange(sum(give), "dp", 1 << b, D)]
            halves[group].append(both)
    placed = []
    for n in range(len(pieces)):
        parts = [*halves[0][n], *halves[1][n]]
        columns = 2 * parts[0].shape[1]
        outs = whole_call(
            functools.partial(block_kernel, blocks, 2),
            "row_blocks",
            chip.reshape(1),
            [struct(size + (8 if n == 0 else 0), columns, dtype=F32)] * blocks,
            parts,
            near=(True, True),
            deps=last if n else [returned],
        )
        got = [exchange(outs[o], "tile", 2 * o, T) for o in range(1, blocks)]
        (mine,) = whole_call(
            functools.partial(sum_kernel, factor),
            "block_sum",
            chip.reshape(1),
            [struct(*outs[0].shape, dtype=F32)],
            [outs[0], *got],
            near=(True, True),
        )
        last = [outs[0]]
        placed += [mine] + [exchange(mine, "dp", o, D) for o in range(1, D)]

    back_order = np.zeros((2, K, NLG), np.int32)
    for w in range(2):
        k, t, c, l = np.meshgrid(
            np.arange(K), np.arange(T), np.arange(chunks), np.arange(lines), indexing="ij"
        )
        back_order[w] = ((t * chunks + c) * 2 * RB + w * RB + l * K + k).reshape(K, NLG)
    edge_output, edge_grad = whole_call(
        lambda s, *refs: unpack_kernel(1, *refs),
        "unpack",
        chip.reshape(1),
        [struct(K * NLG, width)] * 2,
        [returned, jnp.asarray(back_order.reshape(-1, 1))],
        scratch=[pltpu.VMEM((chunks * packed, width), BF)],
    )
    qkv_grad, out_grad = whole_call(
        functools.partial(place_kernel, pieces, D),
        "place",
        me_d.astype(jnp.int32).reshape(1),
        [struct(size, 3 * width, dtype=F32), struct(size, width, dtype=F32)],
        placed,
        near=(True, False),
    )
    gain_sum = (placed[0] + placed[1])[size:, : width // 8].reshape(width)
    gain_grad = lax.dynamic_slice_in_dim(gain_sum, me_t * size, size)
    shape = edge_tokens.shape
    return (
        faces[0],
        edge_output.reshape(shape),
        faces[1],
        edge_grad.reshape(shape),
        qkv_grad,
        out_grad,
        gain_grad,
    )


def solution(mesh):
    return jax.shard_map(
        local,
        mesh=mesh,
        in_specs=(
            P("dp", "tile", None, None),
            P("dp", "tile", None, None),
            P("dp", "tile", None, None),
            P("dp", "tile", None, None),
            P(),
            P(),
            P(),
            P(),
            P(),
        ),
        out_specs=(
            P("dp", "tile", None, None),
            P("dp", "tile", None, None),
            P("dp", "tile", None, None),
            P("dp", "tile", None, None),
            P("tile", None),
            P("tile", None),
            P("tile"),
        ),
        check_vma=False,
    )
```

```python
import functools

import jax
import jax.numpy as jnp
import numpy as np
from jax import lax
from jax.experimental import pallas as pl
from jax.experimental.pallas import tpu as pltpu
from jax.sharding import PartitionSpec as P

HEADS = 16
BF = jnp.bfloat16
F32 = jnp.float32
VMEM_BYTES = 60 * 1024 * 1024
SMALL_BYTES = 28 * 1024 * 1024
WEIGHT_BYTES = 54 * 1024 * 1024


def nn(a, b):
    return lax.dot_general(a, b, (((1,), (0,)), ((), ())), preferred_element_type=F32)


def nt(a, b):
    return lax.dot_general(a, b, (((1,), (1,)), ((), ())), preferred_element_type=F32)


def tn(a, b):
    return lax.dot_general(a, b, (((0,), (0,)), ((), ())), preferred_element_type=F32)


def one_hot(index_ref, width):
    rows = index_ref.shape[0]
    columns = lax.broadcasted_iota(jnp.int32, (rows, width), 1)
    return jnp.where(columns == index_ref[...], 1.0, 0.0).astype(BF)


def pack_kernel(tok_ref, cot_ref, index_ref, *refs):
    both = refs[-1]
    rows = tok_ref.shape[0]
    both[:rows] = tok_ref[...]
    both[rows:] = cot_ref[...]
    take = index_ref.shape[0] // (len(refs) - 1)
    for c, out in enumerate(refs[:-1]):
        columns = lax.broadcasted_iota(jnp.int32, (take, 2 * rows), 1)
        picked = jnp.where(columns == index_ref[c * take : (c + 1) * take], 1.0, 0.0).astype(BF)
        out[...] = nn(picked, both[...]).astype(BF)


def unpack_kernel(chunks, *refs):
    backs, index_ref, out_tok, out_cot, both = refs[:chunks], refs[chunks], refs[-3], refs[-2], refs[-1]
    take = backs[0].shape[0]
    for c, back in enumerate(backs):
        both[c * take : (c + 1) * take] = back[...]
    rows = out_tok.shape[0]
    for w, out in enumerate((out_tok, out_cot)):
        columns = lax.broadcasted_iota(jnp.int32, (rows, chunks * take), 1)
        picked = jnp.where(columns == index_ref[w * rows : (w + 1) * rows], 1.0, 0.0).astype(BF)
        out[...] = nn(picked, both[...]).astype(BF)


def face_kernel(scal_ref, face_ref, fcot_ref, gain_ref, normed_ref, early_ref):
    hidden = face_ref[...].astype(F32)
    inverse = lax.rsqrt(jnp.mean(hidden * hidden, axis=-1, keepdims=True) + 1e-06)
    normed = (hidden * inverse * gain_ref[...]).astype(BF)
    normed_ref[...] = normed
    early_ref[...] = jnp.where(scal_ref[0] == 0, fcot_ref[...], normed)


def flips(line_ref, rotation_ref, base, lines):
    line = line_ref[:, 2:3]
    flip = jnp.zeros_like(line)
    for l in range(lines):
        turned = (rotation_ref[base + l] >= 2).astype(jnp.int32)
        flip = jnp.where(line == l, turned, flip)
    return jnp.where(flip != 0, line_ref[:, 1:2], line_ref[:, 0:1])


def turn_pair(rotation_ref, at):
    turn = rotation_ref[at]
    cosine = (turn == 0).astype(F32) - (turn == 2).astype(F32)
    sine = (turn == 1).astype(F32) - (turn == 3).astype(F32)
    return cosine, sine


def one_hot_rows(index, width):
    columns = lax.broadcasted_iota(jnp.int32, (index.shape[0], width), 1)
    return jnp.where(columns == index, 1.0, 0.0).astype(BF)


def edge_kernel(
    lines,
    scal_ref,
    rotation_ref,
    counts_ref,
    arrived_ref,
    index_ref,
    gain_ref,
    z_ref,
    g_ref,
    normed_ref,
    early_ref,
):
    half = z_ref.shape[1] // 2
    edges = z_ref.shape[0]
    edge_len = edges // lines
    base = scal_ref[0]
    index = flips(index_ref, rotation_ref, base, lines)
    picked = one_hot_rows(index, arrived_ref.shape[0])
    first = nn(picked, arrived_ref[:, :half])
    second = nn(picked, arrived_ref[:, half:])
    for l in range(lines):
        cosine, sine = turn_pair(rotation_ref, base + l)

        def turned(at):
            u, v = first[at : at + edge_len], second[at : at + edge_len]
            return jnp.concatenate([cosine * u - sine * v, sine * u + cosine * v], axis=1)

        rows = slice(l * edge_len, (l + 1) * edge_len)
        hidden = turned(l * edge_len)
        g = turned(edges + l * edge_len).astype(BF)
        z_ref[rows] = hidden.astype(BF)
        g_ref[rows] = g
        inverse = lax.rsqrt(jnp.mean(hidden * hidden, axis=-1, keepdims=True) + 1e-06)
        normed = (hidden * inverse * gain_ref[...]).astype(BF)
        normed_ref[rows] = normed
        early_ref[rows] = jnp.where(scal_ref[2] == 0, g, normed)


def layer_kernel(
    lines, first_chunk, drop, scal_ref, rotation_ref, counts_ref, face_ref, fcot_ref, *refs
):
    base = scal_ref[0]
    wqkv_hbm, wo_hbm = (refs[4:6]) if first_chunk else refs[5:7]
    wqkv_ref, wo_ref, in_sems, out_sems = refs[-4:]
    refs = refs[:-4]
    tile = 512

    def fetch(j):
        cols = pl.ds(j * tile if isinstance(j, int) else pl.multiple_of(j * tile, tile), tile)
        return pltpu.make_async_copy(wqkv_hbm.at[:, cols], wqkv_ref.at[:, cols], in_sems.at[j])

    tiles = wqkv_ref.shape[1] // tile
    fetch_out = pltpu.make_async_copy(wo_hbm, wo_ref, in_sems.at[tiles])
    for j in range(tiles):
        fetch(j).start()
    fetch_out.start()
    moves = []
    if first_chunk:
        arrived_ref, index_ref, normed_face_ref, gain_ref = refs[:4]
        refs = refs[6 + drop :]
        send_a, send_b = refs[4], refs[6]
        g_edge_ref, normed_edge_ref = refs[8:10]
        early_ref, z_edge_ref = refs[-2:]
        refs = (*refs[:8], *refs[10:-2])
        late_rows = refs[3].shape[0]
        edge_rows = z_edge_ref.shape[0]
        edge_kernel(
            lines,
            scal_ref,
            rotation_ref,
            counts_ref,
            arrived_ref,
            index_ref,
            gain_ref,
            z_edge_ref,
            g_edge_ref,
            normed_edge_ref,
            early_ref,
        )
        for n, (src, dst) in enumerate(((normed_edge_ref, send_a), (early_ref, send_b))):
            to = dst.at[pl.ds(late_rows, edge_rows)]
            moves.append(pltpu.make_async_copy(src, to, out_sems.at[4 + n]))
            moves[-1].start()
    else:
        z_edge_ref, g_edge_ref, normed_edge_ref = refs[:3]
        normed_face_ref, gain_ref = refs[3:5]
        back_index_ref, before_ref = refs[7:9]
        refs = refs[9 + drop :]
    (
        face_out,
        face_grad,
        back_ref,
        keep_a,
        send_a,
        keep_b,
        send_b,
        gain_part,
        z_s,
        g_s,
        norm_s,
        qkv_s,
        dm_s,
        mix_s,
        stk_s,
        dn_s,
        y_s,
        edge_s,
    ) = refs
    width = z_s.shape[1]
    half = width // 2
    face_len = face_ref.shape[2]
    edges = z_edge_ref.shape[0]
    edge_len = edges // lines
    length = face_len + edge_len
    faces = lines * face_len
    head_dim = width // HEADS
    scale = head_dim ** (-0.5)
    gain = gain_ref[...]

    for l in range(lines):
        z_s[l * face_len : (l + 1) * face_len] = face_ref[0, l]
        g_s[l * face_len : (l + 1) * face_len] = fcot_ref[0, l]
    z_s[faces:] = z_edge_ref[...]
    g_s[faces:] = g_edge_ref[...]
    norm_s[:faces] = normed_face_ref[...]
    norm_s[faces:] = normed_edge_ref[...]

    @pl.loop(0, tiles)
    def _(j):
        cols = pl.ds(pl.multiple_of(j * tile, tile), tile)
        fetch(j).wait()
        qkv_s[:, cols] = nn(norm_s[...], wqkv_ref[:, cols]).astype(BF)

    fetch_out.wait()

    @pl.loop(0, width // tile)
    def _(j):
        cols = pl.ds(pl.multiple_of(j * tile, tile), tile)
        dm_s[:, cols] = nt(g_s[...], wo_ref[cols, :]).astype(BF)

    pair = 2 * head_dim
    low = lax.broadcasted_iota(jnp.int32, (length, pair), 1) < head_dim
    key_row = lax.broadcasted_iota(jnp.int32, (length, length), 0)

    def split(x):
        zero = jnp.zeros_like(x)
        return jnp.concatenate([jnp.where(low, x, zero), jnp.where(low, zero, x)], axis=0)

    @pl.loop(0, lines, unroll=True)
    def _(l):
        top = pl.ds(pl.multiple_of(l * face_len, face_len), face_len)
        bottom = pl.ds(pl.multiple_of(faces + l * edge_len, edge_len), edge_len)
        live = key_row < counts_ref[base + l] + face_len

        def load(ref, at):
            return jnp.concatenate([ref[top, at : at + pair], ref[bottom, at : at + pair]], axis=0)

        def store(ref, at, value):
            ref[top, at : at + pair] = value[:face_len].astype(BF)
            ref[bottom, at : at + pair] = value[face_len:].astype(BF)

        for p in range(HEADS // 2):
            at = p * pair
            q = load(qkv_s, at)
            k2 = split(load(qkv_s, width + at))
            v2 = split(load(qkv_s, 2 * width + at))
            dm = load(dm_s, at)
            scores = nt(k2, q * jnp.asarray(scale, BF))
            d_probs = nt(v2, dm)
            probs_b, d_scores = [], []
            for h in range(2):
                part = slice(h * length, (h + 1) * length)
                s = jnp.where(live, scores[part], -1e30)
                e = jnp.exp(s - jnp.max(s, axis=0, keepdims=True))
                probs = e * (1.0 / jnp.sum(e, axis=0, keepdims=True))
                d = d_probs[part]
                inner = jnp.sum(probs * d, axis=0, keepdims=True)
                probs_b.append(probs.astype(BF))
                d_scores.append((probs * (d - inner)).astype(BF))
            pb = jnp.concatenate(probs_b, axis=0)
            ds = jnp.concatenate(d_scores, axis=0)
            store(mix_s, at, tn(pb, v2))
            dv = nn(pb, dm)
            store(stk_s, 2 * width + at, jnp.where(low, dv[:length], dv[length:]))
            store(stk_s, at, tn(ds, k2) * scale)
            dk = nn(ds, q)
            store(stk_s, width + at, jnp.where(low, dk[:length], dk[length:]) * scale)

    total_rows = z_s.shape[0]
    targets = (keep_a, send_a, keep_b, send_b)
    third = [stk_s.at[:, pl.ds(n * width, width)] for n in range(3)]
    sources = (third[0], third[1], third[2], mix_s)

    def ship(at, order):
        for n, src in enumerate(order):
            dst = targets[at + n].at[pl.ds(0, total_rows)]
            pltpu.make_async_copy(sources[src], dst, out_sems.at[at + n]).start()

    for at, bit in ((0, scal_ref[1]), (2, scal_ref[2])):

        @pl.when(bit == 0)
        def _(at=at):
            ship(at, (at, at + 1))

        @pl.when(bit != 0)
        def _(at=at):
            ship(at, (at + 1, at))

    @pl.loop(0, width // tile)
    def _(j):
        cols = pl.ds(pl.multiple_of(j * tile, tile), tile)
        y_s[:, cols] = (nn(mix_s[...], wo_ref[:, cols]) + z_s[:, cols].astype(F32)).astype(BF)
        dn_s[:, cols] = nt(stk_s[...], wqkv_ref[cols, :])

    gain_sum = jnp.zeros((1, width), F32)
    off = 0 if first_chunk else 2 * edges
    for i in range(2 * lines):
        size = face_len if i < lines else edge_len
        start = i * face_len if i < lines else faces + (i - lines) * edge_len
        at = slice(start, start + size)
        hidden = z_s[at].astype(F32)
        inverse = lax.rsqrt(jnp.mean(hidden * hidden, axis=-1, keepdims=True) + 1e-06)
        d_normed = dn_s[at]
        gain_sum = gain_sum + jnp.sum(d_normed * hidden * inverse, axis=0, keepdims=True)
        scaled = d_normed * gain
        mean = jnp.mean(scaled * hidden, axis=-1, keepdims=True)
        dz = inverse * scaled - hidden * (inverse * inverse * inverse * mean)
        dz = (g_s[at].astype(F32) + dz).astype(BF)
        if i < lines:
            face_out[0, i] = y_s[at]
            face_grad[0, i] = dz
        else:
            at = off + edges + start - faces
            edge_s[at : at + size] = dz
    edge_s[off : off + edges] = y_s[faces:]
    lanes = gain_part.shape[1]
    for i in range(width // lanes):
        gain_part[i : i + 1] = gain_sum[:, i * lanes : (i + 1) * lanes]
    for i in range(2 * lines):
        cosine, sine = turn_pair(rotation_ref, base + i % lines)
        rows = slice(off + i * edge_len, off + (i + 1) * edge_len)
        u, v = edge_s[rows, :half].astype(F32), edge_s[rows, half:].astype(F32)
        edge_s[rows, :half] = (cosine * u + sine * v).astype(BF)
        edge_s[rows, half:] = (cosine * v - sine * u).astype(BF)
    if first_chunk:
        back_ref[...] = edge_s[...]
    else:
        edge_s[:off] = before_ref[...]
        picked = one_hot_rows(
            flips(back_index_ref, rotation_ref, base - lines, 2 * lines), 4 * edges
        )
        back_ref[...] = nn(picked, edge_s[...]).astype(BF)

    for n, dst in enumerate(targets):
        pltpu.make_async_copy(sources[n], dst.at[pl.ds(0, total_rows)], out_sems.at[n]).wait()
    for move in moves:
        move.wait()


def weight_kernel(runs, parities, blocks, count, adds, gains, halved, scal_ref, *refs):
    operands = refs[:count]
    add_refs = refs[count : count + adds]
    gain_refs = refs[count + adds : count + adds + gains]
    outs = refs[count + adds + gains :]
    width = operands[-1].shape[1]
    part = width // 2
    size = part // blocks
    rows = len(parities) * part

    def pick(src):
        kept = []
        for own in parities:
            first = scal_ref[0] == (0 if own else 1)
            for b in range(blocks):
                left = src[:, 2 * b * size : (2 * b + 1) * size]
                right = src[:, (2 * b + 1) * size : (2 * b + 2) * size]
                kept.append(jnp.where(first, left, right))
        return jnp.concatenate(kept, axis=1)

    def run(swapped):
        early, late = [], []
        for faces, edges, chunk, late_at in runs:
            edge = operands[edges[swapped]]
            front = operands[late_at].shape[0] - edge.shape[0]
            early += [operands[faces[swapped]][chunk * front : (chunk + 1) * front], edge[...]]
            late.append(operands[late_at][...])
        early, late = jnp.concatenate(early, axis=0), jnp.concatenate(late, axis=0)
        lhs, rhs = (late, early) if swapped else (early, late)
        lhs = pick(lhs)
        if not halved:
            total = tn(lhs, rhs)
            for ref in add_refs:
                total = total + ref[:rows]
            for n, out in enumerate(outs):
                out[:part] = total[n * part : (n + 1) * part]
            return
        for half in range(2):
            mine = (scal_ref[2] if half else 1 - scal_ref[2]) == 0
            left = slice(halved[0], halved[0] + halved[1])
            right = slice(part + halved[0], part + halved[0] + halved[1])
            total = tn(lhs, jnp.where(mine, rhs[:, left], rhs[:, right]))
            for ref in add_refs:
                total = total + jnp.where(mine, ref[:rows, left], ref[:rows, right])
            outs[half][:rows] = total

    @pl.when(scal_ref[1] == 0)
    def _():
        run(0)

    @pl.when(scal_ref[1] != 0)
    def _():
        run(1)

    if gains:
        total = gain_refs[0][...]
        for ref in gain_refs[1:]:
            total = total + ref[...]
        lanes = total.shape[1]
        if halved:
            total = total + add_refs[-1][rows:, :lanes]
        for out in outs:
            if out.shape[0] > rows:
                for n in range(out.shape[1] // lanes):
                    out[rows:, n * lanes : (n + 1) * lanes] = total


def weight_part(
    scal, runs, parities, blocks, operands, adds, halved, gains, deps, held=()
):
    pieces_of = [o if isinstance(o, tuple) else (o, o.shape[0], 0) for o in operands]
    operands = [o for o, _, _ in pieces_of]
    width = operands[-1].shape[1]
    part = width // 2
    rows = len(parities) * part
    depth = len(runs) * pieces_of[runs[0][3]][1]
    extra = gains[0].shape[0] if gains else 0
    used = len(operands) + len(adds) + len(gains)

    def kernel(scal_ref, *refs):
        refs[-1][...] = jnp.zeros_like(refs[-1])
        refs = refs[:used] + refs[used + len(deps) : -1]
        weight_kernel(
            runs, parities, blocks, len(operands), len(adds), len(gains), halved, scal_ref, *refs
        )

    def spec(shape):
        return pl.BlockSpec(shape, lambda i, s: (0, 0))

    near = pl.BlockSpec(memory_space=pltpu.VMEM)
    if halved:
        shapes = [(rows + extra, halved[1])] * 2
    else:
        shapes = [(part + extra, width)] * len(parities)
    return pl.pallas_call(
        kernel,
        grid_spec=pltpu.PrefetchScalarGridSpec(
            num_scalar_prefetch=1,
            grid=(1,),
            in_specs=[
                near
                if n in held
                else pl.BlockSpec((size, width), lambda i, s, at=at: (at, 0))
                for n, (_, size, at) in enumerate(pieces_of)
            ]
            + [near] * len(adds)
            + [spec(g.shape) for g in gains]
            + [pl.BlockSpec(memory_space=pl.ANY)] * len(deps),
            out_specs=[near] * (len(shapes) + 1),
        ),
        out_shape=[jax.ShapeDtypeStruct(s, F32) for s in [*shapes, (8, 128)]],
        compiler_params=pltpu.CompilerParams(vmem_limit_bytes=SMALL_BYTES if len(runs) == 1 else WEIGHT_BYTES),
        cost_estimate=pl.CostEstimate(
            flops=1 << 33 if len(runs) > 1 else 1024, bytes_accessed=1024, transcendentals=0
        ),
        name="weight_part",
    )(scal, *operands, *adds, *gains, *deps)


def block_kernel(blocks, count, scal_ref, *refs):
    groups = (refs[:count], refs[count : 2 * count])
    outs = refs[2 * count :]
    columns = groups[0][0].shape[1]
    size = groups[1][0].shape[0] // blocks
    whole = blocks * size
    for o, out in enumerate(outs):
        at = pl.ds(pl.multiple_of((scal_ref[0] ^ o) * size, size), size)
        for n, parts in enumerate(groups):
            total = parts[0][at]
            for p in parts[1:]:
                total = total + p[at]
            out[:size, n * columns : (n + 1) * columns] = total
        if out.shape[0] > size:
            total = groups[0][0][whole:]
            for p in groups[0][1:]:
                total = total + p[whole:]
            out[size:, :columns] = total
            out[size:, columns:] = total


def sum_kernel(factor, scal_ref, *refs):
    total = refs[0][...]
    for ref in refs[1:-1]:
        total = total + ref[...]
    refs[-1][...] = total * factor


def place_kernel(pieces, devices, scal_ref, *refs):
    qkv_ref, out_ref = refs[-2], refs[-1]
    size, width = out_ref.shape
    bits = devices.bit_length() - 1
    for m, src in enumerate(refs[:-2]):
        n, o = m // devices, m % devices
        part = src.shape[1] // 2
        device = scal_ref[0] ^ o
        for group in range(2):
            value = (slice(0, size), slice(group * part, (group + 1) * part))
            rest = [b for b in range(bits) if b != group]
            at = ((device >> rest[0]) & 1) * (width // 2) + sum(pieces[:n])
            unit = pieces[n]
            for b in rest[1:]:
                unit = unit // 2
                at = at + ((device >> b) & 1) * unit
            which = (device >> group) & 1
            if group == 0:
                cols = pl.ds(pl.multiple_of(at + which * width, 128), part)
                qkv_ref[:, cols] = src[value]
            else:

                @pl.when(which == 0)
                def _(src=src, value=value, at=at, part=part):
                    cols = pl.ds(pl.multiple_of(at + 2 * width, 128), part)
                    qkv_ref[:, cols] = src[value]

                @pl.when(which != 0)
                def _(src=src, value=value, at=at, part=part):
                    out_ref[:, pl.ds(pl.multiple_of(at, 128), part)] = src[value]


def exchange(x, axis, bits, size):
    return lax.ppermute(x, axis, [(i, i ^ bits) for i in range(size)])


def whole_call(kernel, name, scal, out_shape, operands, deps=(), scratch=(), flops=0, limit=SMALL_BYTES, near=(False, False)):
    scal = scal if isinstance(scal, tuple) else (scal,)

    def body(*refs):
        used = len(scal) + len(operands)
        kernel(*refs[:used], *refs[used + len(deps) :])

    def spec(shape):
        return pl.BlockSpec(shape, lambda i, *s: (0,) * len(shape))

    vmem = pl.BlockSpec(memory_space=pltpu.VMEM)
    moved = sum(int(np.prod(o.shape)) * o.dtype.itemsize for o in [*operands, *out_shape])
    return pl.pallas_call(
        body,
        grid_spec=pltpu.PrefetchScalarGridSpec(
            num_scalar_prefetch=len(scal),
            grid=(1,),
            in_specs=[vmem if near[0] else spec(o.shape) for o in operands]
            + [pl.BlockSpec(memory_space=pl.ANY)] * len(deps),
            out_specs=[vmem if near[1] else spec(o.shape) for o in out_shape],
            scratch_shapes=list(scratch),
        ),
        out_shape=out_shape,
        compiler_params=pltpu.CompilerParams(vmem_limit_bytes=limit),
        cost_estimate=pl.CostEstimate(flops=1024, bytes_accessed=1024, transcendentals=0),
        name=name,
    )(*scal, *operands, *deps)


def local(
    face_tokens,
    edge_tokens,
    face_cotangent,
    edge_cotangent,
    rotation,
    counts,
    norm_gain,
    qkv_weight,
    out_weight,
):
    T = lax.axis_size("tile")
    D = lax.axis_size("dp")
    me_t = lax.axis_index("tile")
    me_d = lax.axis_index("dp")
    LD, FL, width = face_tokens.shape[1:]
    K = edge_tokens.shape[1]
    EL = K * T
    NLG = edge_tokens.shape[2]
    length = FL + EL
    chunks = 2
    lines = LD // chunks
    RB = lines * K
    packed = T * 2 * RB
    factor = float(D * T * LD * length) ** (-0.5)
    x_bit = (me_d % 2).astype(jnp.int32)
    y_bit = ((me_d // 2) % 2).astype(jnp.int32)
    gain = norm_gain.reshape(1, width)

    def struct(*shape, dtype=BF):
        return jax.ShapeDtypeStruct(shape, dtype)

    order = np.zeros((chunks, T, 2, lines, K), np.int32)
    for c in range(chunks):
        for w in range(2):
            t, l, k = np.meshgrid(np.arange(T), np.arange(lines), np.arange(K), indexing="ij")
            order[c, :, w] = w * K * NLG + k * NLG + t * LD + c * lines + l

    face_rows = face_tokens.reshape(LD * FL, width)
    face_cots = face_cotangent.reshape(LD * FL, width)
    face_normed, face_early = whole_call(
        face_kernel,
        "face_norm",
        y_bit.reshape(1),
        [struct(LD * FL, width)] * 2,
        [face_rows, face_cots, gain],
        limit=VMEM_BYTES,
    )
    sent = []
    for c in range(chunks):
        sent += whole_call(
            lambda s, *refs: pack_kernel(*refs),
            "pack",
            y_bit.reshape(1),
            [struct(packed, width)],
            [
                edge_tokens.reshape(K * NLG, width),
                edge_cotangent.reshape(K * NLG, width),
                jnp.asarray(order[c].reshape(-1, 1)),
            ],
            deps=[face_early] if c else [],
            scratch=[pltpu.VMEM((2 * K * NLG, width), BF)],
            limit=VMEM_BYTES,
        )
    arrived = [lax.all_to_all(s, "tile", split_axis=0, concat_axis=0, tiled=True) for s in sent]
    got_face_a = exchange(face_normed, "dp", 1, D)
    got_face_b = exchange(face_early, "dp", 2, D)

    edges = lines * EL
    l, p = np.meshgrid(np.arange(lines), np.arange(EL), indexing="ij")
    table = []
    for pos in (p, EL - 1 - p):
        row = (pos // K) * (2 * RB) + l * K + pos % K
        table.append(np.stack([row, row + RB]))
    table.append(np.stack([l, l]))
    index = jnp.asarray(np.stack(table, axis=-1).reshape(-1, 3).astype(np.int32))
    t, c, w, l, k = np.meshgrid(
        np.arange(T),
        np.arange(chunks),
        np.arange(2),
        np.arange(lines),
        np.arange(K),
        indexing="ij",
    )
    at = 2 * c * edges + w * edges + l * EL
    pos = t * K + k
    table = [at + pos, at + EL - 1 - pos, c * lines + l]
    back_index = jnp.asarray(np.stack(table, axis=-1).reshape(-1, 3).astype(np.int32))
    edge_parts, results, got_edges, got_late = [], [], [], []
    faces = None
    for c in range(chunks):
        base = (me_t * LD + c * lines).astype(jnp.int32)
        scal = (jnp.stack([base, x_bit, y_bit]), rotation, counts)
        rows_all = lines * length
        row_shape = (rows_all, width)
        face_spec = pl.BlockSpec((1, lines, FL, width), lambda i, *s, c=c: (0, c, 0, 0))
        normed_spec = pl.BlockSpec((lines * FL, width), lambda i, *s, c=c: (c, 0))

        def full(shape):
            return pl.BlockSpec(shape, lambda i, *s: (0,) * len(shape))

        if c == 0:
            operands = [face_tokens, face_cotangent, arrived[c], index]
            operands += [face_normed, gain, qkv_weight, out_weight]
            tail = []
        else:
            z_edge, g_edge, normed_edge, early_edge = whole_call(
                functools.partial(edge_kernel, lines),
                "edge_norm",
                scal,
                [struct(edges, width)] * 4,
                [arrived[c], index, gain],
                deps=[results[0][5]],
                limit=VMEM_BYTES,
                near=(True, False),
            )
            operands = [face_tokens, face_cotangent, z_edge, g_edge, normed_edge]
            operands += [face_normed, gain, qkv_weight, out_weight, back_index, results[0][0]]
            tail = [*faces, got_face_a, got_face_b]
        in_specs = [
            face_spec
            if n < 2
            else normed_spec
            if o is face_normed
            else pl.BlockSpec(memory_space=pl.ANY)
            if o is qkv_weight or o is out_weight
            else pl.BlockSpec(memory_space=pltpu.VMEM)
            if n == 2 and c == 0
            else full(o.shape)
            for n, o in enumerate(operands)
        ]
        in_specs += [pl.BlockSpec(memory_space=pl.ANY)] * len(tail)
        aliases = {} if c == 0 else {3 + len(operands): 0, 4 + len(operands): 1}
        operands += tail
        back_rows = 2 * edges if c == 0 else packed * chunks
        edge_outs = [(edges, width)] * 2 if c == 0 else []
        send_shape = (rows_all + (edges if c == 0 else 0), width)
        outs = pl.pallas_call(
            functools.partial(layer_kernel, lines, c == 0, len(tail)),
            grid_spec=pltpu.PrefetchScalarGridSpec(
                num_scalar_prefetch=3,
                grid=(1,),
                in_specs=in_specs,
                out_specs=[face_spec, face_spec, full((back_rows, width))]
                + [pl.BlockSpec(memory_space=pl.ANY)] * 4
                + [full((8, width // 8))]
                + [full(e) for e in edge_outs],
                scratch_shapes=[
                    pltpu.VMEM(row_shape, BF),
                    pltpu.VMEM(row_shape, BF),
                    pltpu.VMEM(row_shape, BF),
                    pltpu.VMEM((rows_all, 3 * width), BF),
                    pltpu.VMEM(row_shape, BF),
                    pltpu.VMEM(row_shape, BF),
                    pltpu.VMEM((rows_all, 3 * width), BF),
                    pltpu.VMEM(row_shape, F32),
                    pltpu.VMEM(row_shape, BF),
                    pltpu.VMEM((2 * edges * (c + 1), width), BF),
                ]
                + ([pltpu.VMEM((edges, width), BF)] * 2 if c == 0 else [])
                + [
                    pltpu.VMEM(qkv_weight.shape, BF),
                    pltpu.VMEM(out_weight.shape, BF),
                    pltpu.SemaphoreType.DMA((3 * width // 512 + 1,)),
                    pltpu.SemaphoreType.DMA((6,)),
                ],
            ),
            out_shape=[struct(*face_tokens.shape)] * 2
            + [struct(back_rows, width)]
            + [struct(*row_shape), struct(*send_shape)] * 2
            + [struct(8, width // 8, dtype=F32)]
            + [struct(*e) for e in edge_outs],
            input_output_aliases=aliases,
            compiler_params=pltpu.CompilerParams(vmem_limit_bytes=VMEM_BYTES),
            cost_estimate=pl.CostEstimate(flops=1 << 35, bytes_accessed=1 << 20, transcendentals=0),
            name="layer",
        )(*scal, *operands)
        faces = outs[:2]
        results.append(outs[2:])
        late_a, late_b = exchange(outs[4], "dp", 1, D), exchange(outs[6], "dp", 2, D)
        if c == 0:
            g_edge, normed_edge = outs[8:]
            edges_a, edges_b = (late_a, edges, rows_all // edges), (late_b, edges, rows_all // edges)
            late_a, late_b = (late_a, rows_all, 0), (late_b, rows_all, 0)
        else:
            edges_a = exchange(normed_edge, "dp", 1, D)
            edges_b = exchange(early_edge, "dp", 2, D)
        edge_parts.append((normed_edge, g_edge))
        got_edges.append((edges_a, edges_b))
        got_late.append((late_a, late_b))
    returned = lax.all_to_all(results[1][0], "tile", split_axis=0, concat_axis=0, tiled=True)

    blocks = T // 2
    chip = (me_t // 2).astype(jnp.int32)
    core = (me_t % 2).astype(jnp.int32)
    quarter = width // 8
    pieces = (2 * quarter, 2 * quarter)
    size = width // T
    bits = D.bit_length() - 1
    groups = []
    for group in range(2):
        first = [b for b in range(bits) if b != group][0]
        swap = y_bit if group else jnp.zeros_like(y_bit)
        scal = jnp.stack([core, swap, ((me_d >> first) & 1).astype(jnp.int32)])
        late = [r[1 + 2 * group] for r in results]
        got_face = (got_face_a, got_face_b)[group]
        normed_e, g_e = [e[0] for e in edge_parts], [e[1] for e in edge_parts]
        got_e = [e[group] for e in got_edges]
        got_l = [e[group] for e in got_late]
        operands = [face_normed, face_cots, *normed_e, *g_e, got_face, got_e[0], late[0], late[1], got_l[0]]
        runs = [((0, 1), (2, 4), 0, 8), ((0, 1), (3, 5), 1, 9), ((6, 6), (7, 7), 0, 10)]
        start = weight_part(
            scal, runs, (False, True), blocks, operands, [], None, [],
            [*got_edges[1], got_late[0][0][0], got_late[0][1][0]]
            + [g[2][-1] for g in groups],
        )
        groups.append((scal, [got_face, got_e[1], got_l[1]], start, first))
    theirs = []
    runs = [((0, 0), (1, 1), 1, 2)]
    gains = [[r[5] for r in results], []]
    starts = [g[2] for g in groups]
    for group, (scal, operands, start, first) in enumerate(groups):
        send, token = weight_part(
            scal, runs, (False,), blocks, operands, [start[0]], None, gains[group],
            last if group else [starts[1][-1]],
            held=(2,),
        )
        last = [token]
        theirs.append(exchange(send, "tile", 1, T))
    halves = [[], []]
    for n, cut in enumerate(pieces):
        for group, (scal, operands, start, first) in enumerate(groups):
            give, keep, token = weight_part(
                scal, runs, (True,), blocks, operands, [start[1], theirs[group]],
                (sum(pieces[:n]), cut), [] if n else gains[group], last, held=(2,),
            )
            last = [token]
            both = [keep, exchange(give, "dp", 1 << first, D)]
            for b in range(bits):
                if b in (group, first):
                    continue
                columns = both[0].shape[1] // 2
                mine = (me_d >> b) & 1
                keep = [lax.dynamic_slice_in_dim(p, mine * columns, columns, 1) for p in both]
                give = [lax.dynamic_slice_in_dim(p, (1 - mine) * columns, columns, 1) for p in both]
                both = [sum(keep), exchange(sum(give), "dp", 1 << b, D)]
            halves[group].append(both)
    placed = []
    for n in range(len(pieces)):
        parts = [*halves[0][n], *halves[1][n]]
        columns = 2 * parts[0].shape[1]
        outs = whole_call(
            functools.partial(block_kernel, blocks, 2),
            "row_blocks",
            chip.reshape(1),
            [struct(size + (8 if n == 0 else 0), columns, dtype=F32)] * blocks,
            parts,
            near=(True, True),
            deps=last if n else [returned],
        )
        got = [exchange(outs[o], "tile", 2 * o, T) for o in range(1, blocks)]
        (mine,) = whole_call(
            functools.partial(sum_kernel, factor),
            "block_sum",
            chip.reshape(1),
            [struct(*outs[0].shape, dtype=F32)],
            [outs[0], *got],
            near=(True, True),
        )
        last = [outs[0]]
        placed += [mine] + [exchange(mine, "dp", o, D) for o in range(1, D)]

    back_order = np.zeros((2, K, NLG), np.int32)
    for w in range(2):
        k, t, c, l = np.meshgrid(
            np.arange(K), np.arange(T), np.arange(chunks), np.arange(lines), indexing="ij"
        )
        back_order[w] = ((t * chunks + c) * 2 * RB + w * RB + l * K + k).reshape(K, NLG)
    edge_output, edge_grad = whole_call(
        lambda s, *refs: unpack_kernel(1, *refs),
        "unpack",
        chip.reshape(1),
        [struct(K * NLG, width)] * 2,
        [returned, jnp.asarray(back_order.reshape(-1, 1))],
        scratch=[pltpu.VMEM((chunks * packed, width), BF)],
    )
    qkv_grad, out_grad = whole_call(
        functools.partial(place_kernel, pieces, D),
        "place",
        me_d.astype(jnp.int32).reshape(1),
        [struct(size, 3 * width, dtype=F32), struct(size, width, dtype=F32)],
        placed,
        near=(True, False),
    )
    gain_sum = (placed[0] + placed[1])[size:, : width // 8].reshape(width)
    gain_grad = lax.dynamic_slice_in_dim(gain_sum, me_t * size, size)
    shape = edge_tokens.shape
    return (
        faces[0],
        edge_output.reshape(shape),
        faces[1],
        edge_grad.reshape(shape),
        qkv_grad,
        out_grad,
        gain_grad,
    )


def solution(mesh):
    return jax.shard_map(
        local,
        mesh=mesh,
        in_specs=(
            P("dp", "tile", None, None),
            P("dp", "tile", None, None),
            P("dp", "tile", None, None),
            P("dp", "tile", None, None),
            P(),
            P(),
            P(),
            P(),
            P(),
        ),
        out_specs=(
            P("dp", "tile", None, None),
            P("dp", "tile", None, None),
            P("dp", "tile", None, None),
            P("dp", "tile", None, None),
            P("tile", None),
            P("tile", None),
            P("tile"),
        ),
        check_vma=False,
    )
```
